32 devices in a mesh: frames: 4 (over y, x), rows: 2 (over core), batch: 4 (over z).
Axes of the slice: x: 2, y: 2, z: 4, core: 2. Of those that a mesh axis runs over, the one named last changes fastest.
Arguments:
- video: bfloat16 [32, 32, 128, 320], P(('batch', 'frames'), 'rows'), parts along dimension 0, may hold values from -6 to 6
- w_spatial: bfloat16 [3, 3, 320, 320], replicated, may hold values from -0.109375 to 0.109375
- b_spatial: float32 [320], replicated, may hold values from -3 to 3
- w_temporal: bfloat16 [3, 320, 320], replicated, may hold values from -0.1875 to 0.1875
- b_temporal: float32 [320], replicated, may hold values from -3 to 3
Outputs:
- downsampled: bfloat16 [16, 32, 128, 320], P(('batch', 'frames'), 'rows'), parts along dimension 0
The draws below stay inside these ranges and needn't reach their ends.
There are 4 independent parts, one for each index of `batch`. The reference program is written for one: setup_inputs(seed, part) draws one part's arguments, and reference() takes and returns one part's arrays. A program takes and returns all parts, laid end to end along the dimension named above; an argument that names none is the same for every part. Nothing has to cross between parts.
All inputs are finite; a program needn't handle non-finite values.
Results may differ from the reference program's by a relative error of at most 0.0042.
Values may be sent and summed in bfloat16 or wider, within the bound.
No kernel may reach another device: no remote copies, remote signals or barrier semaphores. Data moves between devices by JAX's collectives and lax.ppermute only.
A program may use at most 64 MiB of HBM per device.

```python
import jax
import jax.numpy as jnp
from jax import lax

C = 320
W = 128
FRAMES = 8
H = 32


def levels(rng, dims, shards, least, top_value):
    factor_of = 1.0
    for dim, parts in shards:
        heights = jax.random.uniform(jax.random.fold_in(jax.random.fold_in(rng, 6), dim), (parts,), jnp.float32, least / len(shards), top_value / len(shards))
        factor_of = factor_of * jnp.repeat(jnp.exp(heights), dims[dim] // parts).reshape((-1,) + (1,) * (len(dims) - 1 - dim))
    return factor_of


def noise(stream_key, dims, spread, most, shards=(), held_as=jnp.bfloat16):
    loudness = levels(stream_key, dims, shards, -0.22, 0.18) if shards else 1.0
    drawn = jax.random.normal(stream_key, dims, jnp.float32) * spread * loudness
    return jnp.minimum(jnp.maximum(drawn, -most), most).astype(held_as)


def setup_inputs(seed: int = 0, part: int = 0) -> dict:
    key_list = jax.random.split(jax.random.key(seed), 6)
    part_splits = jax.random.split(jax.random.fold_in(key_list[5], part), 6)
    video = noise(part_splits[0], (FRAMES, H, W, C), 1.0, 6.0, ((0, 4), (1, 2)))
    w_spatial = noise(key_list[1], (3, 3, C, C), (9 * C) ** -0.5, 0.109375)
    b_spatial = noise(key_list[2], (C,), 0.5, 3.0, (), jnp.float32)
    w_temporal = noise(key_list[3], (3, C, C), (3 * C) ** -0.5, 0.1875)
    b_temporal = noise(key_list[4], (C,), 0.5, 3.0, (), jnp.float32)
    return {"video": video, "w_spatial": w_spatial, "b_spatial": b_spatial, "w_temporal": w_temporal, "b_temporal": b_temporal}


def reference(video, w_spatial, b_spatial, w_temporal, b_temporal):
    channels = video.shape[3]
    width = video.shape[2]
    height = video.shape[1]
    kernel = w_spatial.reshape(3, 3 * channels, channels)

    def spatial_frame(frame):
        padded = jnp.pad(frame, ((1, 1), (1, 1), (0, 0)))
        columns = jnp.concatenate([padded[:, 0:width], padded[:, 1:width + 1], padded[:, 2:width + 2]], axis=-1)
        summed = jnp.zeros((height, width, channels), jnp.float32) + b_spatial
        for row_tap in range(3):
            summed = summed + jnp.dot(columns[row_tap:row_tap + height], kernel[row_tap], preferred_element_type=jnp.float32)
        return jax.nn.silu(summed).astype(jnp.bfloat16)

    activated = lax.map(spatial_frame, video)
    even_frames = activated[0::2]
    odd_frames = activated[1::2]
    prev_frames = jnp.concatenate([jnp.zeros_like(odd_frames[:1]), odd_frames[:-1]], axis=0)
    total = jnp.dot(prev_frames, w_temporal[0], preferred_element_type=jnp.float32)
    total = total + jnp.dot(even_frames, w_temporal[1], preferred_element_type=jnp.float32)
    total = total + jnp.dot(odd_frames, w_temporal[2], preferred_element_type=jnp.float32)
    return (total + b_temporal).astype(jnp.bfloat16)
```

```python
import functools

import jax
import jax.numpy as jnp
from jax import lax
from jax.experimental import pallas as pl
from jax.experimental.pallas import tpu as pltpu
from jax.sharding import PartitionSpec as P

F32 = jnp.float32
BF16 = jnp.bfloat16
VMEM = pl.BlockSpec(memory_space=pltpu.VMEM)
ANY = pl.BlockSpec(memory_space=pl.ANY)
PARAMS = pltpu.CompilerParams(vmem_limit_bytes=20 * 2**20)


def ring(axis):
    count = lax.axis_size(axis)
    return [(i, (i + 1) % count) for i in range(count)]


def neighbour_rows(top, bottom):
    count = lax.axis_size("rows")
    if count == 2:
        mine = jnp.where(lax.axis_index("rows") == 0, bottom, top)
        got = lax.ppermute(mine, "rows", ring("rows"))
        return got, got
    above = lax.ppermute(bottom, "rows", ring("rows"))
    below = lax.ppermute(top, "rows", [(b, a) for a, b in ring("rows")])
    return above, below


def silu(v):
    half = 0.5 * v
    return half + half * jnp.tanh(half)


def prepare_kernel(ws_ref, bs_ref, wt_ref, bt_ref, conv_ref, mix_ref, cb_ref, mb_ref):
    taps, channels = ws_ref.shape[0], ws_ref.shape[2]
    for j in range(taps):
        block = ws_ref[:, j].reshape(taps * channels, channels)
        conv_ref[j * channels : (j + 1) * channels, :] = block.T
    mix_ref[...] = wt_ref[...].reshape(taps * channels, channels).T
    width = cb_ref.shape[1]
    cb_ref[...] = jnp.broadcast_to(bs_ref[...], (width, channels)).T
    mb_ref[...] = jnp.broadcast_to(bt_ref[...], (width, channels)).T


def conv_rows(columns, conv, bias, channels, width):
    stacked = jnp.concatenate(columns, axis=1)
    products = jnp.dot(conv, stacked, preferred_element_type=F32)
    lane = lax.broadcasted_iota(jnp.int32, (1, width), 1)
    rows = []
    for q in range(len(columns)):
        part = products[:, q * width : (q + 1) * width]
        left = jnp.where(lane == 0, 0.0, pltpu.roll(part[:channels], 1, 1))
        right = jnp.where(lane == width - 1, 0.0, pltpu.roll(part[2 * channels :], width - 1, 1))
        rows.append(silu(left + part[channels : 2 * channels] + right + bias).astype(BF16))
    return jnp.concatenate(rows, axis=1)


def own_kernel(x_ref, above_ref, below_ref, conv_ref, mix_ref, cb_ref, mb_ref, out_ref, xs, *, group):
    frames, rows, channels, width = x_ref.shape
    index, count = lax.axis_index("rows"), lax.axis_size("rows")
    zero = jnp.zeros((channels, width), BF16)
    for f in range(frames):
        xs[f, 0] = jnp.where(index > 0, above_ref[f, 0], zero)
        xs[f, rows + 1] = jnp.where(index < count - 1, below_ref[f, 0], zero)
    xs[:, 1 : rows + 1] = x_ref[...]

    def body(p, carry):
        h = p * group
        parts = []
        for f in range(frames):
            columns = [xs[f, pl.ds(h + q, 3)].reshape(3 * channels, width) for q in range(group)]
            parts.append(conv_rows(columns, conv_ref[...], cb_ref[...], channels, width))
        mixed = jnp.dot(mix_ref[:, channels:], jnp.concatenate(parts, axis=0), preferred_element_type=F32)
        for q in range(group):
            out_ref[h + q] = mixed[:, q * width : (q + 1) * width] + mb_ref[...]
        return carry

    lax.fori_loop(0, rows // group, body, 0)


def incoming_kernel(*refs, pieces, groups, seeded):
    refs = list(refs)
    own_ref, conv_ref, mix_ref, cb_ref = refs[:4]
    above_ref, below_ref = refs[4:6]
    piece_refs = refs[6 : 6 + len(pieces)]
    out_ref, stage, sem = refs[-3:]
    rows, channels, width = own_ref.shape
    index, count = lax.axis_index("rows"), lax.axis_size("rows")
    first = lax.axis_index("frames") == 0
    zero = jnp.zeros((channels, width), BF16)
    where = {}
    for ref, held in zip(piece_refs, pieces):
        for k, r in enumerate(held):
            where[r] = (ref, k)

    def row(r):
        if r < 0:
            return jnp.where(index > 0, above_ref[0], zero)
        if r >= rows:
            return jnp.where(index < count - 1, below_ref[0], zero)
        ref, k = where[r]
        return ref[k]

    copies = []
    slot = 0
    for start, size in groups:
        columns = [
            jnp.concatenate([row(start + q + i - 1) for i in range(3)], axis=0) for q in range(size)
        ]
        act = conv_rows(columns, conv_ref[...], cb_ref[...], channels, width)
        act = jnp.where(first, jnp.zeros_like(act), act)
        mixed = jnp.dot(mix_ref[:, :channels], act, preferred_element_type=F32)
        for q in range(size):
            total = own_ref[start + q] + mixed[:, q * width : (q + 1) * width]
            stage[slot + q] = total.astype(BF16)
        copy = pltpu.make_async_copy(
            stage.at[pl.ds(slot, size)], out_ref.at[pl.ds(start, size)], sem.at[len(copies)]
        )
        copy.start()
        copies.append(copy)
        slot += size
    for copy in copies:
        copy.wait()


def incoming_rows(out, own, weights, edges, arrived, groups):
    conv, mix, cb = weights
    rows, channels, width = own.shape
    pieces = [held for held, _ in arrived]
    operands = [own, conv, mix, cb, *edges] + [array for _, array in arrived]
    in_specs = [VMEM] * len(operands)
    aliases = {}
    if out is not None:
        aliases = {len(operands): 0}
        operands.append(out)
        in_specs.append(ANY)
    return pl.pallas_call(
        functools.partial(incoming_kernel, pieces=pieces, groups=groups, seeded=out is not None),
        out_shape=jax.ShapeDtypeStruct(own.shape, BF16),
        in_specs=in_specs,
        out_specs=ANY,
        input_output_aliases=aliases,
        scratch_shapes=[
            pltpu.VMEM((sum(size for _, size in groups), channels, width), BF16),
            pltpu.SemaphoreType.DMA((len(groups),)),
        ],
        compiler_params=PARAMS,
    )(*operands)


def per_device(video, w_spatial, b_spatial, w_temporal, b_temporal):
    frames, rows, width, channels = video.shape
    x = jnp.transpose(video, (0, 1, 3, 2))
    last = x[frames - 1]

    chunk_rows = [[0, 1, 2, 13, 14, 15], list(range(3, 11)), [11, 12]]

    def chunk(held):
        runs = []
        for r in held:
            if runs and runs[-1][1] == r:
                runs[-1][1] = r + 1
            else:
                runs.append([r, r + 1])
        return jnp.concatenate([last[a:b] for a, b in runs], axis=0)

    arrived = [(held, lax.ppermute(chunk(held), "frames", ring("frames"))) for held in chunk_rows]
    above, below = neighbour_rows(x[:, :1], x[:, rows - 1 :])
    edges = neighbour_rows(arrived[0][1][:1], arrived[0][1][-1:])

    square = jax.ShapeDtypeStruct((3 * channels, 3 * channels), BF16)
    flat = jax.ShapeDtypeStruct((channels, 3 * channels), BF16)
    bias = jax.ShapeDtypeStruct((channels, width), F32)
    conv, mix, cb, mb = pl.pallas_call(
        prepare_kernel,
        out_shape=(square, flat, bias, bias),
        in_specs=[VMEM] * 4,
        out_specs=(VMEM,) * 4,
        compiler_params=PARAMS,
    )(w_spatial, b_spatial.reshape(1, channels), w_temporal, b_temporal.reshape(1, channels))

    own = pl.pallas_call(
        functools.partial(own_kernel, group=4),
        out_shape=jax.ShapeDtypeStruct((rows, channels, width), F32),
        in_specs=[VMEM] * 7,
        out_specs=VMEM,
        scratch_shapes=[pltpu.VMEM((frames, rows + 2, channels, width), BF16)],
        compiler_params=PARAMS,
    )(x, above, below, conv, mix, cb, mb)

    weights = (conv, mix, cb)
    out = incoming_rows(None, own, weights, edges, arrived[:1], [(0, 2), (14, 2)])
    out = incoming_rows(out, own, weights, edges, arrived[:2], [(2, 4), (6, 4)])
    out = incoming_rows(out, own, weights, edges, arrived, [(10, 4)])
    return jnp.transpose(out[None], (0, 1, 3, 2))


def solution(mesh):
    in_specs = (P(("batch", "frames"), "rows", None, None), P(), P(), P(), P())
    out_specs = P(("batch", "frames"), "rows", None, None)
    return jax.shard_map(
        per_device, mesh=mesh, in_specs=in_specs, out_specs=out_specs, check_vma=False
    )
```

```python
import functools

import jax
import jax.numpy as jnp
from jax import lax
from jax.experimental import pallas as pl
from jax.experimental.pallas import tpu as pltpu
from jax.sharding import PartitionSpec as P

F32 = jnp.float32
BF16 = jnp.bfloat16
VMEM = pl.BlockSpec(memory_space=pltpu.VMEM)
ANY = pl.BlockSpec(memory_space=pl.ANY)
HEAD_LIMIT = 62 * 2**20
PARAMS = pltpu.CompilerParams(vmem_limit_bytes=20 * 2**20)


def flipped():
    return lax.axis_index("rows") == 0


def first_row(place, size, rows):
    return jnp.where(flipped(), rows - place - size, place)


def ring(axis):
    count = lax.axis_size(axis)
    return [(i, (i + 1) % count) for i in range(count)]


def cost(flops, moved):
    return pl.CostEstimate(flops=flops, bytes_accessed=moved, transcendentals=0)


def silu(v):
    half = 0.5 * v
    return half + half * jnp.tanh(half)


def row_copies(x_ref, outs, spans, sem):
    rows = x_ref.shape[1]
    copies = []
    for k, (out, (frame, count, place, size)) in enumerate(zip(outs, spans)):
        source = x_ref.at[pl.ds(frame, count), pl.ds(first_row(place, size, rows), size)]
        copies.append(pltpu.make_async_copy(source, out, sem.at[k]))
    for copy in copies:
        copy.start()
    return copies


def row_shapes(x, spans):
    return [jax.ShapeDtypeStruct((count, size) + x.shape[2:], x.dtype) for _, count, _, size in spans]


def slice_kernel(x_ref, *refs, spans):
    for copy in row_copies(x_ref, refs[:-1], spans, refs[-1]):
        copy.wait()


def prepare_kernel(x_ref, ws_ref, bs_ref, wt_ref, bt_ref, conv_ref, mix_ref, cb_ref, mb_ref, piece_ref, sem, *, spans):
    copies = row_copies(x_ref, [piece_ref], spans, sem)
    taps, channels = ws_ref.shape[0], ws_ref.shape[2]
    for j in range(taps):
        blocks = [ws_ref[jnp.where(flipped(), taps - 1 - i, i), j] for i in range(taps)]
        conv_ref[j * channels : (j + 1) * channels, :] = jnp.concatenate(blocks, axis=0).T
    mix_ref[...] = wt_ref[...].reshape(taps * channels, channels).T
    width = cb_ref.shape[1]
    cb_ref[...] = jnp.broadcast_to(bs_ref[...], (width, channels)).T
    mb_ref[...] = jnp.broadcast_to(bt_ref[...], (width, channels)).T
    for copy in copies:
        copy.wait()


def conv_rows(columns, conv, bias, channels, width):
    stacked = jnp.concatenate(columns, axis=1)
    products = jnp.dot(conv, stacked, preferred_element_type=F32)
    lane = lax.broadcasted_iota(jnp.int32, (1, width), 1)
    rows = []
    for q in range(len(columns)):
        part = products[:, q * width : (q + 1) * width]
        left = jnp.where(lane == 0, 0.0, pltpu.roll(part[:channels], 1, 1))
        right = jnp.where(lane == width - 1, 0.0, pltpu.roll(part[2 * channels :], width - 1, 1))
        rows.append(silu(left + part[channels : 2 * channels] + right + bias).astype(BF16))
    return jnp.concatenate(rows, axis=1)


def own_kernel(x_ref, beside_ref, conv_ref, mix_ref, cb_ref, mb_ref, out_ref, piece_ref, xs, *, group, spans):
    frames, rows, channels, width = x_ref.shape
    ((frame, _, place, size),) = spans
    piece_ref[0] = x_ref[frame, pl.ds(first_row(place, size, rows), size)]
    for f in range(frames):
        xs[f, 0] = beside_ref[f, 0]
        xs[f, rows + 1] = jnp.zeros((channels, width), BF16)

    def fill(s, carry):
        for f in range(frames):
            xs[f, s + 1] = x_ref[f, first_row(s, 1, rows)]
        return carry

    lax.fori_loop(0, rows, fill, 0)

    def body(p, carry):
        h = p * group
        parts = []
        for f in range(frames):
            columns = [xs[f, pl.ds(h + q, 3)].reshape(3 * channels, width) for q in range(group)]
            parts.append(conv_rows(columns, conv_ref[...], cb_ref[...], channels, width))
        mixed = jnp.dot(mix_ref[:, channels:], jnp.concatenate(parts, axis=0), preferred_element_type=F32)
        for q in range(group):
            out_ref[h + q] = mixed[:, q * width : (q + 1) * width] + mb_ref[...]
        return carry

    lax.fori_loop(0, rows // group, body, 0)


def incoming_kernel(own_ref, conv_ref, mix_ref, cb_ref, kept_ref, piece_ref, *refs, low, place, group, aliased):
    refs = refs[1:] if aliased else refs
    out_ref, carry_ref, xs, stage, sem = refs
    rows, channels, width = own_ref.shape
    kept, size = kept_ref.shape[0], piece_ref.shape[1]
    count = stage.shape[0]
    flip = flipped()
    xs[0:kept] = kept_ref[...]
    for k in range(size):
        xs[kept + k] = piece_ref[0, jnp.where(flip, size - 1 - k, k)]
    if xs.shape[0] > kept + size:
        xs[kept + size] = jnp.zeros((channels, width), BF16)
    carry_ref[...] = xs[pl.ds(xs.shape[0] - 2, 2)]
    first = lax.axis_index("frames") == 0

    @pl.when(first)
    def _():
        for q in range(count):
            stage[jnp.where(flip, count - 1 - q, q)] = own_ref[low + q].astype(BF16)

    @pl.when(jnp.logical_not(first))
    def _():
        def body(p, carry):
            h = p * group
            columns = [xs[pl.ds(h + q, 3)].reshape(3 * channels, width) for q in range(group)]
            act = conv_rows(columns, conv_ref[...], cb_ref[...], channels, width)
            mixed = jnp.dot(mix_ref[:, :channels], act, preferred_element_type=F32)
            for q in range(group):
                total = own_ref[low + h + q] + mixed[:, q * width : (q + 1) * width]
                stage[jnp.where(flip, count - 1 - h - q, h + q)] = total.astype(BF16)
            return carry

        lax.fori_loop(0, count // group, body, 0)

    copy = pltpu.make_async_copy(stage, out_ref.at[pl.ds(first_row(low, count, rows), count)], sem)
    copy.start()
    copy.wait()


def incoming_rows(out, own, weights, kept, piece, low, place, last):
    conv, mix, cb = weights
    rows, channels, width = own.shape
    held = kept.shape[0] + piece.shape[1] + (1 if last else 0)
    count = held - 2
    group = next(g for g in (4, 3, 2, 1) if count % g == 0)
    operands = [own, conv, mix, cb, kept, piece]
    in_specs = [VMEM] * len(operands)
    aliases = {}
    if out is not None:
        aliases = {len(operands): 0}
        operands.append(out)
        in_specs.append(ANY)
    return pl.pallas_call(
        functools.partial(
            incoming_kernel, low=low, place=place, group=group, aliased=out is not None
        ),
        out_shape=(
            jax.ShapeDtypeStruct(own.shape, BF16),
            jax.ShapeDtypeStruct((2, channels, width), BF16),
        ),
        in_specs=in_specs,
        out_specs=(ANY, VMEM),
        input_output_aliases=aliases,
        scratch_shapes=[
            pltpu.VMEM((held, channels, width), BF16),
            pltpu.VMEM((count, channels, width), BF16),
            pltpu.SemaphoreType.DMA,
        ],
        compiler_params=PARAMS,
        cost_estimate=cost(0, 0),
    )(*operands)


def per_device(video, w_spatial, b_spatial, w_temporal, b_temporal):
    frames, rows, width, channels = video.shape
    x = jnp.transpose(video, (0, 1, 3, 2))
    sizes = [rows - rows // 4 - 1, rows // 4, 1]
    places = [sum(sizes[:k]) for k in range(len(sizes))]

    spans = [(frames - 1, 1, place, size) for place, size in zip(places, sizes)]

    head_spans = [spans[0], (0, frames, 0, 1)]
    head, boundary = pl.pallas_call(
        functools.partial(slice_kernel, spans=head_spans),
        out_shape=row_shapes(x, head_spans),
        in_specs=[ANY],
        out_specs=[ANY] * 2,
        scratch_shapes=[pltpu.SemaphoreType.DMA((2,))],
        compiler_params=pltpu.CompilerParams(vmem_limit_bytes=HEAD_LIMIT),
    )(x)
    arrived = [lax.ppermute(head, "frames", ring("frames"))]
    beside = lax.ppermute(boundary, "rows", ring("rows"))

    square = jax.ShapeDtypeStruct((3 * channels, 3 * channels), BF16)
    flat = jax.ShapeDtypeStruct((channels, 3 * channels), BF16)
    bias = jax.ShapeDtypeStruct((channels, width), F32)
    conv, mix, cb, mb, piece = pl.pallas_call(
        functools.partial(prepare_kernel, spans=spans[1:2]),
        out_shape=[square, flat, bias, bias] + row_shapes(x, spans[1:2]),
        in_specs=[ANY] + [VMEM] * 4,
        out_specs=[VMEM] * 4 + [ANY],
        scratch_shapes=[pltpu.SemaphoreType.DMA((1,))],
        compiler_params=PARAMS,
        cost_estimate=cost(0, 2 * 12 * channels * channels * 2),
    )(x, w_spatial, b_spatial.reshape(1, channels), w_temporal, b_temporal.reshape(1, channels))
    arrived.append(lax.ppermute(piece, "frames", ring("frames")))

    own, piece = pl.pallas_call(
        functools.partial(own_kernel, group=4, spans=spans[2:]),
        out_shape=[jax.ShapeDtypeStruct((rows, channels, width), F32)] + row_shapes(x, spans[2:]),
        in_specs=[VMEM] * 6,
        out_specs=[VMEM] * 2,
        scratch_shapes=[pltpu.VMEM((frames, rows + 2, channels, width), BF16)],
        compiler_params=PARAMS,
        cost_estimate=cost(2 * rows * width * channels * channels * 20, 8 * rows * channels * width),
    )(x, beside, conv, mix, cb, mb)
    arrived.append(lax.ppermute(piece, "frames", ring("frames")))

    own, arrived[0] = lax.optimization_barrier((own, arrived[0]))
    size = sizes[0]
    edge = jnp.where(flipped(), arrived[0][0, size - 1 :], arrived[0][0, :1])
    kept = lax.ppermute(edge, "rows", ring("rows"))

    weights = (conv, mix, cb)
    out, low = None, 0
    for k, piece in enumerate(arrived):
        last = k == len(arrived) - 1
        out, kept = incoming_rows(out, own, weights, kept, piece, low, places[k], last)
        low = places[k] + sizes[k] - 1
    return jnp.transpose(out[None], (0, 1, 3, 2))


def solution(mesh):
    in_specs = (P(("batch", "frames"), "rows", None, None), P(), P(), P(), P())
    out_specs = P(("batch", "frames"), "rows", None, None)
    return jax.shard_map(
        per_device, mesh=mesh, in_specs=in_specs, out_specs=out_specs, check_vma=False
    )
```

```python
import functools

import jax
import jax.numpy as jnp
from jax import lax
from jax.experimental import pallas as pl
from jax.experimental.pallas import tpu as pltpu
from jax.sharding import PartitionSpec as P

F32 = jnp.float32
BF16 = jnp.bfloat16
VMEM = pl.BlockSpec(memory_space=pltpu.VMEM)
ANY = pl.BlockSpec(memory_space=pl.ANY)
HEAD_LIMIT = 53 * 2**20
PARAMS = pltpu.CompilerParams(vmem_limit_bytes=20 * 2**20)


def flipped():
    return lax.axis_index("rows") == 0


def first_row(place, size, rows):
    return jnp.where(flipped(), rows - place - size, place)


def ring(axis):
    count = lax.axis_size(axis)
    return [(i, (i + 1) % count) for i in range(count)]


def cost(flops, moved):
    return pl.CostEstimate(flops=flops, bytes_accessed=moved, transcendentals=0)


def silu(v):
    half = 0.5 * v
    return half + half * jnp.tanh(half)


def row_copies(x_ref, outs, spans, sem):
    rows = x_ref.shape[1]
    copies = []
    for k, (out, (frame, count, place, size)) in enumerate(zip(outs, spans)):
        source = x_ref.at[pl.ds(frame, count), pl.ds(first_row(place, size, rows), size)]
        copies.append(pltpu.make_async_copy(source, out, sem.at[k]))
    for copy in copies:
        copy.start()
    return copies


def row_shapes(x, spans):
    return [jax.ShapeDtypeStruct((count, size) + x.shape[2:], x.dtype) for _, count, _, size in spans]


def slice_kernel(x_ref, *refs, spans):
    for copy in row_copies(x_ref, refs[:-1], spans, refs[-1]):
        copy.wait()


def prepare_kernel(x_ref, ws_ref, bs_ref, wt_ref, bt_ref, conv_ref, mix_ref, cb_ref, mb_ref, piece_ref, sem, *, spans):
    copies = row_copies(x_ref, [piece_ref], spans, sem)
    taps, channels = ws_ref.shape[0], ws_ref.shape[2]
    for j in range(taps):
        blocks = [ws_ref[jnp.where(flipped(), taps - 1 - i, i), j] for i in range(taps)]
        conv_ref[j * channels : (j + 1) * channels, :] = jnp.concatenate(blocks, axis=0).T
    mix_ref[...] = wt_ref[...].reshape(taps * channels, channels).T
    width = cb_ref.shape[1]
    cb_ref[...] = jnp.broadcast_to(bs_ref[...], (width, channels)).T
    mb_ref[...] = jnp.broadcast_to(bt_ref[...], (width, channels)).T
    for copy in copies:
        copy.wait()


def conv_rows(columns, conv, bias, channels, width):
    stacked = jnp.concatenate(columns, axis=1)
    products = jnp.dot(conv, stacked, preferred_element_type=F32)
    lane = lax.broadcasted_iota(jnp.int32, (1, width), 1)
    rows = []
    for q in range(len(columns)):
        part = products[:, q * width : (q + 1) * width]
        left = jnp.where(lane == 0, 0.0, pltpu.roll(part[:channels], 1, 1))
        right = jnp.where(lane == width - 1, 0.0, pltpu.roll(part[2 * channels :], width - 1, 1))
        rows.append(silu(left + part[channels : 2 * channels] + right + bias).astype(BF16))
    return jnp.concatenate(rows, axis=1)


def own_kernel(x_ref, beside_ref, conv_ref, mix_ref, cb_ref, mb_ref, out_ref, *refs, group, spans):
    piece_refs, xs = refs[:-1], refs[-1]
    frames, rows, channels, width = x_ref.shape
    for ref, (frame, _, place, size) in zip(piece_refs, spans):
        ref[0] = x_ref[frame, pl.ds(first_row(place, size, rows), size)]
    for f in range(frames):
        xs[f, 0] = beside_ref[f, 0]
        xs[f, rows + 1] = jnp.zeros((channels, width), BF16)

    def fill(s, carry):
        for f in range(frames):
            xs[f, s + 1] = x_ref[f, first_row(s, 1, rows)]
        return carry

    lax.fori_loop(0, rows, fill, 0)

    def body(p, carry):
        h = p * group
        parts = []
        for f in range(frames):
            columns = [xs[f, pl.ds(h + q, 3)].reshape(3 * channels, width) for q in range(group)]
            parts.append(conv_rows(columns, conv_ref[...], cb_ref[...], channels, width))
        mixed = jnp.dot(mix_ref[:, channels:], jnp.concatenate(parts, axis=0), preferred_element_type=F32)
        for q in range(group):
            out_ref[h + q] = mixed[:, q * width : (q + 1) * width] + mb_ref[...]
        return carry

    lax.fori_loop(0, rows // group, body, 0)


def incoming_kernel(own_ref, conv_ref, mix_ref, cb_ref, *refs, pieces, low, group):
    kept_ref, piece_refs = refs[0], refs[1 : 1 + pieces]
    out_ref, carry_ref, xs, stage, sem = refs[-5:]
    rows, channels, width = own_ref.shape
    count = stage.shape[0]
    flip = flipped()
    held = kept_ref.shape[0]
    xs[0:held] = kept_ref[...]
    for ref in piece_refs:
        size = ref.shape[1]
        for k in range(size):
            xs[held + k] = ref[0, jnp.where(flip, size - 1 - k, k)]
        held += size
    if xs.shape[0] > held:
        xs[held] = jnp.zeros((channels, width), BF16)
    carry_ref[...] = xs[pl.ds(xs.shape[0] - 2, 2)]
    first = lax.axis_index("frames") == 0

    @pl.when(first)
    def _():
        for q in range(count):
            stage[jnp.where(flip, count - 1 - q, q)] = own_ref[low + q].astype(BF16)

    @pl.when(jnp.logical_not(first))
    def _():
        def body(p, carry):
            h = p * group
            columns = [xs[pl.ds(h + q, 3)].reshape(3 * channels, width) for q in range(group)]
            act = conv_rows(columns, conv_ref[...], cb_ref[...], channels, width)
            mixed = jnp.dot(mix_ref[:, :channels], act, preferred_element_type=F32)
            for q in range(group):
                total = own_ref[low + h + q] + mixed[:, q * width : (q + 1) * width]
                stage[jnp.where(flip, count - 1 - h - q, h + q)] = total.astype(BF16)
            return carry

        lax.fori_loop(0, count // group, body, 0)

    copy = pltpu.make_async_copy(stage, out_ref.at[pl.ds(first_row(low, count, rows), count)], sem)
    copy.start()
    copy.wait()


def incoming_rows(out, own, weights, kept, pieces, low, last):
    conv, mix, cb = weights
    rows, channels, width = own.shape
    held = kept.shape[0] + sum(piece.shape[1] for piece in pieces) + (1 if last else 0)
    count = held - 2
    group = next(g for g in (5, 4, 3, 2, 1) if count % g == 0)
    operands = [own, conv, mix, cb, kept, *pieces]
    in_specs = [VMEM] * len(operands)
    aliases = {}
    if out is not None:
        aliases = {len(operands): 0}
        operands.append(out)
        in_specs.append(ANY)
    return pl.pallas_call(
        functools.partial(incoming_kernel, pieces=len(pieces), low=low, group=group),
        out_shape=(
            jax.ShapeDtypeStruct(own.shape, BF16),
            jax.ShapeDtypeStruct((2, channels, width), BF16),
        ),
        in_specs=in_specs,
        out_specs=(ANY, VMEM),
        input_output_aliases=aliases,
        scratch_shapes=[
            pltpu.VMEM((held, channels, width), BF16),
            pltpu.VMEM((count, channels, width), BF16),
            pltpu.SemaphoreType.DMA,
        ],
        compiler_params=PARAMS,
        cost_estimate=cost(0, 0),
    )(*operands)


def per_device(video, w_spatial, b_spatial, w_temporal, b_temporal):
    frames, rows, width, channels = video.shape
    x = jnp.transpose(video, (0, 1, 3, 2))
    sizes = [5, rows - 10, 4, 1]
    steps = [(0, 2), (2, 3), (3, 4)]
    places = [sum(sizes[:k]) for k in range(len(sizes))]
    spans = [(frames - 1, 1, place, size) for place, size in zip(places, sizes)]

    head_spans = [spans[0], (0, frames, 0, 1)]
    head, boundary = pl.pallas_call(
        functools.partial(slice_kernel, spans=head_spans),
        out_shape=row_shapes(x, head_spans),
        in_specs=[ANY],
        out_specs=[VMEM] * 2,
        scratch_shapes=[pltpu.SemaphoreType.DMA((2,))],
        compiler_params=pltpu.CompilerParams(vmem_limit_bytes=HEAD_LIMIT),
    )(x)
    arrived = [lax.ppermute(head, "frames", ring("frames"))]
    beside = lax.ppermute(boundary, "rows", ring("rows"))

    square = jax.ShapeDtypeStruct((3 * channels, 3 * channels), BF16)
    flat = jax.ShapeDtypeStruct((channels, 3 * channels), BF16)
    bias = jax.ShapeDtypeStruct((channels, width), F32)
    conv, mix, cb, mb, piece = pl.pallas_call(
        functools.partial(prepare_kernel, spans=spans[1:2]),
        out_shape=[square, flat, bias, bias] + row_shapes(x, spans[1:2]),
        in_specs=[ANY] + [VMEM] * 4,
        out_specs=[VMEM] * 5,
        scratch_shapes=[pltpu.SemaphoreType.DMA((1,))],
        compiler_params=PARAMS,
        cost_estimate=cost(0, 2 * 12 * channels * channels * 2),
    )(x, w_spatial, b_spatial.reshape(1, channels), w_temporal, b_temporal.reshape(1, channels))
    arrived.append(lax.ppermute(piece, "frames", ring("frames")))

    own, *pieces = pl.pallas_call(
        functools.partial(own_kernel, group=4, spans=spans[2:]),
        out_shape=[jax.ShapeDtypeStruct((rows, channels, width), F32)] + row_shapes(x, spans[2:]),
        in_specs=[VMEM] * 6,
        out_specs=[VMEM] * (len(sizes) - 1),
        scratch_shapes=[pltpu.VMEM((frames, rows + 2, channels, width), BF16)],
        compiler_params=PARAMS,
        cost_estimate=cost(2 * rows * width * channels * channels * 20, 8 * rows * channels * width),
    )(x, beside, conv, mix, cb, mb)
    arrived += [lax.ppermute(piece, "frames", ring("frames")) for piece in pieces]

    own, arrived[0] = lax.optimization_barrier((own, arrived[0]))
    size = sizes[0]
    edge = jnp.where(flipped(), arrived[0][0, size - 1 :], arrived[0][0, :1])
    kept = lax.ppermute(edge, "rows", ring("rows"))

    weights = (conv, mix, cb)
    out, low = None, 0
    for begin, end in steps:
        out, kept = incoming_rows(out, own, weights, kept, arrived[begin:end], low, end == len(arrived))
        low = places[end - 1] + sizes[end - 1] - 1
    return jnp.transpose(out[None], (0, 1, 3, 2))


def solution(mesh):
    in_specs = (P(("batch", "frames"), "rows", None, None), P(), P(), P(), P())
    out_specs = P(("batch", "frames"), "rows", None, None)
    return jax.shard_map(
        per_device, mesh=mesh, in_specs=in_specs, out_specs=out_specs, check_vma=False
    )
```

```python
import functools

import jax
import jax.numpy as jnp
from jax import lax
from jax.experimental import pallas as pl
from jax.experimental.pallas import tpu as pltpu
from jax.sharding import PartitionSpec as P

F32 = jnp.float32
BF16 = jnp.bfloat16
VMEM = pl.BlockSpec(memory_space=pltpu.VMEM)
ANY = pl.BlockSpec(memory_space=pl.ANY)
HEAD_LIMIT = 53 * 2**20
PARAMS = pltpu.CompilerParams(vmem_limit_bytes=20 * 2**20)


def flipped():
    return lax.axis_index("rows") == 0


def first_row(place, size, rows):
    return jnp.where(flipped(), rows - place - size, place)


def ring(axis):
    count = lax.axis_size(axis)
    return [(i, (i + 1) % count) for i in range(count)]


def cost(flops, moved):
    return pl.CostEstimate(flops=flops, bytes_accessed=moved, transcendentals=0)


def silu(v):
    half = 0.5 * v
    return half + half * jnp.tanh(half)


def row_copies(x_ref, outs, spans, sem):
    rows = x_ref.shape[1]
    copies = []
    for out, (frame, count, place, size) in zip(outs, spans):
        for q in range(size):
            source = x_ref.at[pl.ds(frame, count), first_row(place + q, 1, rows)]
            copies.append(pltpu.make_async_copy(source, out.at[:, q], sem.at[len(copies)]))
    for copy in copies:
        copy.start()
    return copies


def keep_rows(x_ref, outs, spans):
    for out, (frame, _, place, size) in zip(outs, spans):
        for q in range(size):
            out[0, q] = x_ref[frame, first_row(place + q, 1, x_ref.shape[1])]


def row_shapes(x, spans):
    return [jax.ShapeDtypeStruct((count, size) + x.shape[2:], x.dtype) for _, count, _, size in spans]


def slice_kernel(x_ref, *refs, spans):
    for copy in row_copies(x_ref, refs[:-1], spans, refs[-1]):
        copy.wait()


def prepare_kernel(x_ref, ws_ref, bs_ref, wt_ref, bt_ref, conv_ref, mix_ref, cb_ref, mb_ref, *piece_refs, spans):
    keep_rows(x_ref, piece_refs, spans)
    taps, channels = ws_ref.shape[0], ws_ref.shape[2]
    for j in range(taps):
        blocks = [ws_ref[jnp.where(flipped(), taps - 1 - i, i), j] for i in range(taps)]
        conv_ref[j * channels : (j + 1) * channels, :] = jnp.concatenate(blocks, axis=0).T
    mix_ref[...] = wt_ref[...].reshape(taps * channels, channels).T
    width = cb_ref.shape[1]
    cb_ref[...] = jnp.broadcast_to(bs_ref[...], (width, channels)).T
    mb_ref[...] = jnp.broadcast_to(bt_ref[...], (width, channels)).T


def conv_rows(columns, conv, bias, channels, width):
    stacked = jnp.concatenate(columns, axis=1)
    products = jnp.dot(conv, stacked, preferred_element_type=F32)
    lane = lax.broadcasted_iota(jnp.int32, (1, width), 1)
    rows = []
    for q in range(len(columns)):
        part = products[:, q * width : (q + 1) * width]
        left = jnp.where(lane == 0, 0.0, pltpu.roll(part[:channels], 1, 1))
        right = jnp.where(lane == width - 1, 0.0, pltpu.roll(part[2 * channels :], width - 1, 1))
        rows.append(silu(left + part[channels : 2 * channels] + right + bias).astype(BF16))
    return jnp.concatenate(rows, axis=1)


def own_kernel(x_ref, beside_ref, conv_ref, mix_ref, cb_ref, mb_ref, out_ref, *refs, group, spans):
    piece_refs, xs = refs[:-1], refs[-1]
    frames, rows, channels, width = x_ref.shape
    keep_rows(x_ref, piece_refs, spans)
    for f in range(frames):
        xs[f, 0] = beside_ref[f, 0]
        xs[f, rows + 1] = jnp.zeros((channels, width), BF16)

    def fill(s, carry):
        for f in range(frames):
            xs[f, s + 1] = x_ref[f, first_row(s, 1, rows)]
        return carry

    lax.fori_loop(0, rows, fill, 0)

    def body(p, carry):
        h = p * group
        parts = []
        for f in range(frames):
            columns = [xs[f, pl.ds(h + q, 3)].reshape(3 * channels, width) for q in range(group)]
            parts.append(conv_rows(columns, conv_ref[...], cb_ref[...], channels, width))
        mixed = jnp.dot(mix_ref[:, channels:], jnp.concatenate(parts, axis=0), preferred_element_type=F32)
        for q in range(group):
            out_ref[h + q] = mixed[:, q * width : (q + 1) * width] + mb_ref[...]
        return carry

    lax.fori_loop(0, rows // group, body, 0)


def incoming_kernel(own_ref, conv_ref, mix_ref, cb_ref, *refs, pieces, carry, low, group):
    kept_ref, piece_refs = refs[0], refs[1 : 1 + pieces]
    out_ref, carry_refs, (xs, stage, sem) = refs[-4 - carry], refs[-3 - carry : -3], refs[-3:]
    rows, channels, width = own_ref.shape
    count = stage.shape[0]
    flip = flipped()
    held = kept_ref.shape[0]
    xs[0:held] = kept_ref[...]
    for ref in piece_refs:
        size = ref.shape[1]
        xs[held : held + size] = ref[0]
        held += size
    if xs.shape[0] > held:
        xs[held] = jnp.zeros((channels, width), BF16)
    for ref in carry_refs:
        ref[...] = xs[pl.ds(xs.shape[0] - 2, 2)]
    first = lax.axis_index("frames") == 0

    @pl.when(first)
    def _():
        for q in range(count):
            stage[jnp.where(flip, count - 1 - q, q)] = own_ref[low + q].astype(BF16)

    @pl.when(jnp.logical_not(first))
    def _():
        def body(p, carry):
            h = p * group
            columns = [xs[pl.ds(h + q, 3)].reshape(3 * channels, width) for q in range(group)]
            act = conv_rows(columns, conv_ref[...], cb_ref[...], channels, width)
            mixed = jnp.dot(mix_ref[:, :channels], act, preferred_element_type=F32)
            for q in range(group):
                total = own_ref[low + h + q] + mixed[:, q * width : (q + 1) * width]
                stage[jnp.where(flip, count - 1 - h - q, h + q)] = total.astype(BF16)
            return carry

        lax.fori_loop(0, count // group, body, 0)

    copy = pltpu.make_async_copy(stage, out_ref.at[pl.ds(first_row(low, count, rows), count)], sem)
    copy.start()
    copy.wait()


def incoming_rows(out, own, weights, kept, pieces, low, last):
    conv, mix, cb = weights
    rows, channels, width = own.shape
    held = kept.shape[0] + sum(piece.shape[1] for piece in pieces) + (1 if last else 0)
    count = held - 2
    group = next(g for g in (5, 4, 3, 2, 1) if count % g == 0)
    operands = [own, conv, mix, cb, kept, *pieces]
    in_specs = [VMEM] * len(operands)
    two_rows = jax.ShapeDtypeStruct((2, channels, width), BF16)
    aliases = {}
    if out is not None:
        aliases = {len(operands): 0}
        operands.append(out)
        in_specs.append(ANY)
    return pl.pallas_call(
        functools.partial(incoming_kernel, pieces=len(pieces), carry=0 if last else 1, low=low, group=group),
        out_shape=[jax.ShapeDtypeStruct(own.shape, BF16)] + ([] if last else [two_rows]),
        in_specs=in_specs,
        out_specs=[ANY] + ([] if last else [VMEM]),
        input_output_aliases=aliases,
        scratch_shapes=[
            pltpu.VMEM((held, channels, width), BF16),
            pltpu.VMEM((count, channels, width), BF16),
            pltpu.SemaphoreType.DMA,
        ],
        compiler_params=PARAMS,
        cost_estimate=cost(0, 0),
    )(*operands)


def per_device(video, w_spatial, b_spatial, w_temporal, b_temporal):
    frames, rows, width, channels = video.shape
    x = jnp.transpose(video, (0, 1, 3, 2))
    sizes = [5, rows - 10, 4, 1]
    steps = [(0, 2), (2, 3), (3, 4)]
    places = [sum(sizes[:k]) for k in range(len(sizes))]
    spans = [(frames - 1, 1, place, size) for place, size in zip(places, sizes)]

    head_spans = [spans[0], (0, frames, 0, 1)]
    head, boundary = pl.pallas_call(
        functools.partial(slice_kernel, spans=head_spans),
        out_shape=row_shapes(x, head_spans),
        in_specs=[ANY],
        out_specs=[VMEM] * 2,
        scratch_shapes=[pltpu.SemaphoreType.DMA((sizes[0] + 1,))],
        compiler_params=pltpu.CompilerParams(vmem_limit_bytes=HEAD_LIMIT),
    )(x)
    arrived = [lax.ppermute(head, "frames", ring("frames"))]
    beside = lax.ppermute(boundary, "rows", ring("rows"))

    square = jax.ShapeDtypeStruct((3 * channels, 3 * channels), BF16)
    flat = jax.ShapeDtypeStruct((channels, 3 * channels), BF16)
    bias = jax.ShapeDtypeStruct((channels, width), F32)
    conv, mix, cb, mb, piece = pl.pallas_call(
        functools.partial(prepare_kernel, spans=spans[1:2]),
        out_shape=[square, flat, bias, bias] + row_shapes(x, spans[1:2]),
        in_specs=[VMEM] * 5,
        out_specs=[VMEM] * 5,
        compiler_params=PARAMS,
        cost_estimate=cost(0, 2 * 12 * channels * channels * 2),
    )(x, w_spatial, b_spatial.reshape(1, channels), w_temporal, b_temporal.reshape(1, channels))
    arrived.append(lax.ppermute(piece, "frames", ring("frames")))

    own, *pieces = pl.pallas_call(
        functools.partial(own_kernel, group=4, spans=spans[2:]),
        out_shape=[jax.ShapeDtypeStruct((rows, channels, width), F32)] + row_shapes(x, spans[2:]),
        in_specs=[VMEM] * 6,
        out_specs=[VMEM] * (len(sizes) - 1),
        scratch_shapes=[pltpu.VMEM((frames, rows + 2, channels, width), BF16)],
        compiler_params=PARAMS,
        cost_estimate=cost(2 * rows * width * channels * channels * 20, 8 * rows * channels * width),
    )(x, beside, conv, mix, cb, mb)
    arrived += [lax.ppermute(piece, "frames", ring("frames")) for piece in pieces]

    own, arrived[0] = lax.optimization_barrier((own, arrived[0]))
    kept = [lax.ppermute(arrived[0][0, :1], "rows", ring("rows"))]

    weights = (conv, mix, cb)
    out, low = None, 0
    for begin, end in steps:
        out, *kept = incoming_rows(out, own, weights, kept[0], arrived[begin:end], low, end == len(arrived))
        low = places[end - 1] + sizes[end - 1] - 1
    return jnp.transpose(out[None], (0, 1, 3, 2))


def solution(mesh):
    in_specs = (P(("batch", "frames"), "rows", None, None), P(), P(), P(), P())
    out_specs = P(("batch", "frames"), "rows", None, None)
    return jax.shard_map(
        per_device, mesh=mesh, in_specs=in_specs, out_specs=out_specs, check_vma=False
    )
```

```python
import functools

import jax
import jax.numpy as jnp
from jax import lax
from jax.experimental import pallas as pl
from jax.experimental.pallas import tpu as pltpu
from jax.sharding import PartitionSpec as P

F32 = jnp.float32
BF16 = jnp.bfloat16
VMEM = pl.BlockSpec(memory_space=pltpu.VMEM)
ANY = pl.BlockSpec(memory_space=pl.ANY)
HEAD_LIMIT = 53 * 2**20
PARAMS = pltpu.CompilerParams(vmem_limit_bytes=20 * 2**20)


def flipped():
    return lax.axis_index("rows") == 0


def first_row(place, size, rows):
    return jnp.where(flipped(), rows - place - size, place)


def ring(axis):
    count = lax.axis_size(axis)
    return [(i, (i + 1) % count) for i in range(count)]


def cost(flops, moved):
    return pl.CostEstimate(flops=flops, bytes_accessed=moved, transcendentals=0)


def silu(v):
    half = 0.5 * v
    return half + half * jnp.tanh(half)


def span_of(x_ref, span):
    frame, count, place, size = span
    return x_ref.at[pl.ds(frame, count), pl.ds(first_row(place, size, x_ref.shape[1]), size)]


def keep_rows(x_ref, outs, spans):
    for out, span in zip(outs, spans):
        out[...] = span_of(x_ref, span)[...]


def row_shapes(x, spans):
    return [jax.ShapeDtypeStruct((count, size) + x.shape[2:], x.dtype) for _, count, _, size in spans]


def slice_kernel(x_ref, *refs, spans):
    outs, sem = refs[:-1], refs[-1]
    copies = [
        pltpu.make_async_copy(span_of(x_ref, span), out, sem.at[k])
        for k, (out, span) in enumerate(zip(outs, spans))
    ]
    for copy in copies:
        copy.start()
    for copy in copies:
        copy.wait()


def edge_kernel(piece_ref, out_ref):
    size = piece_ref.shape[1]
    out_ref[0] = piece_ref[0, jnp.where(flipped(), size - 1, 0)]


def prepare_kernel(x_ref, ws_ref, bs_ref, wt_ref, bt_ref, conv_ref, mix_ref, cb_ref, mb_ref, *piece_refs, spans):
    keep_rows(x_ref, piece_refs, spans)
    taps, channels = ws_ref.shape[0], ws_ref.shape[2]
    for j in range(taps):
        blocks = [ws_ref[jnp.where(flipped(), taps - 1 - i, i), j] for i in range(taps)]
        conv_ref[j * channels : (j + 1) * channels, :] = jnp.concatenate(blocks, axis=0).T
    mix_ref[...] = wt_ref[...].reshape(taps * channels, channels).T
    width = cb_ref.shape[1]
    cb_ref[...] = jnp.broadcast_to(bs_ref[...], (width, channels)).T
    mb_ref[...] = jnp.broadcast_to(bt_ref[...], (width, channels)).T


def conv_rows(columns, conv, bias, channels, width):
    stacked = jnp.concatenate(columns, axis=1)
    products = jnp.dot(conv, stacked, preferred_element_type=F32)
    lane = lax.broadcasted_iota(jnp.int32, (1, width), 1)
    rows = []
    for q in range(len(columns)):
        part = products[:, q * width : (q + 1) * width]
        left = jnp.where(lane == 0, 0.0, pltpu.roll(part[:channels], 1, 1))
        right = jnp.where(lane == width - 1, 0.0, pltpu.roll(part[2 * channels :], width - 1, 1))
        rows.append(silu(left + part[channels : 2 * channels] + right + bias).astype(BF16))
    return jnp.concatenate(rows, axis=1)


def own_kernel(x_ref, beside_ref, conv_ref, mix_ref, cb_ref, mb_ref, out_ref, *refs, group, spans):
    piece_refs, xs = refs[:-1], refs[-1]
    frames, rows, channels, width = x_ref.shape
    keep_rows(x_ref, piece_refs, spans)
    for f in range(frames):
        xs[f, 0] = beside_ref[f, 0]
        xs[f, rows + 1] = jnp.zeros((channels, width), BF16)

    def fill(s, carry):
        for f in range(frames):
            xs[f, s + 1] = x_ref[f, first_row(s, 1, rows)]
        return carry

    lax.fori_loop(0, rows, fill, 0)

    def body(p, carry):
        h = p * group
        parts = []
        for f in range(frames):
            columns = [xs[f, pl.ds(h + q, 3)].reshape(3 * channels, width) for q in range(group)]
            parts.append(conv_rows(columns, conv_ref[...], cb_ref[...], channels, width))
        mixed = jnp.dot(mix_ref[:, channels:], jnp.concatenate(parts, axis=0), preferred_element_type=F32)
        for q in range(group):
            out_ref[h + q] = mixed[:, q * width : (q + 1) * width] + mb_ref[...]
        return carry

    lax.fori_loop(0, rows // group, body, 0)


def incoming_kernel(own_ref, conv_ref, mix_ref, cb_ref, *refs, pieces, low, count, group, ready, last):
    rows, channels, width = own_ref.shape
    flip = flipped()
    kept_ref, piece_refs, refs = refs[0], refs[1 : 1 + pieces], refs[1 + pieces :]
    copies = []
    if ready:
        ready_ref, refs = refs[0], refs[1:]
        refs = refs[1:] if low > ready else refs
        out_ref, refs = refs[0], refs[1:]
        sem, refs = refs[-1], refs[:-1]
        place = first_row(low - ready, ready, rows)
        copies.append(pltpu.make_async_copy(ready_ref, out_ref.at[pl.ds(place, ready)], sem.at[0]))
        copies[0].start()
    made_ref, carry_refs, xs = (refs[1], [], refs[0]) if last else (refs[0], [refs[1]], refs[2])
    held = kept_ref.shape[0]
    xs[0:held] = kept_ref[...]
    for ref in piece_refs:
        size = ref.shape[1]
        for k in range(size):
            xs[held + k] = ref[0, jnp.where(flip, size - 1 - k, k)]
        held += size
    if last:
        xs[held] = jnp.zeros((channels, width), BF16)
    for ref in carry_refs:
        ref[...] = xs[pl.ds(held - 2, 2)]
    first = lax.axis_index("frames") == 0

    @pl.when(first)
    def _():
        for q in range(count):
            made_ref[jnp.where(flip, count - 1 - q, q)] = own_ref[low + q].astype(BF16)

    @pl.when(jnp.logical_not(first))
    def _():
        def body(p, carry):
            h = p * group
            columns = [xs[pl.ds(h + q, 3)].reshape(3 * channels, width) for q in range(group)]
            act = conv_rows(columns, conv_ref[...], cb_ref[...], channels, width)
            mixed = jnp.dot(mix_ref[:, :channels], act, preferred_element_type=F32)
            for q in range(group):
                total = own_ref[low + h + q] + mixed[:, q * width : (q + 1) * width]
                made_ref[jnp.where(flip, count - 1 - h - q, h + q)] = total.astype(BF16)
            return carry

        lax.fori_loop(0, count // group, body, 0)

    if last:
        place = first_row(low, count, rows)
        copies.append(pltpu.make_async_copy(made_ref, out_ref.at[pl.ds(place, count)], sem.at[1]))
        copies[-1].start()
    for copy in copies:
        copy.wait()


def incoming_rows(out, made, own, weights, kept, pieces, low, last):
    conv, mix, cb = weights
    rows, channels, width = own.shape
    held = kept.shape[0] + sum(piece.shape[1] for piece in pieces) + (1 if last else 0)
    count = held - 2
    group = next(g for g in (5, 4, 3, 2, 1) if count % g == 0)
    row_array = lambda n: jax.ShapeDtypeStruct((n, channels, width), BF16)
    operands = [own, conv, mix, cb, kept, *pieces]
    in_specs = [VMEM] * len(operands)
    out_shape, out_specs, scratch, aliases = [], [], [pltpu.VMEM((held, channels, width), BF16)], {}
    if made is not None:
        operands.append(made)
        in_specs.append(VMEM)
        if out is not None:
            aliases = {len(operands): 0}
            operands.append(out)
            in_specs.append(ANY)
        out_shape.append(row_array(rows))
        out_specs.append(ANY)
    if last:
        scratch.append(pltpu.VMEM((count, channels, width), BF16))
    else:
        out_shape += [row_array(count), row_array(2)]
        out_specs += [VMEM] * 2
    if made is not None:
        scratch.append(pltpu.SemaphoreType.DMA((2,)))
    results = pl.pallas_call(
        functools.partial(
            incoming_kernel,
            pieces=len(pieces),
            low=low,
            count=count,
            group=group,
            ready=0 if made is None else made.shape[0],
            last=last,
        ),
        out_shape=out_shape,
        in_specs=in_specs,
        out_specs=out_specs,
        input_output_aliases=aliases,
        scratch_shapes=scratch,
        compiler_params=PARAMS,
        cost_estimate=cost(0, 0),
    )(*operands)
    if last:
        return results[0], None, None
    return (None if made is None else results[0]), results[-2], results[-1]


def per_device(video, w_spatial, b_spatial, w_temporal, b_temporal):
    frames, rows, width, channels = video.shape
    x = jnp.transpose(video, (0, 1, 3, 2))
    sizes, early, steps = [5, 4, 4, 2, 1], 2, [(0, 2), (2, 3), (3, 4), (4, 5)]
    places = [sum(sizes[:k]) for k in range(len(sizes))]
    spans = [(frames - 1, 1, place, size) for place, size in zip(places, sizes)]

    head_spans = [spans[0], (0, frames, 0, 1)]
    head, boundary = pl.pallas_call(
        functools.partial(slice_kernel, spans=head_spans),
        out_shape=row_shapes(x, head_spans),
        in_specs=[ANY],
        out_specs=[VMEM] * 2,
        scratch_shapes=[pltpu.SemaphoreType.DMA((2,))],
        compiler_params=pltpu.CompilerParams(vmem_limit_bytes=HEAD_LIMIT),
    )(x)
    arrived = [lax.ppermute(head, "frames", ring("frames"))]
    beside = lax.ppermute(boundary, "rows", ring("rows"))

    square = jax.ShapeDtypeStruct((3 * channels, 3 * channels), BF16)
    flat = jax.ShapeDtypeStruct((channels, 3 * channels), BF16)
    bias = jax.ShapeDtypeStruct((channels, width), F32)
    late = spans[1 + early :]
    conv, mix, cb, mb, *pieces = pl.pallas_call(
        functools.partial(prepare_kernel, spans=spans[1 : 1 + early]),
        out_shape=[square, flat, bias, bias] + row_shapes(x, spans[1 : 1 + early]),
        in_specs=[VMEM] * 5,
        out_specs=[VMEM] * (4 + early),
        compiler_params=PARAMS,
        cost_estimate=cost(0, 2 * 12 * channels * channels * 2),
    )(x, w_spatial, b_spatial.reshape(1, channels), w_temporal, b_temporal.reshape(1, channels))
    arrived += [lax.ppermute(piece, "frames", ring("frames")) for piece in pieces]

    own, *pieces = pl.pallas_call(
        functools.partial(own_kernel, group=4, spans=late),
        out_shape=[jax.ShapeDtypeStruct((rows, channels, width), F32)] + row_shapes(x, late),
        in_specs=[VMEM] * 6,
        out_specs=[VMEM] * (1 + len(late)),
        scratch_shapes=[pltpu.VMEM((frames, rows + 2, channels, width), BF16)],
        compiler_params=PARAMS,
        cost_estimate=cost(2 * rows * width * channels * channels * 20, 8 * rows * channels * width),
    )(x, beside, conv, mix, cb, mb)
    arrived += [lax.ppermute(piece, "frames", ring("frames")) for piece in pieces]

    own, arrived[0] = lax.optimization_barrier((own, arrived[0]))
    edge = pl.pallas_call(
        edge_kernel,
        out_shape=jax.ShapeDtypeStruct((1, channels, width), BF16),
        in_specs=[VMEM],
        out_specs=VMEM,
        compiler_params=PARAMS,
        cost_estimate=cost(0, 0),
    )(arrived[0])
    kept = lax.ppermute(edge, "rows", ring("rows"))

    weights = (conv, mix, cb)
    out, made, low = None, None, 0
    for begin, end in steps:
        last = end == len(arrived)
        out, made, kept = incoming_rows(out, made, own, weights, kept, arrived[begin:end], low, last)
        low = places[end - 1] + sizes[end - 1] - 1
    return jnp.transpose(out[None], (0, 1, 3, 2))


def solution(mesh):
    in_specs = (P(("batch", "frames"), "rows", None, None), P(), P(), P(), P())
    out_specs = P(("batch", "frames"), "rows", None, None)
    return jax.shard_map(
        per_device, mesh=mesh, in_specs=in_specs, out_specs=out_specs, check_vma=False
    )
```

```python
import functools

import jax
import jax.numpy as jnp
from jax import lax
from jax.experimental import pallas as pl
from jax.experimental.pallas import tpu as pltpu
from jax.sharding import PartitionSpec as P

F32 = jnp.float32
BF16 = jnp.bfloat16
VMEM = pl.BlockSpec(memory_space=pltpu.VMEM)
ANY = pl.BlockSpec(memory_space=pl.ANY)
HEAD_LIMIT = 53 * 2**20
OPEN, CLOSING, LAST = range(3)
PARAMS = pltpu.CompilerParams(vmem_limit_bytes=20 * 2**20)


def flipped():
    return lax.axis_index("rows") == 0


def first_row(place, size, rows):
    return jnp.where(flipped(), rows - place - size, place)


def ring(axis):
    count = lax.axis_size(axis)
    return [(i, (i + 1) % count) for i in range(count)]


def cost(flops, moved):
    return pl.CostEstimate(flops=flops, bytes_accessed=moved, transcendentals=0)


def silu(v):
    half = 0.5 * v
    return half + half * jnp.tanh(half)


def span_of(x_ref, span):
    frame, count, place, size = span
    return x_ref.at[pl.ds(frame, count), pl.ds(first_row(place, size, x_ref.shape[1]), size)]


def keep_rows(x_ref, outs, spans):
    for out, span in zip(outs, spans):
        out[...] = span_of(x_ref, span)[...]


def row_shapes(x, spans):
    return [jax.ShapeDtypeStruct((count, size) + x.shape[2:], x.dtype) for _, count, _, size in spans]


def slice_kernel(x_ref, *refs, spans):
    outs, sem = refs[:-1], refs[-1]
    copies = [
        pltpu.make_async_copy(span_of(x_ref, span), out, sem.at[k])
        for k, (out, span) in enumerate(zip(outs, spans))
    ]
    for copy in copies:
        copy.start()
    for copy in copies:
        copy.wait()


def edge_kernel(piece_ref, out_ref):
    size = piece_ref.shape[1]
    out_ref[0] = piece_ref[0, jnp.where(flipped(), size - 1, 0)]


def prepare_kernel(x_ref, ws_ref, bs_ref, wt_ref, bt_ref, conv_ref, mix_ref, cb_ref, mb_ref, *piece_refs, spans):
    keep_rows(x_ref, piece_refs, spans)
    taps, channels = ws_ref.shape[0], ws_ref.shape[2]
    for j in range(taps):
        blocks = [ws_ref[jnp.where(flipped(), taps - 1 - i, i), j] for i in range(taps)]
        conv_ref[j * channels : (j + 1) * channels, :] = jnp.concatenate(blocks, axis=0).T
    mix_ref[...] = wt_ref[...].reshape(taps * channels, channels).T
    width = cb_ref.shape[1]
    cb_ref[...] = jnp.broadcast_to(bs_ref[...], (width, channels)).T
    mb_ref[...] = jnp.broadcast_to(bt_ref[...], (width, channels)).T


def conv_rows(columns, conv, bias, channels, width):
    stacked = jnp.concatenate(columns, axis=1)
    products = jnp.dot(conv, stacked, preferred_element_type=F32)
    lane = lax.broadcasted_iota(jnp.int32, (1, width), 1)
    rows = []
    for q in range(len(columns)):
        part = products[:, q * width : (q + 1) * width]
        left = jnp.where(lane == 0, 0.0, pltpu.roll(part[:channels], 1, 1))
        right = jnp.where(lane == width - 1, 0.0, pltpu.roll(part[2 * channels :], width - 1, 1))
        rows.append(silu(left + part[channels : 2 * channels] + right + bias).astype(BF16))
    return jnp.concatenate(rows, axis=1)


def own_kernel(x_ref, beside_ref, conv_ref, mix_ref, cb_ref, mb_ref, out_ref, *refs, group, spans):
    piece_refs, xs = refs[:-1], refs[-1]
    frames, rows, channels, width = x_ref.shape
    keep_rows(x_ref, piece_refs, spans)
    for f in range(frames):
        xs[f, 0] = beside_ref[f, 0]
        xs[f, rows + 1] = jnp.zeros((channels, width), BF16)

    def fill(s, carry):
        for f in range(frames):
            xs[f, s + 1] = x_ref[f, first_row(s, 1, rows)]
        return carry

    lax.fori_loop(0, rows, fill, 0)

    def body(p, carry):
        h = p * group
        parts = []
        for f in range(frames):
            columns = [xs[f, pl.ds(h + q, 3)].reshape(3 * channels, width) for q in range(group)]
            parts.append(conv_rows(columns, conv_ref[...], cb_ref[...], channels, width))
        mixed = jnp.dot(mix_ref[:, channels:], jnp.concatenate(parts, axis=0), preferred_element_type=F32)
        for q in range(group):
            out_ref[h + q] = mixed[:, q * width : (q + 1) * width] + mb_ref[...]
        return carry

    lax.fori_loop(0, rows // group, body, 0)


def incoming_kernel(own_ref, conv_ref, mix_ref, cb_ref, *refs, pieces, low, count, group, ready, stage):
    rows, channels, width = own_ref.shape
    flip = flipped()
    first = lax.axis_index("frames") == 0
    kept_ref, piece_refs, refs = refs[0], refs[1 : 1 + pieces], refs[1 + pieces :]
    ready_ref = out_ref = sem = None
    if ready:
        ready_ref, refs = refs[0], refs[1 + (low > ready) :]
        out_ref, refs, sem = refs[0], refs[1:-1], refs[-1]
    if stage == LAST:
        xs, made_ref = refs
    else:
        made_ref, carry_ref, xs = refs[:3]

    def to_output(source, place, size, k):
        target = out_ref.at[pl.ds(first_row(place, size, rows), size)]
        return pltpu.make_async_copy(source, target, sem.at[k])

    def own_rows(target, size):
        for q in range(size):
            target[jnp.where(flip, size - 1 - q, q)] = own_ref[low + q].astype(BF16)

    def convolve():
        held = kept_ref.shape[0]
        xs[0:held] = kept_ref[...]
        for ref in piece_refs:
            size = ref.shape[1]
            for k in range(size):
                xs[held + k] = ref[0, jnp.where(flip, size - 1 - k, k)]
            held += size
        if stage == LAST:
            xs[held] = jnp.zeros((channels, width), BF16)
        else:
            carry_ref[...] = xs[pl.ds(held - 2, 2)]

        def body(p, carry):
            h = p * group
            columns = [xs[pl.ds(h + q, 3)].reshape(3 * channels, width) for q in range(group)]
            act = conv_rows(columns, conv_ref[...], cb_ref[...], channels, width)
            mixed = jnp.dot(mix_ref[:, :channels], act, preferred_element_type=F32)
            for q in range(group):
                total = own_ref[low + h + q] + mixed[:, q * width : (q + 1) * width]
                made_ref[jnp.where(flip, count - 1 - h - q, h + q)] = total.astype(BF16)
            return carry

        lax.fori_loop(0, count // group, body, 0)

    if stage == LAST:

        @pl.when(jnp.logical_not(first))
        def _():
            before = to_output(ready_ref, low - ready, ready, 0)
            before.start()
            convolve()
            after = to_output(made_ref, low, count, 1)
            after.start()
            before.wait()
            after.wait()

        return

    before = to_output(ready_ref, low - ready, ready, 0) if ready else None
    if ready:
        before.start()

    @pl.when(first)
    def _():
        if stage == CLOSING:
            rest = refs[3]
            own_rows(rest, rows - low)
            after = to_output(rest, low, rows - low, 1)
            after.start()
            after.wait()
        else:
            own_rows(made_ref, count)

    @pl.when(jnp.logical_not(first))
    def _():
        convolve()

    if ready:
        before.wait()


def incoming_rows(out, made, own, weights, kept, pieces, low, stage):
    conv, mix, cb = weights
    rows, channels, width = own.shape
    held = kept.shape[0] + sum(piece.shape[1] for piece in pieces) + (stage == LAST)
    count = held - 2
    ready = 0 if made is None else made.shape[0]
    group = next(g for g in (5, 4, 3, 2, 1) if count % g == 0)

    def row_array(size):
        return jax.ShapeDtypeStruct((size, channels, width), BF16)

    operands = [own, conv, mix, cb, kept, *pieces]
    in_specs = [VMEM] * len(operands)
    out_shape, out_specs, aliases = [], [], {}
    if ready:
        operands.append(made)
        in_specs.append(VMEM)
        if out is not None:
            aliases = {len(operands): 0}
            operands.append(out)
            in_specs.append(ANY)
        out_shape.append(row_array(rows))
        out_specs.append(ANY)
    if stage != LAST:
        out_shape += [row_array(count), row_array(2)]
        out_specs += [VMEM] * 2
    scratch = [pltpu.VMEM((held, channels, width), BF16)]
    if stage == LAST:
        scratch.append(pltpu.VMEM((count, channels, width), BF16))
    if stage == CLOSING:
        scratch.append(pltpu.VMEM((rows - low, channels, width), BF16))
    if ready:
        scratch.append(pltpu.SemaphoreType.DMA((2,)))
    results = pl.pallas_call(
        functools.partial(
            incoming_kernel, pieces=len(pieces), low=low, count=count, group=group, ready=ready, stage=stage
        ),
        out_shape=out_shape,
        in_specs=in_specs,
        out_specs=out_specs,
        input_output_aliases=aliases,
        scratch_shapes=scratch,
        compiler_params=PARAMS,
        cost_estimate=cost(0, 0),
    )(*operands)
    if stage == LAST:
        return results[0], None, None
    return (results[0] if ready else None), results[-2], results[-1]


def per_device(video, w_spatial, b_spatial, w_temporal, b_temporal):
    frames, rows, width, channels = video.shape
    x = jnp.transpose(video, (0, 1, 3, 2))
    sizes, early, steps = [5, 4, 4, 2, 1], 2, [(0, 2), (2, 3), (3, 4), (4, 5)]
    places = [sum(sizes[:k]) for k in range(len(sizes))]
    spans = [(frames - 1, 1, place, size) for place, size in zip(places, sizes)]

    head_spans = [spans[0], (0, frames, 0, 1)]
    head, boundary = pl.pallas_call(
        functools.partial(slice_kernel, spans=head_spans),
        out_shape=row_shapes(x, head_spans),
        in_specs=[ANY],
        out_specs=[VMEM] * 2,
        scratch_shapes=[pltpu.SemaphoreType.DMA((2,))],
        compiler_params=pltpu.CompilerParams(vmem_limit_bytes=HEAD_LIMIT),
    )(x)
    arrived = [lax.ppermute(head, "frames", ring("frames"))]
    beside = lax.ppermute(boundary, "rows", ring("rows"))

    square = jax.ShapeDtypeStruct((3 * channels, 3 * channels), BF16)
    flat = jax.ShapeDtypeStruct((channels, 3 * channels), BF16)
    bias = jax.ShapeDtypeStruct((channels, width), F32)
    late = spans[1 + early :]
    conv, mix, cb, mb, *pieces = pl.pallas_call(
        functools.partial(prepare_kernel, spans=spans[1 : 1 + early]),
        out_shape=[square, flat, bias, bias] + row_shapes(x, spans[1 : 1 + early]),
        in_specs=[VMEM] * 5,
        out_specs=[VMEM] * (4 + early),
        compiler_params=PARAMS,
        cost_estimate=cost(0, 2 * 12 * channels * channels * 2),
    )(x, w_spatial, b_spatial.reshape(1, channels), w_temporal, b_temporal.reshape(1, channels))
    arrived += [lax.ppermute(piece, "frames", ring("frames")) for piece in pieces]

    own, *pieces = pl.pallas_call(
        functools.partial(own_kernel, group=4, spans=late),
        out_shape=[jax.ShapeDtypeStruct((rows, channels, width), F32)] + row_shapes(x, late),
        in_specs=[VMEM] * 6,
        out_specs=[VMEM] * (1 + len(late)),
        scratch_shapes=[pltpu.VMEM((frames, rows + 2, channels, width), BF16)],
        compiler_params=PARAMS,
        cost_estimate=cost(2 * rows * width * channels * channels * 20, 8 * rows * channels * width),
    )(x, beside, conv, mix, cb, mb)
    arrived += [lax.ppermute(piece, "frames", ring("frames")) for piece in pieces]

    own, arrived[0] = lax.optimization_barrier((own, arrived[0]))
    edge = pl.pallas_call(
        edge_kernel,
        out_shape=jax.ShapeDtypeStruct((1, channels, width), BF16),
        in_specs=[VMEM],
        out_specs=VMEM,
        compiler_params=PARAMS,
        cost_estimate=cost(0, 0),
    )(arrived[0])
    kept = lax.ppermute(edge, "rows", ring("rows"))

    weights = (conv, mix, cb)
    out, made, low = None, None, 0
    for begin, end in steps:
        stage = {len(arrived): LAST, steps[-1][0]: CLOSING}.get(end, OPEN)
        out, made, kept = incoming_rows(out, made, own, weights, kept, arrived[begin:end], low, stage)
        low = places[end - 1] + sizes[end - 1] - 1
    return jnp.transpose(out[None], (0, 1, 3, 2))


def solution(mesh):
    in_specs = (P(("batch", "frames"), "rows", None, None), P(), P(), P(), P())
    out_specs = P(("batch", "frames"), "rows", None, None)
    return jax.shard_map(
        per_device, mesh=mesh, in_specs=in_specs, out_specs=out_specs, check_vma=False
    )
```

```python
import functools

import jax
import jax.numpy as jnp
from jax import lax
from jax.experimental import pallas as pl
from jax.experimental.pallas import tpu as pltpu
from jax.sharding import PartitionSpec as P

F32 = jnp.float32
BF16 = jnp.bfloat16
VMEM = pl.BlockSpec(memory_space=pltpu.VMEM)
ANY = pl.BlockSpec(memory_space=pl.ANY)
HEAD_LIMIT = 53 * 2**20
LOAD_LIMIT = 50 * 2**20
OPEN, CLOSING, LATE, LAST = range(4)
PARAMS = pltpu.CompilerParams(vmem_limit_bytes=20 * 2**20)


def flipped():
    return lax.axis_index("rows") == 0


def first_row(place, size, rows):
    return jnp.where(flipped(), rows - place - size, place)


def ring(axis):
    count = lax.axis_size(axis)
    return [(i, (i + 1) % count) for i in range(count)]


def next_odd(piece, axis):
    count = lax.axis_size(axis)
    if count % 2:
        return piece
    return lax.ppermute(piece, axis, [(i, (i + 2 * (i % 2)) % count) for i in range(count)])


def within_pairs(piece, axis, keep):
    count = lax.axis_size(axis)
    route = ring(axis) if count % 2 else [(i, i ^ 1) for i in range(count)]
    return lax.ppermute(piece, axis, [(a, b) for a, b in route if b or keep])


def cost(flops, moved):
    return pl.CostEstimate(flops=flops, bytes_accessed=moved, transcendentals=0)


def silu(v):
    half = 0.5 * v
    return half + half * jnp.tanh(half)


def span_of(x_ref, span):
    frame, count, place, size = span
    return x_ref.at[pl.ds(frame, count), pl.ds(first_row(place, size, x_ref.shape[1]), size)]


def keep_rows(x_ref, outs, spans):
    for out, span in zip(outs, spans):
        out[...] = span_of(x_ref, span)[...]


def row_shapes(x, spans):
    return [jax.ShapeDtypeStruct((count, size) + x.shape[2:], x.dtype) for _, count, _, size in spans]


def slice_kernel(x_ref, *refs, spans):
    outs, sem = refs[:-1], refs[-1]
    copies = [
        pltpu.make_async_copy(span_of(x_ref, span), out, sem.at[k])
        for k, (out, span) in enumerate(zip(outs, spans))
    ]
    for copy in copies:
        copy.start()
    for copy in copies:
        copy.wait()


def edge_kernel(piece_ref, tail_ref, out_ref, *tail_out_refs):
    size = piece_ref.shape[1]
    out_ref[0] = piece_ref[0, jnp.where(flipped(), size - 1, 0)]
    place, size = 0, tail_ref.shape[1]
    for ref in tail_out_refs:
        ref[...] = span_of(tail_ref, (0, 1, place, ref.shape[1]))[...]
        place += ref.shape[1]


def prepare_kernel(x_ref, ws_ref, bs_ref, wt_ref, bt_ref, conv_ref, mix_ref, cb_ref, mb_ref, *piece_refs, spans):
    keep_rows(x_ref, piece_refs, spans)
    taps, channels = ws_ref.shape[0], ws_ref.shape[2]
    for j in range(taps):
        blocks = [ws_ref[jnp.where(flipped(), taps - 1 - i, i), j] for i in range(taps)]
        conv_ref[j * channels : (j + 1) * channels, :] = jnp.concatenate(blocks, axis=0).T
    mix_ref[...] = wt_ref[...].reshape(taps * channels, channels).T
    width = cb_ref.shape[1]
    cb_ref[...] = jnp.broadcast_to(bs_ref[...], (width, channels)).T
    mb_ref[...] = jnp.broadcast_to(bt_ref[...], (width, channels)).T


def conv_rows(columns, conv, bias, channels, width):
    stacked = jnp.concatenate(columns, axis=1)
    products = jnp.dot(conv, stacked, preferred_element_type=F32)
    lane = lax.broadcasted_iota(jnp.int32, (1, width), 1)
    rows = []
    for q in range(len(columns)):
        part = products[:, q * width : (q + 1) * width]
        left = jnp.where(lane == 0, 0.0, pltpu.roll(part[:channels], 1, 1))
        right = jnp.where(lane == width - 1, 0.0, pltpu.roll(part[2 * channels :], width - 1, 1))
        rows.append(silu(left + part[channels : 2 * channels] + right + bias).astype(BF16))
    return jnp.concatenate(rows, axis=1)


def own_kernel(x_ref, beside_ref, conv_ref, mix_ref, cb_ref, mb_ref, out_ref, *refs, group, spans):
    piece_refs, xs = refs[:-1], refs[-1]
    frames, rows, channels, width = x_ref.shape
    keep_rows(x_ref, piece_refs, spans)
    for f in range(frames):
        xs[f, 0] = beside_ref[f, 0]
        xs[f, rows + 1] = jnp.zeros((channels, width), BF16)

    def fill(s, carry):
        for f in range(frames):
            xs[f, s + 1] = x_ref[f, first_row(s, 1, rows)]
        return carry

    lax.fori_loop(0, rows, fill, 0)

    def body(p, carry):
        h = p * group
        parts = []
        for f in range(frames):
            columns = [xs[f, pl.ds(h + q, 3)].reshape(3 * channels, width) for q in range(group)]
            parts.append(conv_rows(columns, conv_ref[...], cb_ref[...], channels, width))
        mixed = jnp.dot(mix_ref[:, channels:], jnp.concatenate(parts, axis=0), preferred_element_type=F32)
        for q in range(group):
            out_ref[h + q] = mixed[:, q * width : (q + 1) * width] + mb_ref[...]
        return carry

    lax.fori_loop(0, rows // group, body, 0)


def incoming_kernel(own_ref, conv_ref, mix_ref, cb_ref, *refs, pieces, low, count, group, ready, stage):
    rows, channels, width = own_ref.shape
    flip = flipped()
    first = lax.axis_index("frames") == 0
    kept_ref, piece_refs, refs = refs[0], refs[1 : 1 + pieces], refs[1 + pieces :]
    ready_ref = out_ref = sem = None
    if ready:
        ready_ref, refs = refs[0], refs[1 + (low > ready) :]
        out_ref, refs, sem = refs[0], refs[1:-1], refs[-1]
    if stage == LAST:
        xs, made_ref = refs
    else:
        made_ref, carry_ref, xs = refs[:3]

    def to_output(source, place, size, k):
        target = out_ref.at[pl.ds(first_row(place, size, rows), size)]
        return pltpu.make_async_copy(source, target, sem.at[k])

    def own_rows(target, size):
        for q in range(size):
            target[jnp.where(flip, size - 1 - q, q)] = own_ref[low + q].astype(BF16)

    def convolve():
        held = kept_ref.shape[0]
        xs[0:held] = kept_ref[...]
        for ref in piece_refs:
            size = ref.shape[1]
            for k in range(size):
                xs[held + k] = ref[0, jnp.where(flip, size - 1 - k, k)]
            held += size
        if stage == LAST:
            xs[held] = jnp.zeros((channels, width), BF16)
        else:
            carry_ref[...] = xs[pl.ds(held - 2, 2)]

        def body(p, carry):
            h = p * group
            columns = [xs[pl.ds(h + q, 3)].reshape(3 * channels, width) for q in range(group)]
            act = conv_rows(columns, conv_ref[...], cb_ref[...], channels, width)
            mixed = jnp.dot(mix_ref[:, :channels], act, preferred_element_type=F32)
            for q in range(group):
                total = own_ref[low + h + q] + mixed[:, q * width : (q + 1) * width]
                made_ref[jnp.where(flip, count - 1 - h - q, h + q)] = total.astype(BF16)
            return carry

        lax.fori_loop(0, count // group, body, 0)

    if stage == OPEN:

        @pl.when(first)
        def _():
            own_rows(made_ref, count)

        @pl.when(jnp.logical_not(first))
        def _():
            convolve()

        return

    before = to_output(ready_ref, low - ready, ready, 0)
    if stage == CLOSING:

        @pl.when(first)
        def _():
            rest = refs[3]
            own_rows(rest, rows - low)
            after = to_output(rest, low, rows - low, 1)
            before.start()
            after.start()
            before.wait()
            after.wait()

    @pl.when(jnp.logical_not(first))
    def _():
        before.start()
        convolve()
        if stage == LAST:
            after = to_output(made_ref, low, count, 1)
            after.start()
            after.wait()
        before.wait()


def incoming_rows(out, made, own, weights, kept, pieces, low, stage):
    conv, mix, cb = weights
    rows, channels, width = own.shape
    held = kept.shape[0] + sum(piece.shape[1] for piece in pieces) + (stage == LAST)
    count = held - 2
    ready = 0 if made is None else made.shape[0]
    group = next(g for g in (5, 4, 3, 2, 1) if count % g == 0)

    def row_array(size):
        return jax.ShapeDtypeStruct((size, channels, width), BF16)

    operands = [own, conv, mix, cb, kept, *pieces]
    in_specs = [VMEM] * len(operands)
    out_shape, out_specs, aliases = [], [], {}
    if ready:
        operands.append(made)
        in_specs.append(VMEM)
        if out is not None:
            aliases = {len(operands): 0}
            operands.append(out)
            in_specs.append(ANY)
        out_shape.append(row_array(rows))
        out_specs.append(ANY)
    if stage != LAST:
        out_shape += [row_array(count), row_array(2)]
        out_specs += [VMEM] * 2
    scratch = [pltpu.VMEM((held, channels, width), BF16)]
    if stage == LAST:
        scratch.append(pltpu.VMEM((count, channels, width), BF16))
    if stage == CLOSING:
        scratch.append(pltpu.VMEM((rows - low, channels, width), BF16))
    if ready:
        scratch.append(pltpu.SemaphoreType.DMA((2,)))
    results = pl.pallas_call(
        functools.partial(
            incoming_kernel, pieces=len(pieces), low=low, count=count, group=group, ready=ready, stage=stage
        ),
        out_shape=out_shape,
        in_specs=in_specs,
        out_specs=out_specs,
        input_output_aliases=aliases,
        scratch_shapes=scratch,
        compiler_params=PARAMS,
        cost_estimate=cost(0, 0),
    )(*operands)
    if stage == LAST:
        return results[0], None, None
    return (results[0] if ready else None), results[-2], results[-1]


def per_device(video, w_spatial, b_spatial, w_temporal, b_temporal):
    frames, rows, width, channels = video.shape
    x = jnp.transpose(video, (0, 1, 3, 2))
    sizes, early, steps = [5, 4, 4, 2, 1], 2, [(0, 2), (2, 3), (3, 4), (4, 5)]
    places = [sum(sizes[:k]) for k in range(len(sizes))]
    spans = [(frames - 1, 1, place, size) for place, size in zip(places, sizes)]

    head_spans = [spans[0], (0, frames, 0, 1)]
    head, boundary = pl.pallas_call(
        functools.partial(slice_kernel, spans=head_spans),
        out_shape=row_shapes(x, head_spans),
        in_specs=[ANY],
        out_specs=[VMEM] * 2,
        scratch_shapes=[pltpu.SemaphoreType.DMA((2,))],
        compiler_params=pltpu.CompilerParams(vmem_limit_bytes=HEAD_LIMIT),
    )(x)
    whole = [(0, frames, 0, rows), (frames - 1, 1, places[-2], sizes[-2] + sizes[-1])]
    x, tail = pl.pallas_call(
        functools.partial(slice_kernel, spans=whole),
        out_shape=row_shapes(x, whole),
        in_specs=[ANY],
        out_specs=[VMEM] * 2,
        scratch_shapes=[pltpu.SemaphoreType.DMA((2,))],
        compiler_params=pltpu.CompilerParams(vmem_limit_bytes=LOAD_LIMIT),
        cost_estimate=cost(0, 0),
    )(x)
    arrived = [lax.ppermute(head, "frames", ring("frames"))]
    tail = next_odd(tail, "frames")
    beside = lax.ppermute(boundary, "rows", ring("rows"))

    square = jax.ShapeDtypeStruct((3 * channels, 3 * channels), BF16)
    flat = jax.ShapeDtypeStruct((channels, 3 * channels), BF16)
    bias = jax.ShapeDtypeStruct((channels, width), F32)
    late = spans[1 + early : -2]
    conv, mix, cb, mb, *pieces = pl.pallas_call(
        functools.partial(prepare_kernel, spans=spans[1 : 1 + early]),
        out_shape=[square, flat, bias, bias] + row_shapes(x, spans[1 : 1 + early]),
        in_specs=[VMEM] * 5,
        out_specs=[VMEM] * (4 + early),
        compiler_params=PARAMS,
        cost_estimate=cost(0, 2 * 12 * channels * channels * 2),
    )(x, w_spatial, b_spatial.reshape(1, channels), w_temporal, b_temporal.reshape(1, channels))
    arrived += [lax.ppermute(piece, "frames", ring("frames")) for piece in pieces]

    (own,) = pl.pallas_call(
        functools.partial(own_kernel, group=4, spans=late),
        out_shape=[jax.ShapeDtypeStruct((rows, channels, width), F32)] + row_shapes(x, late),
        in_specs=[VMEM] * 6,
        out_specs=[VMEM] * (1 + len(late)),
        scratch_shapes=[pltpu.VMEM((frames, rows + 2, channels, width), BF16)],
        compiler_params=PARAMS,
        cost_estimate=cost(2 * rows * width * channels * channels * 20, 8 * rows * channels * width),
    )(x, beside, conv, mix, cb, mb)
    own, arrived[0] = lax.optimization_barrier((own, arrived[0]))
    edge, *pieces = pl.pallas_call(
        edge_kernel,
        out_shape=[jax.ShapeDtypeStruct((1, channels, width), BF16)] + row_shapes(x, spans[-2:]),
        in_specs=[VMEM] * 2,
        out_specs=[VMEM] * 3,
        compiler_params=PARAMS,
        cost_estimate=cost(0, 0),
    )(arrived[0], tail)
    arrived += [within_pairs(piece, "frames", piece is pieces[0]) for piece in pieces]
    kept = lax.ppermute(edge, "rows", ring("rows"))

    weights = (conv, mix, cb)
    out, made, low = None, None, 0
    for k, (begin, end) in enumerate(steps):
        stage = LAST if end == len(arrived) else min(k, LATE)
        out, made, kept = incoming_rows(out, made, own, weights, kept, arrived[begin:end], low, stage)
        low = places[end - 1] + sizes[end - 1] - 1
    return jnp.transpose(out[None], (0, 1, 3, 2))


def solution(mesh):
    in_specs = (P(("batch", "frames"), "rows", None, None), P(), P(), P(), P())
    out_specs = P(("batch", "frames"), "rows", None, None)
    return jax.shard_map(
        per_device, mesh=mesh, in_specs=in_specs, out_specs=out_specs, check_vma=False
    )
```

```python
import functools

import jax
import jax.numpy as jnp
from jax import lax
from jax.experimental import pallas as pl
from jax.experimental.pallas import tpu as pltpu
from jax.sharding import PartitionSpec as P

F32 = jnp.float32
BF16 = jnp.bfloat16
VMEM = pl.BlockSpec(memory_space=pltpu.VMEM)
ANY = pl.BlockSpec(memory_space=pl.ANY)
HEAD_LIMIT = 53 * 2**20
LOAD_LIMIT = 50 * 2**20
OPEN, CLOSING, LATE, LAST = range(4)
PARAMS = pltpu.CompilerParams(vmem_limit_bytes=20 * 2**20)


def flipped():
    return lax.axis_index("rows") == 0


def first_row(place, size, rows):
    return jnp.where(flipped(), rows - place - size, place)


def ring(axis):
    count = lax.axis_size(axis)
    return [(i, (i + 1) % count) for i in range(count)]


def next_odd(piece, axis):
    count = lax.axis_size(axis)
    if count % 2:
        return piece
    return lax.ppermute(piece, axis, [(i, (i + 2 * (i % 2)) % count) for i in range(count)])


def within_pairs(piece, axis, keep):
    count = lax.axis_size(axis)
    route = ring(axis) if count % 2 else [(i, i ^ 1) for i in range(count)]
    return lax.ppermute(piece, axis, [(a, b) for a, b in route if b or keep])


def cost(flops, moved):
    return pl.CostEstimate(flops=flops, bytes_accessed=moved, transcendentals=0)


def silu(v):
    half = 0.5 * v
    return half + half * jnp.tanh(half)


def span_of(x_ref, span):
    frame, count, place, size = span
    return x_ref.at[pl.ds(frame, count), pl.ds(first_row(place, size, x_ref.shape[1]), size)]


def keep_rows(x_ref, outs, spans):
    for out, span in zip(outs, spans):
        out[...] = span_of(x_ref, span)[...]


def keep_kernel(x_ref, *outs, spans):
    keep_rows(x_ref, outs, spans)


def row_shapes(x, spans):
    return [jax.ShapeDtypeStruct((count, size) + x.shape[2:], x.dtype) for _, count, _, size in spans]


def slice_kernel(x_ref, *refs, spans):
    outs, sem = refs[:-1], refs[-1]
    copies = [
        pltpu.make_async_copy(span_of(x_ref, span), out, sem.at[k])
        for k, (out, span) in enumerate(zip(outs, spans))
    ]
    for copy in copies:
        copy.start()
    for copy in copies:
        copy.wait()


def edge_kernel(piece_ref, tail_ref, out_ref, *tail_out_refs):
    size = piece_ref.shape[1]
    out_ref[0] = piece_ref[0, jnp.where(flipped(), size - 1, 0)]
    place, size = 0, tail_ref.shape[1]
    for ref in tail_out_refs:
        ref[...] = span_of(tail_ref, (0, 1, place, ref.shape[1]))[...]
        place += ref.shape[1]


def prepare_kernel(x_ref, ws_ref, bs_ref, wt_ref, bt_ref, conv_ref, mix_ref, cb_ref, mb_ref, *piece_refs, spans):
    keep_rows(x_ref, piece_refs, spans)
    taps, channels = ws_ref.shape[0], ws_ref.shape[2]
    for j in range(taps):
        blocks = [ws_ref[jnp.where(flipped(), taps - 1 - i, i), j] for i in range(taps)]
        conv_ref[j * channels : (j + 1) * channels, :] = jnp.concatenate(blocks, axis=0).T
    mix_ref[...] = wt_ref[...].reshape(taps * channels, channels).T
    width = cb_ref.shape[1]
    cb_ref[...] = jnp.broadcast_to(bs_ref[...], (width, channels)).T
    mb_ref[...] = jnp.broadcast_to(bt_ref[...], (width, channels)).T


def conv_rows(columns, conv, bias, channels, width):
    stacked = jnp.concatenate(columns, axis=1)
    products = jnp.dot(conv, stacked, preferred_element_type=F32)
    lane = lax.broadcasted_iota(jnp.int32, (1, width), 1)
    rows = []
    for q in range(len(columns)):
        part = products[:, q * width : (q + 1) * width]
        left = jnp.where(lane == 0, 0.0, pltpu.roll(part[:channels], 1, 1))
        right = jnp.where(lane == width - 1, 0.0, pltpu.roll(part[2 * channels :], width - 1, 1))
        rows.append(silu(left + part[channels : 2 * channels] + right + bias).astype(BF16))
    return jnp.concatenate(rows, axis=1)


def own_kernel(x_ref, beside_ref, conv_ref, mix_ref, cb_ref, mb_ref, out_ref, *refs, group, spans):
    piece_refs, xs = refs[:-1], refs[-1]
    frames, rows, channels, width = x_ref.shape
    keep_rows(x_ref, piece_refs, spans)
    for f in range(frames):
        xs[f, 0] = beside_ref[f, 0]
        xs[f, rows + 1] = jnp.zeros((channels, width), BF16)

    def fill(s, carry):
        for f in range(frames):
            xs[f, s + 1] = x_ref[f, first_row(s, 1, rows)]
        return carry

    lax.fori_loop(0, rows, fill, 0)

    def body(p, carry):
        h = p * group
        parts = []
        for f in range(frames):
            columns = [xs[f, pl.ds(h + q, 3)].reshape(3 * channels, width) for q in range(group)]
            parts.append(conv_rows(columns, conv_ref[...], cb_ref[...], channels, width))
        mixed = jnp.dot(mix_ref[:, channels:], jnp.concatenate(parts, axis=0), preferred_element_type=F32)
        for q in range(group):
            out_ref[h + q] = mixed[:, q * width : (q + 1) * width] + mb_ref[...]
        return carry

    lax.fori_loop(0, rows // group, body, 0)


def incoming_kernel(own_ref, conv_ref, mix_ref, cb_ref, *refs, pieces, low, count, group, ready, stage):
    rows, channels, width = own_ref.shape
    flip = flipped()
    first = lax.axis_index("frames") == 0
    kept_ref, piece_refs, refs = refs[0], refs[1 : 1 + pieces], refs[1 + pieces :]
    ready_ref = out_ref = sem = None
    if ready:
        ready_ref, refs = refs[0], refs[1 + (low > ready) :]
        out_ref, refs, sem = refs[0], refs[1:-1], refs[-1]
    if stage == LAST:
        xs, made_ref = refs
    else:
        made_ref, carry_ref, xs = refs[:3]

    def to_output(source, place, size, k):
        target = out_ref.at[pl.ds(first_row(place, size, rows), size)]
        return pltpu.make_async_copy(source, target, sem.at[k])

    def own_rows(target, size):
        for q in range(size):
            target[jnp.where(flip, size - 1 - q, q)] = own_ref[low + q].astype(BF16)

    def convolve():
        held = kept_ref.shape[0]
        xs[0:held] = kept_ref[...]
        for ref in piece_refs:
            size = ref.shape[1]
            for k in range(size):
                xs[held + k] = ref[0, jnp.where(flip, size - 1 - k, k)]
            held += size
        if stage == LAST:
            xs[held] = jnp.zeros((channels, width), BF16)
        else:
            carry_ref[...] = xs[pl.ds(held - 2, 2)]

        def body(p, carry):
            h = p * group
            columns = [xs[pl.ds(h + q, 3)].reshape(3 * channels, width) for q in range(group)]
            act = conv_rows(columns, conv_ref[...], cb_ref[...], channels, width)
            mixed = jnp.dot(mix_ref[:, :channels], act, preferred_element_type=F32)
            for q in range(group):
                total = own_ref[low + h + q] + mixed[:, q * width : (q + 1) * width]
                made_ref[jnp.where(flip, count - 1 - h - q, h + q)] = total.astype(BF16)
            return carry

        lax.fori_loop(0, count // group, body, 0)

    if stage == OPEN:

        @pl.when(first)
        def _():
            own_rows(made_ref, count)

        @pl.when(jnp.logical_not(first))
        def _():
            convolve()

        return

    before = to_output(ready_ref, low - ready, ready, 0)
    if stage == CLOSING:

        @pl.when(first)
        def _():
            rest = refs[3]
            own_rows(rest, rows - low)
            after = to_output(rest, low, rows - low, 1)
            before.start()
            after.start()
            before.wait()
            after.wait()

    @pl.when(jnp.logical_not(first))
    def _():
        before.start()
        convolve()
        if stage == LAST:
            after = to_output(made_ref, low, count, 1)
            after.start()
            after.wait()
        before.wait()


def incoming_rows(out, made, own, weights, kept, pieces, low, stage):
    conv, mix, cb = weights
    rows, channels, width = own.shape
    held = kept.shape[0] + sum(piece.shape[1] for piece in pieces) + (stage == LAST)
    count = held - 2
    ready = 0 if made is None else made.shape[0]
    group = next(g for g in (5, 4, 3, 2, 1) if count % g == 0)

    def row_array(size):
        return jax.ShapeDtypeStruct((size, channels, width), BF16)

    operands = [own, conv, mix, cb, kept, *pieces]
    in_specs = [VMEM] * len(operands)
    out_shape, out_specs, aliases = [], [], {}
    if ready:
        operands.append(made)
        in_specs.append(VMEM)
        if out is not None:
            aliases = {len(operands): 0}
            operands.append(out)
            in_specs.append(ANY)
        out_shape.append(row_array(rows))
        out_specs.append(ANY)
    if stage != LAST:
        out_shape += [row_array(count), row_array(2)]
        out_specs += [VMEM] * 2
    scratch = [pltpu.VMEM((held, channels, width), BF16)]
    if stage == LAST:
        scratch.append(pltpu.VMEM((count, channels, width), BF16))
    if stage == CLOSING:
        scratch.append(pltpu.VMEM((rows - low, channels, width), BF16))
    if ready:
        scratch.append(pltpu.SemaphoreType.DMA((2,)))
    results = pl.pallas_call(
        functools.partial(
            incoming_kernel, pieces=len(pieces), low=low, count=count, group=group, ready=ready, stage=stage
        ),
        out_shape=out_shape,
        in_specs=in_specs,
        out_specs=out_specs,
        input_output_aliases=aliases,
        scratch_shapes=scratch,
        compiler_params=PARAMS,
        cost_estimate=cost(0, 0),
    )(*operands)
    if stage == LAST:
        return results[0], None, None
    return (results[0] if ready else None), results[-2], results[-1]


def per_device(video, w_spatial, b_spatial, w_temporal, b_temporal):
    frames, rows, width, channels = video.shape
    x = jnp.transpose(video, (0, 1, 3, 2))
    sizes, early, steps = [5, 4, 4, 2, 1], 2, [(0, 2), (2, 3), (3, 4), (4, 5)]
    places = [sum(sizes[:k]) for k in range(len(sizes))]
    spans = [(frames - 1, 1, place, size) for place, size in zip(places, sizes)]

    head_spans = [spans[0], (0, frames, 0, 1)]
    head, boundary = pl.pallas_call(
        functools.partial(slice_kernel, spans=head_spans),
        out_shape=row_shapes(x, head_spans),
        in_specs=[ANY],
        out_specs=[VMEM] * 2,
        scratch_shapes=[pltpu.SemaphoreType.DMA((2,))],
        compiler_params=pltpu.CompilerParams(vmem_limit_bytes=HEAD_LIMIT),
    )(x)
    whole = [(0, frames, 0, rows)]
    (x,) = pl.pallas_call(
        functools.partial(slice_kernel, spans=whole),
        out_shape=row_shapes(x, whole),
        in_specs=[ANY],
        out_specs=[VMEM],
        scratch_shapes=[pltpu.SemaphoreType.DMA((1,))],
        compiler_params=pltpu.CompilerParams(vmem_limit_bytes=LOAD_LIMIT),
        cost_estimate=cost(0, 0),
    )(x)
    ending = [(frames - 1, 1, places[-2], sizes[-2] + sizes[-1])]
    (tail,) = pl.pallas_call(
        functools.partial(keep_kernel, spans=ending),
        out_shape=row_shapes(x, ending),
        in_specs=[VMEM],
        out_specs=[VMEM],
        compiler_params=PARAMS,
        cost_estimate=cost(0, 0),
    )(x)
    arrived = [lax.ppermute(head, "frames", ring("frames"))]
    tail = next_odd(tail, "frames")
    beside = lax.ppermute(boundary, "rows", ring("rows"))

    square = jax.ShapeDtypeStruct((3 * channels, 3 * channels), BF16)
    flat = jax.ShapeDtypeStruct((channels, 3 * channels), BF16)
    bias = jax.ShapeDtypeStruct((channels, width), F32)
    late = spans[1 + early : -2]
    conv, mix, cb, mb, *pieces = pl.pallas_call(
        functools.partial(prepare_kernel, spans=spans[1 : 1 + early]),
        out_shape=[square, flat, bias, bias] + row_shapes(x, spans[1 : 1 + early]),
        in_specs=[VMEM] * 5,
        out_specs=[VMEM] * (4 + early),
        compiler_params=PARAMS,
        cost_estimate=cost(0, 2 * 12 * channels * channels * 2),
    )(x, w_spatial, b_spatial.reshape(1, channels), w_temporal, b_temporal.reshape(1, channels))
    arrived += [lax.ppermute(piece, "frames", ring("frames")) for piece in pieces]

    (own,) = pl.pallas_call(
        functools.partial(own_kernel, group=4, spans=late),
        out_shape=[jax.ShapeDtypeStruct((rows, channels, width), F32)] + row_shapes(x, late),
        in_specs=[VMEM] * 6,
        out_specs=[VMEM] * (1 + len(late)),
        scratch_shapes=[pltpu.VMEM((frames, rows + 2, channels, width), BF16)],
        compiler_params=PARAMS,
        cost_estimate=cost(2 * rows * width * channels * channels * 20, 8 * rows * channels * width),
    )(x, beside, conv, mix, cb, mb)
    own, arrived[0] = lax.optimization_barrier((own, arrived[0]))
    edge, *pieces = pl.pallas_call(
        edge_kernel,
        out_shape=[jax.ShapeDtypeStruct((1, channels, width), BF16)] + row_shapes(x, spans[-2:]),
        in_specs=[VMEM] * 2,
        out_specs=[VMEM] * 3,
        compiler_params=PARAMS,
        cost_estimate=cost(0, 0),
    )(arrived[0], tail)
    arrived += [within_pairs(piece, "frames", piece is pieces[0]) for piece in pieces]
    kept = lax.ppermute(edge, "rows", ring("rows"))

    weights = (conv, mix, cb)
    out, made, low = None, None, 0
    for k, (begin, end) in enumerate(steps):
        stage = LAST if end == len(arrived) else min(k, LATE)
        out, made, kept = incoming_rows(out, made, own, weights, kept, arrived[begin:end], low, stage)
        low = places[end - 1] + sizes[end - 1] - 1
    return jnp.transpose(out[None], (0, 1, 3, 2))


def solution(mesh):
    in_specs = (P(("batch", "frames"), "rows", None, None), P(), P(), P(), P())
    out_specs = P(("batch", "frames"), "rows", None, None)
    return jax.shard_map(
        per_device, mesh=mesh, in_specs=in_specs, out_specs=out_specs, check_vma=False
    )
```

```python
import functools

import jax
import jax.numpy as jnp
from jax import lax
from jax.experimental import pallas as pl
from jax.experimental.pallas import tpu as pltpu
from jax.sharding import PartitionSpec as P

F32 = jnp.float32
BF16 = jnp.bfloat16
VMEM = pl.BlockSpec(memory_space=pltpu.VMEM)
ANY = pl.BlockSpec(memory_space=pl.ANY)
HEAD_LIMIT = 53 * 2**20
LOAD_LIMIT = 50 * 2**20
OPEN, CLOSING, LATE, LAST = range(4)
PARAMS = pltpu.CompilerParams(vmem_limit_bytes=20 * 2**20)


def flipped():
    return lax.axis_index("rows") == 0


def first_row(place, size, rows):
    return jnp.where(flipped(), rows - place - size, place)


def ring(axis):
    count = lax.axis_size(axis)
    return [(i, (i + 1) % count) for i in range(count)]


def next_odd(piece, axis):
    count = lax.axis_size(axis)
    return lax.ppermute(piece, axis, [(i, (i + 2) % count) for i in range(1, count, 2)])


def within_pairs(piece, axis, keep):
    count = lax.axis_size(axis)
    route = ring(axis) if count % 2 else [(i, i ^ 1) for i in range(count)]
    return lax.ppermute(piece, axis, [(a, b) for a, b in route if b or keep])


def cost(flops, moved):
    return pl.CostEstimate(flops=flops, bytes_accessed=moved, transcendentals=0)


def silu(v):
    half = 0.5 * v
    return half + half * jnp.tanh(half)


def span_of(x_ref, span):
    frame, count, place, size = span
    return x_ref.at[pl.ds(frame, count), pl.ds(first_row(place, size, x_ref.shape[1]), size)]


def keep_rows(x_ref, outs, spans):
    for out, span in zip(outs, spans):
        out[...] = span_of(x_ref, span)[...]


def keep_kernel(x_ref, *outs, spans):
    keep_rows(x_ref, outs, spans)


def row_shapes(x, spans):
    return [jax.ShapeDtypeStruct((count, size) + x.shape[2:], x.dtype) for _, count, _, size in spans]


def slice_kernel(x_ref, *refs, spans):
    outs, sem = refs[:-1], refs[-1]
    copies = [
        pltpu.make_async_copy(span_of(x_ref, span), out, sem.at[k])
        for k, (out, span) in enumerate(zip(outs, spans))
    ]
    for copy in copies:
        copy.start()
    for copy in copies:
        copy.wait()


def edge_kernel(piece_ref, tail_ref, relayed_ref, out_ref, *tail_out_refs):
    size = piece_ref.shape[1]
    out_ref[0] = piece_ref[0, jnp.where(flipped(), size - 1, 0)]
    count = lax.axis_size("frames")
    relay = jnp.logical_and(count % 2 == 0, lax.rem(lax.axis_index("frames"), 2) == 1)

    def cut(source_ref):
        place = 0
        for ref in tail_out_refs:
            ref[...] = span_of(source_ref, (0, 1, place, ref.shape[1]))[...]
            place += ref.shape[1]

    pl.when(relay)(lambda: cut(relayed_ref))
    pl.when(jnp.logical_not(relay))(lambda: cut(tail_ref))


def prepare_kernel(x_ref, ws_ref, bs_ref, wt_ref, bt_ref, conv_ref, mix_ref, cb_ref, mb_ref, *piece_refs, spans):
    keep_rows(x_ref, piece_refs, spans)
    taps, channels = ws_ref.shape[0], ws_ref.shape[2]
    for j in range(taps):
        blocks = [ws_ref[jnp.where(flipped(), taps - 1 - i, i), j] for i in range(taps)]
        conv_ref[j * channels : (j + 1) * channels, :] = jnp.concatenate(blocks, axis=0).T
    mix_ref[...] = wt_ref[...].reshape(taps * channels, channels).T
    width = cb_ref.shape[1]
    cb_ref[...] = jnp.broadcast_to(bs_ref[...], (width, channels)).T
    mb_ref[...] = jnp.broadcast_to(bt_ref[...], (width, channels)).T


def conv_rows(columns, conv, bias, channels, width):
    stacked = jnp.concatenate(columns, axis=1)
    products = jnp.dot(conv, stacked, preferred_element_type=F32)
    lane = lax.broadcasted_iota(jnp.int32, (1, width), 1)
    rows = []
    for q in range(len(columns)):
        part = products[:, q * width : (q + 1) * width]
        left = jnp.where(lane == 0, 0.0, pltpu.roll(part[:channels], 1, 1))
        right = jnp.where(lane == width - 1, 0.0, pltpu.roll(part[2 * channels :], width - 1, 1))
        rows.append(silu(left + part[channels : 2 * channels] + right + bias).astype(BF16))
    return jnp.concatenate(rows, axis=1)


def own_kernel(x_ref, beside_ref, conv_ref, mix_ref, cb_ref, mb_ref, out_ref, xs, *, group):
    frames, rows, channels, width = x_ref.shape
    for f in range(frames):
        xs[f, 0] = beside_ref[f, 0]
        xs[f, rows + 1] = jnp.zeros((channels, width), BF16)

    def fill(s, carry):
        for f in range(frames):
            xs[f, s + 1] = x_ref[f, first_row(s, 1, rows)]
        return carry

    lax.fori_loop(0, rows, fill, 0)

    def body(p, carry):
        h = p * group
        parts = []
        for f in range(frames):
            columns = [xs[f, pl.ds(h + q, 3)].reshape(3 * channels, width) for q in range(group)]
            parts.append(conv_rows(columns, conv_ref[...], cb_ref[...], channels, width))
        mixed = jnp.dot(mix_ref[:, channels:], jnp.concatenate(parts, axis=0), preferred_element_type=F32)
        for q in range(group):
            out_ref[h + q] = mixed[:, q * width : (q + 1) * width] + mb_ref[...]
        return carry

    lax.fori_loop(0, rows // group, body, 0)


def incoming_kernel(own_ref, conv_ref, mix_ref, cb_ref, *refs, pieces, low, count, group, ready, stage):
    rows, channels, width = own_ref.shape
    flip = flipped()
    first = lax.axis_index("frames") == 0
    kept_ref, piece_refs, refs = refs[0], refs[1 : 1 + pieces], refs[1 + pieces :]
    ready_ref = out_ref = sem = None
    if ready:
        ready_ref, refs = refs[0], refs[1 + (low > ready) :]
        out_ref, refs, sem = refs[0], refs[1:-1], refs[-1]
    if stage == LAST:
        xs, made_ref = refs
    else:
        made_ref, carry_ref, xs = refs[:3]

    def to_output(source, place, size, k):
        target = out_ref.at[pl.ds(first_row(place, size, rows), size)]
        return pltpu.make_async_copy(source, target, sem.at[k])

    def own_rows(target, size):
        for q in range(size):
            target[jnp.where(flip, size - 1 - q, q)] = own_ref[low + q].astype(BF16)

    def convolve():
        held = kept_ref.shape[0]
        xs[0:held] = kept_ref[...]
        for ref in piece_refs:
            size = ref.shape[1]
            for k in range(size):
                xs[held + k] = ref[0, jnp.where(flip, size - 1 - k, k)]
            held += size
        if stage == LAST:
            xs[held] = jnp.zeros((channels, width), BF16)
        else:
            carry_ref[...] = xs[pl.ds(held - 2, 2)]

        def body(p, carry):
            h = p * group
            columns = [xs[pl.ds(h + q, 3)].reshape(3 * channels, width) for q in range(group)]
            act = conv_rows(columns, conv_ref[...], cb_ref[...], channels, width)
            mixed = jnp.dot(mix_ref[:, :channels], act, preferred_element_type=F32)
            for q in range(group):
                total = own_ref[low + h + q] + mixed[:, q * width : (q + 1) * width]
                made_ref[jnp.where(flip, count - 1 - h - q, h + q)] = total.astype(BF16)
            return carry

        lax.fori_loop(0, count // group, body, 0)

    if stage == OPEN:

        @pl.when(first)
        def _():
            own_rows(made_ref, count)

        @pl.when(jnp.logical_not(first))
        def _():
            convolve()

        return

    before = to_output(ready_ref, low - ready, ready, 0)
    if stage == CLOSING:

        @pl.when(first)
        def _():
            rest = refs[3]
            own_rows(rest, rows - low)
            after = to_output(rest, low, rows - low, 1)
            before.start()
            after.start()
            before.wait()
            after.wait()

    @pl.when(jnp.logical_not(first))
    def _():
        before.start()
        convolve()
        if stage == LAST:
            after = to_output(made_ref, low, count, 1)
            after.start()
            after.wait()
        before.wait()


def incoming_rows(out, made, own, weights, kept, pieces, low, stage):
    conv, mix, cb = weights
    rows, channels, width = own.shape
    held = kept.shape[0] + sum(piece.shape[1] for piece in pieces) + (stage == LAST)
    count = held - 2
    ready = 0 if made is None else made.shape[0]
    group = next(g for g in (5, 4, 3, 2, 1) if count % g == 0)

    def row_array(size):
        return jax.ShapeDtypeStruct((size, channels, width), BF16)

    operands = [own, conv, mix, cb, kept, *pieces]
    in_specs = [VMEM] * len(operands)
    out_shape, out_specs, aliases = [], [], {}
    if ready:
        operands.append(made)
        in_specs.append(VMEM)
        if out is not None:
            aliases = {len(operands): 0}
            operands.append(out)
            in_specs.append(ANY)
        out_shape.append(row_array(rows))
        out_specs.append(ANY)
    if stage != LAST:
        out_shape += [row_array(count), row_array(2)]
        out_specs += [VMEM] * 2
    scratch = [pltpu.VMEM((held, channels, width), BF16)]
    if stage == LAST:
        scratch.append(pltpu.VMEM((count, channels, width), BF16))
    if stage == CLOSING:
        scratch.append(pltpu.VMEM((rows - low, channels, width), BF16))
    if ready:
        scratch.append(pltpu.SemaphoreType.DMA((2,)))
    results = pl.pallas_call(
        functools.partial(
            incoming_kernel, pieces=len(pieces), low=low, count=count, group=group, ready=ready, stage=stage
        ),
        out_shape=out_shape,
        in_specs=in_specs,
        out_specs=out_specs,
        input_output_aliases=aliases,
        scratch_shapes=scratch,
        compiler_params=PARAMS,
        cost_estimate=cost(0, 0),
    )(*operands)
    if stage == LAST:
        return results[0], None, None
    return (results[0] if ready else None), results[-2], results[-1]


def per_device(video, w_spatial, b_spatial, w_temporal, b_temporal):
    frames, rows, width, channels = video.shape
    x = jnp.transpose(video, (0, 1, 3, 2))
    sizes, steps = [rows - 11, 4, 4, 2, 1], [(0, 2), (2, 3), (3, 4), (4, 5)]
    places = [sum(sizes[:k]) for k in range(len(sizes))]
    spans = [(frames - 1, 1, place, size) for place, size in zip(places, sizes)]

    head_spans = [spans[0], (0, frames, 0, 1)]
    head, boundary = pl.pallas_call(
        functools.partial(slice_kernel, spans=head_spans),
        out_shape=row_shapes(x, head_spans),
        in_specs=[ANY],
        out_specs=[VMEM] * 2,
        scratch_shapes=[pltpu.SemaphoreType.DMA((2,))],
        compiler_params=pltpu.CompilerParams(vmem_limit_bytes=HEAD_LIMIT),
    )(x)
    whole = [(0, frames, 0, rows)]
    (x,) = pl.pallas_call(
        functools.partial(slice_kernel, spans=whole),
        out_shape=row_shapes(x, whole),
        in_specs=[ANY],
        out_specs=[VMEM],
        scratch_shapes=[pltpu.SemaphoreType.DMA((1,))],
        compiler_params=pltpu.CompilerParams(vmem_limit_bytes=LOAD_LIMIT),
        cost_estimate=cost(0, 0),
    )(x)
    ending = [(frames - 1, 1, places[-2], sizes[-2] + sizes[-1])]
    (tail,) = pl.pallas_call(
        functools.partial(keep_kernel, spans=ending),
        out_shape=row_shapes(x, ending),
        in_specs=[VMEM],
        out_specs=[VMEM],
        compiler_params=PARAMS,
        cost_estimate=cost(0, 0),
    )(x)
    arrived = [lax.ppermute(head, "frames", ring("frames"))]
    relayed = next_odd(tail, "frames")
    beside = lax.ppermute(boundary, "rows", ring("rows"))

    square = jax.ShapeDtypeStruct((3 * channels, 3 * channels), BF16)
    flat = jax.ShapeDtypeStruct((channels, 3 * channels), BF16)
    bias = jax.ShapeDtypeStruct((channels, width), F32)
    conv, mix, cb, mb, *pieces = pl.pallas_call(
        functools.partial(prepare_kernel, spans=spans[1:3]),
        out_shape=[square, flat, bias, bias] + row_shapes(x, spans[1:3]),
        in_specs=[VMEM] * 5,
        out_specs=[VMEM] * 6,
        compiler_params=PARAMS,
        cost_estimate=cost(0, 2 * 12 * channels * channels * 2),
    )(x, w_spatial, b_spatial.reshape(1, channels), w_temporal, b_temporal.reshape(1, channels))
    arrived += [lax.ppermute(piece, "frames", ring("frames")) for piece in pieces]

    own = pl.pallas_call(
        functools.partial(own_kernel, group=next(g for g in (4, 3, 2, 1) if rows % g == 0)),
        out_shape=jax.ShapeDtypeStruct((rows, channels, width), F32),
        in_specs=[VMEM] * 6,
        out_specs=VMEM,
        scratch_shapes=[pltpu.VMEM((frames, rows + 2, channels, width), BF16)],
        compiler_params=PARAMS,
        cost_estimate=cost(2 * rows * width * channels * channels * 20, 8 * rows * channels * width),
    )(x, beside, conv, mix, cb, mb)
    own, arrived[0] = lax.optimization_barrier((own, arrived[0]))
    edge, *pieces = pl.pallas_call(
        edge_kernel,
        out_shape=[jax.ShapeDtypeStruct((1, channels, width), BF16)] + row_shapes(x, spans[-2:]),
        in_specs=[VMEM] * 3,
        out_specs=[VMEM] * 3,
        compiler_params=PARAMS,
        cost_estimate=cost(0, 0),
    )(arrived[0], tail, relayed)
    arrived += [within_pairs(pieces[0], "frames", True), within_pairs(pieces[1], "frames", False)]
    kept = lax.ppermute(edge, "rows", ring("rows"))

    weights = (conv, mix, cb)
    out, made, low = None, None, 0
    for k, (begin, end) in enumerate(steps):
        stage = LAST if end == len(arrived) else min(k, LATE)
        out, made, kept = incoming_rows(out, made, own, weights, kept, arrived[begin:end], low, stage)
        low = places[end - 1] + sizes[end - 1] - 1
    return jnp.transpose(out[None], (0, 1, 3, 2))


def solution(mesh):
    in_specs = (P(("batch", "frames"), "rows", None, None), P(), P(), P(), P())
    out_specs = P(("batch", "frames"), "rows", None, None)
    return jax.shard_map(
        per_device, mesh=mesh, in_specs=in_specs, out_specs=out_specs, check_vma=False
    )
```

```python
import functools

import jax
import jax.numpy as jnp
from jax import lax
from jax.experimental import pallas as pl
from jax.experimental.pallas import tpu as pltpu
from jax.sharding import PartitionSpec as P

F32 = jnp.float32
BF16 = jnp.bfloat16
VMEM = pl.BlockSpec(memory_space=pltpu.VMEM)
ANY = pl.BlockSpec(memory_space=pl.ANY)
HEAD_LIMIT = 53 * 2**20
LOAD_LIMIT = 50 * 2**20
OPEN, CLOSING, LATE, LAST = range(4)
PARAMS = pltpu.CompilerParams(vmem_limit_bytes=20 * 2**20)


def flipped():
    return lax.axis_index("rows") == 0


def first_row(place, size, rows):
    return jnp.where(flipped(), rows - place - size, place)


def ring(axis):
    count = lax.axis_size(axis)
    return [(i, (i + 1) % count) for i in range(count)]


def next_odd(piece, axis):
    count = lax.axis_size(axis)
    return lax.ppermute(piece, axis, [(i, (i + 2) % count) for i in range(1, count, 2)])


def within_pairs(piece, axis, keep):
    count = lax.axis_size(axis)
    route = ring(axis) if count % 2 else [(i, i ^ 1) for i in range(count)]
    return lax.ppermute(piece, axis, [(a, b) for a, b in route if b or keep])


def cost(flops, moved):
    return pl.CostEstimate(flops=flops, bytes_accessed=moved, transcendentals=0)


def silu(v):
    half = 0.5 * v
    return half + half * jnp.tanh(half)


def span_of(x_ref, span):
    frame, count, place, size = span
    return x_ref.at[pl.ds(frame, count), pl.ds(first_row(place, size, x_ref.shape[1]), size)]


def keep_rows(x_ref, outs, spans):
    for out, span in zip(outs, spans):
        out[...] = span_of(x_ref, span)[...]


def keep_kernel(x_ref, *outs, spans):
    keep_rows(x_ref, outs, spans)


def row_shapes(x, spans):
    return [jax.ShapeDtypeStruct((count, size) + x.shape[2:], x.dtype) for _, count, _, size in spans]


def slice_kernel(x_ref, *refs, spans):
    outs, sem = refs[:-1], refs[-1]
    copies = [
        pltpu.make_async_copy(span_of(x_ref, span), out, sem.at[k])
        for k, (out, span) in enumerate(zip(outs, spans))
    ]
    for copy in copies:
        copy.start()
    for copy in copies:
        copy.wait()


def edge_kernel(piece_ref, tail_ref, relayed_ref, out_ref, *tail_out_refs):
    size = piece_ref.shape[1]
    out_ref[0] = piece_ref[0, jnp.where(flipped(), size - 1, 0)]
    count = lax.axis_size("frames")
    relay = jnp.logical_and(count % 2 == 0, lax.rem(lax.axis_index("frames"), 2) == 1)

    def cut(source_ref):
        place = 0
        for ref in tail_out_refs:
            ref[...] = span_of(source_ref, (0, 1, place, ref.shape[1]))[...]
            place += ref.shape[1]

    pl.when(relay)(lambda: cut(relayed_ref))
    pl.when(jnp.logical_not(relay))(lambda: cut(tail_ref))


def prepare_kernel(x_ref, ws_ref, bs_ref, wt_ref, bt_ref, conv_ref, mix_ref, cb_ref, mb_ref, *piece_refs, spans):
    keep_rows(x_ref, piece_refs, spans)
    taps, channels = ws_ref.shape[0], ws_ref.shape[2]
    for j in range(taps):
        blocks = [ws_ref[jnp.where(flipped(), taps - 1 - i, i), j] for i in range(taps)]
        conv_ref[j * channels : (j + 1) * channels, :] = jnp.concatenate(blocks, axis=0).T
    mix_ref[...] = wt_ref[...].reshape(taps * channels, channels).T
    width = cb_ref.shape[1]
    cb_ref[...] = jnp.broadcast_to(bs_ref[...], (width, channels)).T
    mb_ref[...] = jnp.broadcast_to(bt_ref[...], (width, channels)).T


def conv_rows(columns, conv, bias, channels, width):
    stacked = jnp.concatenate(columns, axis=1)
    products = jnp.dot(conv, stacked, preferred_element_type=F32)
    lane = lax.broadcasted_iota(jnp.int32, (1, width), 1)
    rows = []
    for q in range(len(columns)):
        part = products[:, q * width : (q + 1) * width]
        left = jnp.where(lane == 0, 0.0, pltpu.roll(part[:channels], 1, 1))
        right = jnp.where(lane == width - 1, 0.0, pltpu.roll(part[2 * channels :], width - 1, 1))
        rows.append(silu(left + part[channels : 2 * channels] + right + bias).astype(BF16))
    return jnp.concatenate(rows, axis=1)


def own_kernel(x_ref, beside_ref, conv_ref, mix_ref, cb_ref, mb_ref, out_ref, xs, *, group):
    frames, rows, channels, width = x_ref.shape
    for f in range(frames):
        xs[f, 0] = beside_ref[f, 0]
        xs[f, rows + 1] = jnp.zeros((channels, width), BF16)

    def fill(s, carry):
        for f in range(frames):
            xs[f, s + 1] = x_ref[f, first_row(s, 1, rows)]
        return carry

    lax.fori_loop(0, rows, fill, 0)

    def body(p, carry):
        h = p * group
        parts = []
        for f in range(frames):
            columns = [xs[f, pl.ds(h + q, 3)].reshape(3 * channels, width) for q in range(group)]
            parts.append(conv_rows(columns, conv_ref[...], cb_ref[...], channels, width))
        mixed = jnp.dot(mix_ref[:, channels:], jnp.concatenate(parts, axis=0), preferred_element_type=F32)
        for q in range(group):
            out_ref[h + q] = mixed[:, q * width : (q + 1) * width] + mb_ref[...]
        return carry

    lax.fori_loop(0, rows // group, body, 0)


def incoming_kernel(own_ref, conv_ref, mix_ref, cb_ref, *refs, pieces, low, count, group, ready, stage):
    rows, channels, width = own_ref.shape
    flip = flipped()
    first = lax.axis_index("frames") == 0
    kept_ref, piece_refs, refs = refs[0], refs[1 : 1 + pieces], refs[1 + pieces :]
    ready_ref = out_ref = sem = None
    if ready:
        ready_ref, refs = refs[0], refs[1 + (low > ready) :]
        out_ref, refs, sem = refs[0], refs[1:-1], refs[-1]
    if stage == LAST:
        xs, made_ref = refs
    else:
        made_ref, carry_ref, xs = refs[:3]

    def to_output(source, place, size, k):
        target = out_ref.at[pl.ds(first_row(place, size, rows), size)]
        return pltpu.make_async_copy(source, target, sem.at[k])

    def own_rows(target, size):
        for q in range(size):
            target[jnp.where(flip, size - 1 - q, q)] = own_ref[low + q].astype(BF16)

    def convolve():
        held = kept_ref.shape[0]
        xs[0:held] = kept_ref[...]
        for ref in piece_refs:
            size = ref.shape[1]
            for k in range(size):
                xs[held + k] = ref[0, jnp.where(flip, size - 1 - k, k)]
            held += size
        if stage == LAST:
            xs[held] = jnp.zeros((channels, width), BF16)
        else:
            carry_ref[...] = xs[pl.ds(held - 2, 2)]

        def body(p, carry):
            h = p * group
            columns = [xs[pl.ds(h + q, 3)].reshape(3 * channels, width) for q in range(group)]
            act = conv_rows(columns, conv_ref[...], cb_ref[...], channels, width)
            mixed = jnp.dot(mix_ref[:, :channels], act, preferred_element_type=F32)
            for q in range(group):
                total = own_ref[low + h + q] + mixed[:, q * width : (q + 1) * width]
                made_ref[jnp.where(flip, count - 1 - h - q, h + q)] = total.astype(BF16)
            return carry

        lax.fori_loop(0, count // group, body, 0)

    if stage == OPEN:

        @pl.when(first)
        def _():
            own_rows(made_ref, count)

        @pl.when(jnp.logical_not(first))
        def _():
            convolve()

        return

    before = to_output(ready_ref, low - ready, ready, 0)
    if stage == CLOSING:

        @pl.when(first)
        def _():
            rest = refs[3]
            own_rows(rest, rows - low)
            after = to_output(rest, low, rows - low, 1)
            before.start()
            after.start()
            before.wait()
            after.wait()

    @pl.when(jnp.logical_not(first))
    def _():
        before.start()
        convolve()
        if stage == LAST:
            after = to_output(made_ref, low, count, 1)
            after.start()
            after.wait()
        before.wait()


def incoming_rows(out, made, own, weights, kept, pieces, low, stage):
    conv, mix, cb = weights
    rows, channels, width = own.shape
    held = kept.shape[0] + sum(piece.shape[1] for piece in pieces) + (stage == LAST)
    count = held - 2
    ready = 0 if made is None else made.shape[0]
    group = next(g for g in (5, 4, 3, 2, 1) if count % g == 0)

    def row_array(size):
        return jax.ShapeDtypeStruct((size, channels, width), BF16)

    operands = [own, conv, mix, cb, kept, *pieces]
    in_specs = [VMEM] * len(operands)
    out_shape, out_specs, aliases = [], [], {}
    if ready:
        operands.append(made)
        in_specs.append(VMEM)
        if out is not None:
            aliases = {len(operands): 0}
            operands.append(out)
            in_specs.append(ANY)
        out_shape.append(row_array(rows))
        out_specs.append(ANY)
    if stage != LAST:
        out_shape += [row_array(count), row_array(2)]
        out_specs += [VMEM] * 2
    scratch = [pltpu.VMEM((held, channels, width), BF16)]
    if stage == LAST:
        scratch.append(pltpu.VMEM((count, channels, width), BF16))
    if stage == CLOSING:
        scratch.append(pltpu.VMEM((rows - low, channels, width), BF16))
    if ready:
        scratch.append(pltpu.SemaphoreType.DMA((2,)))
    results = pl.pallas_call(
        functools.partial(
            incoming_kernel, pieces=len(pieces), low=low, count=count, group=group, ready=ready, stage=stage
        ),
        out_shape=out_shape,
        in_specs=in_specs,
        out_specs=out_specs,
        input_output_aliases=aliases,
        scratch_shapes=scratch,
        compiler_params=PARAMS,
        cost_estimate=cost(0, 0),
    )(*operands)
    if stage == LAST:
        return results[0], None, None
    return (results[0] if ready else None), results[-2], results[-1]


def per_device(video, w_spatial, b_spatial, w_temporal, b_temporal):
    frames, rows, width, channels = video.shape
    x = jnp.transpose(video, (0, 1, 3, 2))
    sizes, steps = [rows - 11, 4, 4, 2, 1], [(0, 2), (2, 3), (3, 4), (4, 5)]
    places = [sum(sizes[:k]) for k in range(len(sizes))]
    spans = [(frames - 1, 1, place, size) for place, size in zip(places, sizes)]

    head_spans = [spans[0], (0, frames, 0, 1)]
    head, boundary = pl.pallas_call(
        functools.partial(slice_kernel, spans=head_spans),
        out_shape=row_shapes(x, head_spans),
        in_specs=[ANY],
        out_specs=[VMEM] * 2,
        scratch_shapes=[pltpu.SemaphoreType.DMA((2,))],
        compiler_params=pltpu.CompilerParams(vmem_limit_bytes=HEAD_LIMIT),
    )(x)
    whole = [(0, frames, 0, rows)]
    (x,) = pl.pallas_call(
        functools.partial(slice_kernel, spans=whole),
        out_shape=row_shapes(x, whole),
        in_specs=[ANY],
        out_specs=[VMEM],
        scratch_shapes=[pltpu.SemaphoreType.DMA((1,))],
        compiler_params=pltpu.CompilerParams(vmem_limit_bytes=LOAD_LIMIT),
        cost_estimate=cost(0, 0),
    )(x)
    ending = [(frames - 1, 1, places[-2], sizes[-2] + sizes[-1])]
    (tail,) = pl.pallas_call(
        functools.partial(keep_kernel, spans=ending),
        out_shape=row_shapes(x, ending),
        in_specs=[VMEM],
        out_specs=[VMEM],
        compiler_params=PARAMS,
        cost_estimate=cost(0, 0),
    )(x)
    arrived = [lax.ppermute(head, "frames", ring("frames"))]
    relayed = next_odd(tail, "frames")
    beside = lax.ppermute(boundary, "rows", ring("rows"))

    square = jax.ShapeDtypeStruct((3 * channels, 3 * channels), BF16)
    flat = jax.ShapeDtypeStruct((channels, 3 * channels), BF16)
    bias = jax.ShapeDtypeStruct((channels, width), F32)
    conv, mix, cb, mb, *pieces = pl.pallas_call(
        functools.partial(prepare_kernel, spans=spans[1:3]),
        out_shape=[square, flat, bias, bias] + row_shapes(x, spans[1:3]),
        in_specs=[VMEM] * 5,
        out_specs=[VMEM] * 6,
        compiler_params=PARAMS,
        cost_estimate=cost(0, 2 * 12 * channels * channels * 2),
    )(x, w_spatial, b_spatial.reshape(1, channels), w_temporal, b_temporal.reshape(1, channels))
    arrived += [lax.ppermute(piece, "frames", ring("frames")) for piece in pieces]

    own = pl.pallas_call(
        functools.partial(own_kernel, group=next(g for g in (8, 4, 3, 2, 1) if rows % g == 0)),
        out_shape=jax.ShapeDtypeStruct((rows, channels, width), F32),
        in_specs=[VMEM] * 6,
        out_specs=VMEM,
        scratch_shapes=[pltpu.VMEM((frames, rows + 2, channels, width), BF16)],
        compiler_params=PARAMS,
        cost_estimate=cost(2 * rows * width * channels * channels * 20, 8 * rows * channels * width),
    )(x, beside, conv, mix, cb, mb)
    own, arrived[0] = lax.optimization_barrier((own, arrived[0]))
    edge, *pieces = pl.pallas_call(
        edge_kernel,
        out_shape=[jax.ShapeDtypeStruct((1, channels, width), BF16)] + row_shapes(x, spans[-2:]),
        in_specs=[VMEM] * 3,
        out_specs=[VMEM] * 3,
        compiler_params=PARAMS,
        cost_estimate=cost(0, 0),
    )(arrived[0], tail, relayed)
    arrived += [within_pairs(pieces[0], "frames", True), within_pairs(pieces[1], "frames", False)]
    kept = lax.ppermute(edge, "rows", ring("rows"))

    weights = (conv, mix, cb)
    out, made, low = None, None, 0
    for k, (begin, end) in enumerate(steps):
        stage = LAST if end == len(arrived) else min(k, LATE)
        out, made, kept = incoming_rows(out, made, own, weights, kept, arrived[begin:end], low, stage)
        low = places[end - 1] + sizes[end - 1] - 1
    return jnp.transpose(out[None], (0, 1, 3, 2))


def solution(mesh):
    in_specs = (P(("batch", "frames"), "rows", None, None), P(), P(), P(), P())
    out_specs = P(("batch", "frames"), "rows", None, None)
    return jax.shard_map(
        per_device, mesh=mesh, in_specs=in_specs, out_specs=out_specs, check_vma=False
    )
```

```python
import functools

import jax
import jax.numpy as jnp
from jax import lax
from jax.experimental import pallas as pl
from jax.experimental.pallas import tpu as pltpu
from jax.sharding import PartitionSpec as P

F32 = jnp.float32
BF16 = jnp.bfloat16
VMEM = pl.BlockSpec(memory_space=pltpu.VMEM)
ANY = pl.BlockSpec(memory_space=pl.ANY)
HEAD_LIMIT = 53 * 2**20
LOAD_LIMIT = 50 * 2**20
OPEN, CLOSING, LATE, LAST = range(4)
PARAMS = pltpu.CompilerParams(vmem_limit_bytes=20 * 2**20)


def flipped():
    return lax.axis_index("rows") == 0


def first_row(place, size, rows):
    return jnp.where(flipped(), rows - place - size, place)


def ring(axis):
    count = lax.axis_size(axis)
    return [(i, (i + 1) % count) for i in range(count)]


def next_odd(piece, axis):
    count = lax.axis_size(axis)
    return lax.ppermute(piece, axis, [(i, (i + 2) % count) for i in range(1, count, 2)])


def within_pairs(piece, axis, keep):
    count = lax.axis_size(axis)
    route = ring(axis) if count % 2 else [(i, i ^ 1) for i in range(count)]
    return lax.ppermute(piece, axis, [(a, b) for a, b in route if b or keep])


def cost(flops, moved):
    return pl.CostEstimate(flops=flops, bytes_accessed=moved, transcendentals=0)


def silu(v):
    half = 0.5 * v
    return half + half * jnp.tanh(half)


def span_of(x_ref, span):
    frame, count, place, size = span
    return x_ref.at[pl.ds(frame, count), pl.ds(first_row(place, size, x_ref.shape[1]), size)]


def keep_rows(x_ref, outs, spans):
    for out, span in zip(outs, spans):
        out[...] = span_of(x_ref, span)[...]


def keep_kernel(x_ref, *outs, spans):
    keep_rows(x_ref, outs, spans)


def row_shapes(x, spans):
    return [jax.ShapeDtypeStruct((count, size) + x.shape[2:], x.dtype) for _, count, _, size in spans]


def slice_kernel(x_ref, *refs, spans):
    outs, sem = refs[:-1], refs[-1]
    copies = [
        pltpu.make_async_copy(span_of(x_ref, span), out, sem.at[k])
        for k, (out, span) in enumerate(zip(outs, spans))
    ]
    for copy in copies:
        copy.start()
    for copy in copies:
        copy.wait()


def edge_kernel(piece_ref, tail_ref, relayed_ref, out_ref, *tail_out_refs):
    size = piece_ref.shape[1]
    out_ref[0] = piece_ref[0, jnp.where(flipped(), size - 1, 0)]
    count = lax.axis_size("frames")
    relay = jnp.logical_and(count % 2 == 0, lax.rem(lax.axis_index("frames"), 2) == 1)

    def cut(source_ref):
        place = 0
        for ref in tail_out_refs:
            ref[...] = span_of(source_ref, (0, 1, place, ref.shape[1]))[...]
            place += ref.shape[1]

    pl.when(relay)(lambda: cut(relayed_ref))
    pl.when(jnp.logical_not(relay))(lambda: cut(tail_ref))


def prepare_kernel(x_ref, ws_ref, bs_ref, wt_ref, bt_ref, conv_ref, wide_ref, mix_ref, cb_ref, mb_ref, *piece_refs, spans):
    keep_rows(x_ref, piece_refs, spans)
    taps, channels = ws_ref.shape[0], ws_ref.shape[2]
    wide = []
    for i in range(taps):
        wide.append(ws_ref[jnp.where(flipped(), taps - 1 - i, i)].reshape(taps * channels, channels))
    wide_ref[...] = jnp.concatenate(wide, axis=0).T
    for j in range(taps):
        blocks = [part[j * channels : (j + 1) * channels] for part in wide]
        conv_ref[j * channels : (j + 1) * channels, :] = jnp.concatenate(blocks, axis=0).T
    mix_ref[...] = wt_ref[...].reshape(taps * channels, channels).T
    width = cb_ref.shape[1]
    cb_ref[...] = jnp.broadcast_to(bs_ref[...], (width, channels)).T
    mb_ref[...] = jnp.broadcast_to(bt_ref[...], (width, channels)).T


def conv_rows(columns, conv, bias, channels, width):
    stacked = jnp.concatenate(columns, axis=1)
    products = jnp.dot(conv, stacked, preferred_element_type=F32)
    lane = lax.broadcasted_iota(jnp.int32, (1, width), 1)
    rows = []
    for q in range(len(columns)):
        part = products[:, q * width : (q + 1) * width]
        left = jnp.where(lane == 0, 0.0, pltpu.roll(part[:channels], 1, 1))
        right = jnp.where(lane == width - 1, 0.0, pltpu.roll(part[2 * channels :], width - 1, 1))
        rows.append(silu(left + part[channels : 2 * channels] + right + bias).astype(BF16))
    return jnp.concatenate(rows, axis=1)


def shifted_rows(row):
    width = row.shape[-1]
    lane = lax.broadcasted_iota(jnp.int32, (1, width), 1)
    wide = row.astype(F32)
    left = jnp.where(lane == 0, 0.0, pltpu.roll(wide, 1, 1)).astype(BF16)
    right = jnp.where(lane == width - 1, 0.0, pltpu.roll(wide, width - 1, 1)).astype(BF16)
    return jnp.concatenate([left, row, right], axis=0)


def own_kernel(x_ref, beside_ref, conv_ref, mix_ref, cb_ref, mb_ref, out_ref, xs, *, group):
    frames, rows, channels, width = x_ref.shape
    for f in range(frames):
        xs[f, 0] = beside_ref[f, 0]
        xs[f, rows + 1] = jnp.zeros((channels, width), BF16)

    def fill(s, carry):
        for f in range(frames):
            xs[f, s + 1] = x_ref[f, first_row(s, 1, rows)]
        return carry

    lax.fori_loop(0, rows, fill, 0)

    def body(p, carry):
        h = p * group
        parts = []
        for f in range(frames):
            columns = [xs[f, pl.ds(h + q, 3)].reshape(3 * channels, width) for q in range(group)]
            parts.append(conv_rows(columns, conv_ref[...], cb_ref[...], channels, width))
        mixed = jnp.dot(mix_ref[:, channels:], jnp.concatenate(parts, axis=0), preferred_element_type=F32)
        for q in range(group):
            out_ref[h + q] = mixed[:, q * width : (q + 1) * width] + mb_ref[...]
        return carry

    lax.fori_loop(0, rows // group, body, 0)


def incoming_kernel(own_ref, wide_ref, mix_ref, cb_ref, *refs, pieces, low, count, ready, stage):
    rows, channels, width = own_ref.shape
    flip = flipped()
    first = lax.axis_index("frames") == 0
    kept_ref, piece_refs, refs = refs[0], refs[1 : 1 + pieces], refs[1 + pieces :]
    ready_ref = out_ref = sem = None
    if ready:
        ready_ref, refs = refs[0], refs[1 + (low > ready) :]
        out_ref, refs, sem = refs[0], refs[1:-1], refs[-1]
    if stage == LAST:
        xs, made_ref = refs
    else:
        made_ref, carry_ref, xs = refs[:3]

    def to_output(source, place, size, k):
        target = out_ref.at[pl.ds(first_row(place, size, rows), size)]
        return pltpu.make_async_copy(source, target, sem.at[k])

    def own_rows(target, size):
        for q in range(size):
            target[jnp.where(flip, size - 1 - q, q)] = own_ref[low + q].astype(BF16)

    def convolve():
        slots = [] if stage == OPEN else [kept_ref.at[k] for k in range(kept_ref.shape[0])]
        fresh = [kept_ref.at[0]] if stage == OPEN else []
        for ref in piece_refs:
            size = ref.shape[1]
            fresh += [ref.at[0, jnp.where(flip, size - 1 - k, k)] for k in range(size)]
        total = len(slots) + len(fresh)
        for k, ref in enumerate(fresh):
            place = len(slots)
            slot = xs.at[k] if stage == LAST or place < total - 2 else carry_ref.at[place - total + 2]
            slot[...] = shifted_rows(ref[...])
            slots.append(slot)
        if stage == LAST:
            xs[len(fresh)] = jnp.zeros((3 * channels, width), BF16)
            slots.append(xs.at[len(fresh)])
        for h in range(0, count, 8):
            group = range(h, min(h + 8, count))
            columns = [jnp.concatenate([slots[q + i][...] for i in range(3)], axis=0) for q in group]
            summed = jnp.dot(wide_ref[...], jnp.concatenate(columns, axis=1), preferred_element_type=F32)
            act = [
                silu(summed[:, (q - h) * width : (q - h + 1) * width] + cb_ref[...]).astype(BF16) for q in group
            ]
            mixed = jnp.dot(mix_ref[:, :channels], jnp.concatenate(act, axis=1), preferred_element_type=F32)
            for q in group:
                term = mixed[:, (q - h) * width : (q - h + 1) * width]
                made_ref[jnp.where(flip, count - 1 - q, q)] = (own_ref[low + q] + term).astype(BF16)

    if stage == OPEN:

        @pl.when(first)
        def _():
            own_rows(made_ref, count)

        @pl.when(jnp.logical_not(first))
        def _():
            convolve()

        return

    before = to_output(ready_ref, low - ready, ready, 0)
    if stage == CLOSING:

        @pl.when(first)
        def _():
            rest = refs[3]
            own_rows(rest, rows - low)
            after = to_output(rest, low, rows - low, 1)
            before.start()
            after.start()
            before.wait()
            after.wait()

    @pl.when(jnp.logical_not(first))
    def _():
        before.start()
        convolve()
        if stage == LAST:
            after = to_output(made_ref, low, count, 1)
            after.start()
            after.wait()
        before.wait()


def incoming_rows(out, made, own, weights, kept, pieces, low, stage):
    wide, mix, cb = weights
    rows, channels, width = own.shape
    held = kept.shape[0] + sum(piece.shape[1] for piece in pieces) + (stage == LAST)
    count = held - 2
    ready = 0 if made is None else made.shape[0]

    def row_array(size):
        return jax.ShapeDtypeStruct((size, channels, width), BF16)

    operands = [own, wide, mix, cb, kept, *pieces]
    in_specs = [VMEM] * len(operands)
    out_shape, out_specs, aliases = [], [], {}
    if ready:
        operands.append(made)
        in_specs.append(VMEM)
        if out is not None:
            aliases = {len(operands): 0}
            operands.append(out)
            in_specs.append(ANY)
        out_shape.append(row_array(rows))
        out_specs.append(ANY)
    if stage != LAST:
        out_shape += [row_array(count), jax.ShapeDtypeStruct((2, 3 * channels, width), BF16)]
        out_specs += [VMEM] * 2
    scratch = [pltpu.VMEM((held, 3 * channels, width), BF16)]
    if stage == LAST:
        scratch.append(pltpu.VMEM((count, channels, width), BF16))
    if stage == CLOSING:
        scratch.append(pltpu.VMEM((rows - low, channels, width), BF16))
    if ready:
        scratch.append(pltpu.SemaphoreType.DMA((2,)))
    results = pl.pallas_call(
        functools.partial(
            incoming_kernel, pieces=len(pieces), low=low, count=count, ready=ready, stage=stage
        ),
        out_shape=out_shape,
        in_specs=in_specs,
        out_specs=out_specs,
        input_output_aliases=aliases,
        scratch_shapes=scratch,
        compiler_params=PARAMS,
        cost_estimate=cost(0, 0),
    )(*operands)
    if stage == LAST:
        return results[0], None, None
    return (results[0] if ready else None), results[-2], results[-1]


def per_device(video, w_spatial, b_spatial, w_temporal, b_temporal):
    frames, rows, width, channels = video.shape
    x = jnp.transpose(video, (0, 1, 3, 2))
    sizes, steps = [rows - 11, 4, 4, 2, 1], [(0, 2), (2, 3), (3, 4), (4, 5)]
    places = [sum(sizes[:k]) for k in range(len(sizes))]
    spans = [(frames - 1, 1, place, size) for place, size in zip(places, sizes)]

    head_spans = [spans[0], (0, frames, 0, 1)]
    head, boundary = pl.pallas_call(
        functools.partial(slice_kernel, spans=head_spans),
        out_shape=row_shapes(x, head_spans),
        in_specs=[ANY],
        out_specs=[VMEM] * 2,
        scratch_shapes=[pltpu.SemaphoreType.DMA((2,))],
        compiler_params=pltpu.CompilerParams(vmem_limit_bytes=HEAD_LIMIT),
    )(x)
    whole = [(0, frames, 0, rows)]
    (x,) = pl.pallas_call(
        functools.partial(slice_kernel, spans=whole),
        out_shape=row_shapes(x, whole),
        in_specs=[ANY],
        out_specs=[VMEM],
        scratch_shapes=[pltpu.SemaphoreType.DMA((1,))],
        compiler_params=pltpu.CompilerParams(vmem_limit_bytes=LOAD_LIMIT),
        cost_estimate=cost(0, 0),
    )(x)
    ending = [(frames - 1, 1, places[-2], sizes[-2] + sizes[-1])]
    (tail,) = pl.pallas_call(
        functools.partial(keep_kernel, spans=ending),
        out_shape=row_shapes(x, ending),
        in_specs=[VMEM],
        out_specs=[VMEM],
        compiler_params=PARAMS,
        cost_estimate=cost(0, 0),
    )(x)
    arrived = [lax.ppermute(head, "frames", ring("frames"))]
    relayed = next_odd(tail, "frames")
    beside = lax.ppermute(boundary, "rows", ring("rows"))

    square = jax.ShapeDtypeStruct((3 * channels, 3 * channels), BF16)
    broad = jax.ShapeDtypeStruct((channels, 9 * channels), BF16)
    flat = jax.ShapeDtypeStruct((channels, 3 * channels), BF16)
    bias = jax.ShapeDtypeStruct((channels, width), F32)
    conv, wide, mix, cb, mb, *pieces = pl.pallas_call(
        functools.partial(prepare_kernel, spans=spans[1:3]),
        out_shape=[square, broad, flat, bias, bias] + row_shapes(x, spans[1:3]),
        in_specs=[VMEM] * 5,
        out_specs=[VMEM] * 7,
        compiler_params=PARAMS,
        cost_estimate=cost(0, 2 * 12 * channels * channels * 2),
    )(x, w_spatial, b_spatial.reshape(1, channels), w_temporal, b_temporal.reshape(1, channels))
    arrived += [lax.ppermute(piece, "frames", ring("frames")) for piece in pieces]

    own = pl.pallas_call(
        functools.partial(own_kernel, group=next(g for g in (8, 4, 3, 2, 1) if rows % g == 0)),
        out_shape=jax.ShapeDtypeStruct((rows, channels, width), F32),
        in_specs=[VMEM] * 6,
        out_specs=VMEM,
        scratch_shapes=[pltpu.VMEM((frames, rows + 2, channels, width), BF16)],
        compiler_params=PARAMS,
        cost_estimate=cost(2 * rows * width * channels * channels * 20, 8 * rows * channels * width),
    )(x, beside, conv, mix, cb, mb)
    own, arrived[0] = lax.optimization_barrier((own, arrived[0]))
    edge, *pieces = pl.pallas_call(
        edge_kernel,
        out_shape=[jax.ShapeDtypeStruct((1, channels, width), BF16)] + row_shapes(x, spans[-2:]),
        in_specs=[VMEM] * 3,
        out_specs=[VMEM] * 3,
        compiler_params=PARAMS,
        cost_estimate=cost(0, 0),
    )(arrived[0], tail, relayed)
    arrived += [within_pairs(pieces[0], "frames", True), within_pairs(pieces[1], "frames", False)]
    kept = lax.ppermute(edge, "rows", ring("rows"))

    weights = (wide, mix, cb)
    out, made, low = None, None, 0
    for k, (begin, end) in enumerate(steps):
        stage = LAST if end == len(arrived) else min(k, LATE)
        out, made, kept = incoming_rows(out, made, own, weights, kept, arrived[begin:end], low, stage)
        low = places[end - 1] + sizes[end - 1] - 1
    return jnp.transpose(out[None], (0, 1, 3, 2))


def solution(mesh):
    in_specs = (P(("batch", "frames"), "rows", None, None), P(), P(), P(), P())
    out_specs = P(("batch", "frames"), "rows", None, None)
    return jax.shard_map(
        per_device, mesh=mesh, in_specs=in_specs, out_specs=out_specs, check_vma=False
    )
```

```python
import functools

import jax
import jax.numpy as jnp
from jax import lax
from jax.experimental import pallas as pl
from jax.experimental.pallas import tpu as pltpu
from jax.sharding import PartitionSpec as P

F32 = jnp.float32
BF16 = jnp.bfloat16
VMEM = pl.BlockSpec(memory_space=pltpu.VMEM)
ANY = pl.BlockSpec(memory_space=pl.ANY)
HEAD_LIMIT = 53 * 2**20
LOAD_LIMIT = 50 * 2**20
OPEN, CLOSING, LATE, LAST = range(4)
PARAMS = pltpu.CompilerParams(vmem_limit_bytes=20 * 2**20)


def flipped():
    return lax.axis_index("rows") == 0


def first_row(place, size, rows):
    return jnp.where(flipped(), rows - place - size, place)


def ring(axis):
    count = lax.axis_size(axis)
    return [(i, (i + 1) % count) for i in range(count)]


def next_odd(piece, axis):
    count = lax.axis_size(axis)
    return lax.ppermute(piece, axis, [(i, (i + 2) % count) for i in range(1, count, 2)])


def within_pairs(piece, axis, keep):
    count = lax.axis_size(axis)
    route = ring(axis) if count % 2 else [(i, i ^ 1) for i in range(count)]
    return lax.ppermute(piece, axis, [(a, b) for a, b in route if b or keep])


def cost(flops, moved):
    return pl.CostEstimate(flops=flops, bytes_accessed=moved, transcendentals=0)


def silu(v):
    half = 0.5 * v
    return half + half * jnp.tanh(half)


def span_of(x_ref, span):
    frame, count, place, size = span
    return x_ref.at[pl.ds(frame, count), pl.ds(first_row(place, size, x_ref.shape[1]), size)]


def keep_rows(x_ref, outs, spans):
    for out, span in zip(outs, spans):
        out[...] = span_of(x_ref, span)[...]


def load_kernel(x_ref, head_ref, *refs, spans):
    slice_kernel(x_ref, *refs, spans=spans)


def keep_kernel(x_ref, *outs, spans):
    keep_rows(x_ref, outs, spans)


def row_shapes(x, spans):
    return [jax.ShapeDtypeStruct((count, size) + x.shape[2:], x.dtype) for _, count, _, size in spans]


def slice_kernel(x_ref, *refs, spans):
    outs, sem = refs[:-1], refs[-1]
    copies = [
        pltpu.make_async_copy(span_of(x_ref, span), out, sem.at[k])
        for k, (out, span) in enumerate(zip(outs, spans))
    ]
    for copy in copies:
        copy.start()
    for copy in copies:
        copy.wait()


def edge_kernel(piece_ref, tail_ref, relayed_ref, second_ref, out_ref, *tail_out_refs):
    size = piece_ref.shape[1]
    out_ref[0] = piece_ref[0, jnp.where(flipped(), size - 1, 0)]
    count = lax.axis_size("frames")
    relay = jnp.logical_and(count % 2 == 0, lax.rem(lax.axis_index("frames"), 2) == 1)

    def cut(source_ref):
        place = 0
        for ref in tail_out_refs:
            ref[...] = span_of(source_ref, (0, 1, place, ref.shape[1]))[...]
            place += ref.shape[1]

    pl.when(relay)(lambda: cut(relayed_ref))
    pl.when(jnp.logical_not(relay))(lambda: cut(tail_ref))


def prepare_kernel(x_ref, ws_ref, bs_ref, wt_ref, bt_ref, conv_ref, wide_ref, mix_ref, cb_ref, mb_ref, *piece_refs, spans):
    keep_rows(x_ref, piece_refs, spans)
    taps, channels = ws_ref.shape[0], ws_ref.shape[2]
    wide = []
    for i in range(taps):
        wide.append(ws_ref[jnp.where(flipped(), taps - 1 - i, i)].reshape(taps * channels, channels))
    wide_ref[...] = jnp.concatenate(wide, axis=0).T
    for j in range(taps):
        blocks = [part[j * channels : (j + 1) * channels] for part in wide]
        conv_ref[j * channels : (j + 1) * channels, :] = jnp.concatenate(blocks, axis=0).T
    mix_ref[...] = wt_ref[...].reshape(taps * channels, channels).T
    width = cb_ref.shape[1]
    cb_ref[...] = jnp.broadcast_to(bs_ref[...], (width, channels)).T
    mb_ref[...] = jnp.broadcast_to(bt_ref[...], (width, channels)).T


def conv_rows(columns, conv, bias, channels, width):
    stacked = jnp.concatenate(columns, axis=1)
    products = jnp.dot(conv, stacked, preferred_element_type=F32)
    lane = lax.broadcasted_iota(jnp.int32, (1, width), 1)
    rows = []
    for q in range(len(columns)):
        part = products[:, q * width : (q + 1) * width]
        left = jnp.where(lane == 0, 0.0, pltpu.roll(part[:channels], 1, 1))
        right = jnp.where(lane == width - 1, 0.0, pltpu.roll(part[2 * channels :], width - 1, 1))
        rows.append(silu(left + part[channels : 2 * channels] + right + bias).astype(BF16))
    return jnp.concatenate(rows, axis=1)


def shifted_rows(row):
    width = row.shape[-1]
    lane = lax.broadcasted_iota(jnp.int32, (1, width), 1)
    wide = row.astype(F32)
    left = jnp.where(lane == 0, 0.0, pltpu.roll(wide, 1, 1)).astype(BF16)
    right = jnp.where(lane == width - 1, 0.0, pltpu.roll(wide, width - 1, 1)).astype(BF16)
    return jnp.concatenate([left, row, right], axis=0)


def own_kernel(x_ref, beside_ref, conv_ref, mix_ref, cb_ref, mb_ref, early_ref, out_ref, xs, *, group):
    frames, rows, channels, width = x_ref.shape
    for f in range(frames):
        xs[f, 0] = beside_ref[f, 0]
        xs[f, rows + 1] = jnp.zeros((channels, width), BF16)

    def fill(s, carry):
        for f in range(frames):
            xs[f, s + 1] = x_ref[f, first_row(s, 1, rows)]
        return carry

    lax.fori_loop(0, rows, fill, 0)

    def body(p, carry):
        h = p * group
        parts = []
        for f in range(frames):
            columns = [xs[f, pl.ds(h + q, 3)].reshape(3 * channels, width) for q in range(group)]
            parts.append(conv_rows(columns, conv_ref[...], cb_ref[...], channels, width))
        mixed = jnp.dot(mix_ref[:, channels:], jnp.concatenate(parts, axis=0), preferred_element_type=F32)
        for q in range(group):
            out_ref[h + q] = mixed[:, q * width : (q + 1) * width] + mb_ref[...]
        return carry

    lax.fori_loop(0, rows // group, body, 0)


def incoming_kernel(own_ref, wide_ref, mix_ref, cb_ref, *refs, pieces, low, count, ready, stage):
    rows, channels, width = own_ref.shape
    flip = flipped()
    first = lax.axis_index("frames") == 0
    kept_ref, piece_refs, refs = refs[0], refs[1 : 1 + pieces], refs[1 + pieces :]
    ready_ref = out_ref = sem = None
    if ready:
        ready_ref, refs = refs[0], refs[1 + (low > ready) :]
        out_ref, refs, sem = refs[0], refs[1:-1], refs[-1]
    if stage == LAST:
        xs, made_ref = refs
    else:
        made_ref, carry_ref, xs = refs[:3]

    def to_output(source, place, size, k):
        target = out_ref.at[pl.ds(first_row(place, size, rows), size)]
        return pltpu.make_async_copy(source, target, sem.at[k])

    def own_rows(target, size):
        for q in range(size):
            target[jnp.where(flip, size - 1 - q, q)] = own_ref[low + q].astype(BF16)

    def convolve():
        slots = [] if stage == OPEN else [kept_ref.at[k] for k in range(kept_ref.shape[0])]
        fresh = [kept_ref.at[0]] if stage == OPEN else []
        for ref in piece_refs:
            size = ref.shape[1]
            fresh += [ref.at[0, jnp.where(flip, size - 1 - k, k)] for k in range(size)]
        total = len(slots) + len(fresh)
        for k, ref in enumerate(fresh):
            place = len(slots)
            slot = xs.at[k] if stage == LAST or place < total - 2 else carry_ref.at[place - total + 2]
            slot[...] = shifted_rows(ref[...])
            slots.append(slot)
        if stage == LAST:
            xs[len(fresh)] = jnp.zeros((3 * channels, width), BF16)
            slots.append(xs.at[len(fresh)])
        for h in range(0, count, 8):
            group = range(h, min(h + 8, count))
            columns = [jnp.concatenate([slots[q + i][...] for i in range(3)], axis=0) for q in group]
            summed = jnp.dot(wide_ref[...], jnp.concatenate(columns, axis=1), preferred_element_type=F32)
            act = [
                silu(summed[:, (q - h) * width : (q - h + 1) * width] + cb_ref[...]).astype(BF16) for q in group
            ]
            mixed = jnp.dot(mix_ref[:, :channels], jnp.concatenate(act, axis=1), preferred_element_type=F32)
            for q in group:
                term = mixed[:, (q - h) * width : (q - h + 1) * width]
                made_ref[jnp.where(flip, count - 1 - q, q)] = (own_ref[low + q] + term).astype(BF16)

    if stage == OPEN:

        @pl.when(first)
        def _():
            own_rows(made_ref, count)

        @pl.when(jnp.logical_not(first))
        def _():
            convolve()

        return

    before = to_output(ready_ref, low - ready, ready, 0)
    if stage == CLOSING:

        @pl.when(first)
        def _():
            rest = refs[3]
            own_rows(rest, rows - low)
            after = to_output(rest, low, rows - low, 1)
            before.start()
            after.start()
            before.wait()
            after.wait()

    @pl.when(jnp.logical_not(first))
    def _():
        before.start()
        convolve()
        if stage == LAST:
            after = to_output(made_ref, low, count, 1)
            after.start()
            after.wait()
        before.wait()


def incoming_rows(out, made, own, weights, kept, pieces, low, stage):
    wide, mix, cb = weights
    rows, channels, width = own.shape
    held = kept.shape[0] + sum(piece.shape[1] for piece in pieces) + (stage == LAST)
    count = held - 2
    ready = 0 if made is None else made.shape[0]

    def row_array(size):
        return jax.ShapeDtypeStruct((size, channels, width), BF16)

    operands = [own, wide, mix, cb, kept, *pieces]
    in_specs = [VMEM] * len(operands)
    out_shape, out_specs, aliases = [], [], {}
    if ready:
        operands.append(made)
        in_specs.append(VMEM)
        if out is not None:
            aliases = {len(operands): 0}
            operands.append(out)
            in_specs.append(ANY)
        out_shape.append(row_array(rows))
        out_specs.append(ANY)
    if stage != LAST:
        out_shape += [row_array(count), jax.ShapeDtypeStruct((2, 3 * channels, width), BF16)]
        out_specs += [VMEM] * 2
    scratch = [pltpu.VMEM((held, 3 * channels, width), BF16)]
    if stage == LAST:
        scratch.append(pltpu.VMEM((count, channels, width), BF16))
    if stage == CLOSING:
        scratch.append(pltpu.VMEM((rows - low, channels, width), BF16))
    if ready:
        scratch.append(pltpu.SemaphoreType.DMA((2,)))
    results = pl.pallas_call(
        functools.partial(
            incoming_kernel, pieces=len(pieces), low=low, count=count, ready=ready, stage=stage
        ),
        out_shape=out_shape,
        in_specs=in_specs,
        out_specs=out_specs,
        input_output_aliases=aliases,
        scratch_shapes=scratch,
        compiler_params=PARAMS,
        cost_estimate=cost(0, 0),
    )(*operands)
    if stage == LAST:
        return results[0], None, None
    return (results[0] if ready else None), results[-2], results[-1]


def per_device(video, w_spatial, b_spatial, w_temporal, b_temporal):
    frames, rows, width, channels = video.shape
    x = jnp.transpose(video, (0, 1, 3, 2))
    sizes, steps = [3, rows - 10, 4, 2, 1], [(0, 2), (2, 3), (3, 4), (4, 5)]
    places = [sum(sizes[:k]) for k in range(len(sizes))]
    spans = [(frames - 1, 1, place, size) for place, size in zip(places, sizes)]

    (head,) = pl.pallas_call(
        functools.partial(slice_kernel, spans=spans[:1]),
        out_shape=row_shapes(x, spans[:1]),
        in_specs=[ANY],
        out_specs=[VMEM],
        scratch_shapes=[pltpu.SemaphoreType.DMA((1,))],
        compiler_params=pltpu.CompilerParams(vmem_limit_bytes=HEAD_LIMIT),
    )(x)
    whole = [(0, frames, 0, rows)]
    (x,) = pl.pallas_call(
        functools.partial(load_kernel, spans=whole),
        out_shape=row_shapes(x, whole),
        in_specs=[ANY] * 2,
        out_specs=[VMEM],
        scratch_shapes=[pltpu.SemaphoreType.DMA((1,))],
        compiler_params=pltpu.CompilerParams(vmem_limit_bytes=LOAD_LIMIT),
        cost_estimate=cost(0, 0),
    )(x, head)
    kept_spans = [(0, frames, 0, 1), (frames - 1, 1, places[-2], sizes[-2] + sizes[-1]), spans[1]]
    boundary, tail, second = pl.pallas_call(
        functools.partial(keep_kernel, spans=kept_spans),
        out_shape=row_shapes(x, kept_spans),
        in_specs=[VMEM],
        out_specs=[VMEM] * 3,
        compiler_params=PARAMS,
        cost_estimate=cost(0, 0),
    )(x)
    arrived = [lax.ppermute(piece, "frames", ring("frames")) for piece in (head, second)]
    relayed = next_odd(tail, "frames")
    beside = lax.ppermute(boundary, "rows", ring("rows"))

    square = jax.ShapeDtypeStruct((3 * channels, 3 * channels), BF16)
    broad = jax.ShapeDtypeStruct((channels, 9 * channels), BF16)
    flat = jax.ShapeDtypeStruct((channels, 3 * channels), BF16)
    bias = jax.ShapeDtypeStruct((channels, width), F32)
    conv, wide, mix, cb, mb, *pieces = pl.pallas_call(
        functools.partial(prepare_kernel, spans=spans[2:3]),
        out_shape=[square, broad, flat, bias, bias] + row_shapes(x, spans[2:3]),
        in_specs=[VMEM] * 5,
        out_specs=[VMEM] * 6,
        compiler_params=PARAMS,
        cost_estimate=cost(0, 2 * 12 * channels * channels * 2),
    )(x, w_spatial, b_spatial.reshape(1, channels), w_temporal, b_temporal.reshape(1, channels))
    arrived += [lax.ppermute(piece, "frames", ring("frames")) for piece in pieces]

    own = pl.pallas_call(
        functools.partial(own_kernel, group=next(g for g in (8, 4, 3, 2, 1) if rows % g == 0)),
        out_shape=jax.ShapeDtypeStruct((rows, channels, width), F32),
        in_specs=[VMEM] * 6 + [ANY],
        out_specs=VMEM,
        scratch_shapes=[pltpu.VMEM((frames, rows + 2, channels, width), BF16)],
        compiler_params=PARAMS,
        cost_estimate=cost(2 * rows * width * channels * channels * 20, 8 * rows * channels * width),
    )(x, beside, conv, mix, cb, mb, arrived[0])
    own, arrived[0] = lax.optimization_barrier((own, arrived[0]))
    edge, *pieces = pl.pallas_call(
        edge_kernel,
        out_shape=[jax.ShapeDtypeStruct((1, channels, width), BF16)] + row_shapes(x, spans[-2:]),
        in_specs=[VMEM] * 3 + [ANY],
        out_specs=[VMEM] * 3,
        compiler_params=PARAMS,
        cost_estimate=cost(0, 0),
    )(arrived[0], tail, relayed, arrived[1])
    arrived += [within_pairs(pieces[0], "frames", True), within_pairs(pieces[1], "frames", False)]
    kept = lax.ppermute(edge, "rows", ring("rows"))

    weights = (wide, mix, cb)
    out, made, low = None, None, 0
    for k, (begin, end) in enumerate(steps):
        stage = LAST if end == len(arrived) else min(k, LATE)
        out, made, kept = incoming_rows(out, made, own, weights, kept, arrived[begin:end], low, stage)
        low = places[end - 1] + sizes[end - 1] - 1
    return jnp.transpose(out[None], (0, 1, 3, 2))


def solution(mesh):
    in_specs = (P(("batch", "frames"), "rows", None, None), P(), P(), P(), P())
    out_specs = P(("batch", "frames"), "rows", None, None)
    return jax.shard_map(
        per_device, mesh=mesh, in_specs=in_specs, out_specs=out_specs, check_vma=False
    )
```

```python
import functools

import jax
import jax.numpy as jnp
from jax import lax
from jax.experimental import pallas as pl
from jax.experimental.pallas import tpu as pltpu
from jax.sharding import PartitionSpec as P

F32 = jnp.float32
BF16 = jnp.bfloat16
VMEM = pl.BlockSpec(memory_space=pltpu.VMEM)
ANY = pl.BlockSpec(memory_space=pl.ANY)
HEAD_LIMIT = 53 * 2**20
LOAD_LIMIT = 50 * 2**20
OPEN, CLOSING, LATE, LAST = range(4)
PARAMS = pltpu.CompilerParams(vmem_limit_bytes=20 * 2**20)


def flipped():
    return lax.axis_index("rows") == 0


def first_row(place, size, rows):
    return jnp.where(flipped(), rows - place - size, place)


def ring(axis):
    count = lax.axis_size(axis)
    return [(i, (i + 1) % count) for i in range(count)]


def next_odd(piece, axis):
    count = lax.axis_size(axis)
    return lax.ppermute(piece, axis, [(i, (i + 2) % count) for i in range(1, count, 2)])


def within_pairs(piece, axis, keep):
    count = lax.axis_size(axis)
    route = ring(axis) if count % 2 else [(i, i ^ 1) for i in range(count)]
    return lax.ppermute(piece, axis, [(a, b) for a, b in route if b or keep])


def cost(flops, moved):
    return pl.CostEstimate(flops=flops, bytes_accessed=moved, transcendentals=0)


def silu(v):
    half = 0.5 * v
    return half + half * jnp.tanh(half)


def span_of(x_ref, span):
    frame, count, place, size = span
    return x_ref.at[pl.ds(frame, count), pl.ds(first_row(place, size, x_ref.shape[1]), size)]


def keep_rows(x_ref, outs, spans):
    for out, span in zip(outs, spans):
        out[...] = span_of(x_ref, span)[...]


def load_kernel(x_ref, head_ref, *refs, spans):
    slice_kernel(x_ref, *refs, spans=spans)


def keep_kernel(x_ref, *outs, spans):
    keep_rows(x_ref, outs, spans)


def row_shapes(x, spans):
    return [jax.ShapeDtypeStruct((count, size) + x.shape[2:], x.dtype) for _, count, _, size in spans]


def slice_kernel(x_ref, *refs, spans):
    outs, sem = refs[:-1], refs[-1]
    copies = [
        pltpu.make_async_copy(span_of(x_ref, span), out, sem.at[k])
        for k, (out, span) in enumerate(zip(outs, spans))
    ]
    for copy in copies:
        copy.start()
    for copy in copies:
        copy.wait()


def edge_kernel(piece_ref, tail_ref, relayed_ref, second_ref, out_ref, *tail_out_refs):
    size = piece_ref.shape[1]
    out_ref[0] = piece_ref[0, jnp.where(flipped(), size - 1, 0)]
    count = lax.axis_size("frames")
    relay = jnp.logical_and(count % 2 == 0, lax.rem(lax.axis_index("frames"), 2) == 1)

    def cut(source_ref):
        place = 0
        for ref in tail_out_refs:
            ref[...] = span_of(source_ref, (0, 1, place, ref.shape[1]))[...]
            place += ref.shape[1]

    pl.when(relay)(lambda: cut(relayed_ref))
    pl.when(jnp.logical_not(relay))(lambda: cut(tail_ref))


def prepare_kernel(x_ref, ws_ref, bs_ref, wt_ref, bt_ref, conv_ref, wide_ref, mix_ref, cb_ref, mb_ref, *piece_refs, spans):
    keep_rows(x_ref, piece_refs, spans)
    taps, channels = ws_ref.shape[0], ws_ref.shape[2]
    wide = []
    for i in range(taps):
        wide.append(ws_ref[jnp.where(flipped(), taps - 1 - i, i)].reshape(taps * channels, channels))
    wide_ref[...] = jnp.concatenate(wide, axis=0).T
    for j in range(taps):
        blocks = [part[j * channels : (j + 1) * channels] for part in wide]
        conv_ref[j * channels : (j + 1) * channels, :] = jnp.concatenate(blocks, axis=0).T
    mix_ref[...] = wt_ref[...].reshape(taps * channels, channels).T
    width = cb_ref.shape[1]
    cb_ref[...] = jnp.broadcast_to(bs_ref[...], (width, channels)).T
    mb_ref[...] = jnp.broadcast_to(bt_ref[...], (width, channels)).T


def conv_rows(columns, conv, bias, channels, width):
    stacked = jnp.concatenate(columns, axis=1)
    products = jnp.dot(conv, stacked, preferred_element_type=F32)
    lane = lax.broadcasted_iota(jnp.int32, (1, width), 1)
    rows = []
    for q in range(len(columns)):
        part = products[:, q * width : (q + 1) * width]
        left = jnp.where(lane == 0, 0.0, pltpu.roll(part[:channels], 1, 1))
        right = jnp.where(lane == width - 1, 0.0, pltpu.roll(part[2 * channels :], width - 1, 1))
        rows.append(silu(left + part[channels : 2 * channels] + right + bias).astype(BF16))
    return jnp.concatenate(rows, axis=1)


def shifted_rows(row):
    width = row.shape[-1]
    lane = lax.broadcasted_iota(jnp.int32, (1, width), 1)
    wide = row.astype(F32)
    left = jnp.where(lane == 0, 0.0, pltpu.roll(wide, 1, 1)).astype(BF16)
    right = jnp.where(lane == width - 1, 0.0, pltpu.roll(wide, width - 1, 1)).astype(BF16)
    return jnp.concatenate([left, row, right], axis=0)


def own_kernel(x_ref, beside_ref, conv_ref, mix_ref, cb_ref, mb_ref, early_ref, out_ref, xs, *, group):
    frames, rows, channels, width = x_ref.shape
    for f in range(frames):
        xs[f, 0] = beside_ref[f, 0]
        xs[f, rows + 1] = jnp.zeros((channels, width), BF16)

    def fill(s, carry):
        for f in range(frames):
            xs[f, s + 1] = x_ref[f, first_row(s, 1, rows)]
        return carry

    lax.fori_loop(0, rows, fill, 0)

    def body(p, carry):
        h = p * group
        parts = []
        for f in range(frames):
            columns = [xs[f, pl.ds(h + q, 3)].reshape(3 * channels, width) for q in range(group)]
            parts.append(conv_rows(columns, conv_ref[...], cb_ref[...], channels, width))
        mixed = jnp.dot(mix_ref[:, channels:], jnp.concatenate(parts, axis=0), preferred_element_type=F32)
        for q in range(group):
            out_ref[h + q] = mixed[:, q * width : (q + 1) * width] + mb_ref[...]
        return carry

    lax.fori_loop(0, rows // group, body, 0)


def incoming_kernel(own_ref, wide_ref, mix_ref, cb_ref, *refs, pieces, low, count, ready, stage):
    rows, channels, width = own_ref.shape
    flip = flipped()
    first = lax.axis_index("frames") == 0
    kept_ref, piece_refs, refs = refs[0], refs[1 : 1 + pieces], refs[1 + pieces :]
    ready_ref = out_ref = sem = None
    if ready:
        ready_ref, refs = refs[0], refs[1 + (low > ready) :]
        out_ref, refs, sem = refs[0], refs[1:-1], refs[-1]
    if stage == LAST:
        xs, made_ref = refs
    else:
        made_ref, carry_ref, xs = refs[:3]

    def to_output(source, place, size, k):
        target = out_ref.at[pl.ds(first_row(place, size, rows), size)]
        return pltpu.make_async_copy(source, target, sem.at[k])

    def own_rows(target, size):
        for q in range(size):
            target[jnp.where(flip, size - 1 - q, q)] = own_ref[low + q].astype(BF16)

    def convolve():
        slots = [] if stage == OPEN else [kept_ref.at[k] for k in range(kept_ref.shape[0])]
        fresh = [kept_ref.at[0]] if stage == OPEN else []
        for ref in piece_refs:
            size = ref.shape[1]
            fresh += [ref.at[0, jnp.where(flip, size - 1 - k, k)] for k in range(size)]
        total = len(slots) + len(fresh)
        for k, ref in enumerate(fresh):
            place = len(slots)
            slot = xs.at[k] if stage == LAST or place < total - 2 else carry_ref.at[place - total + 2]
            slot[...] = shifted_rows(ref[...])
            slots.append(slot)
        if stage == LAST:
            xs[len(fresh)] = jnp.zeros((3 * channels, width), BF16)
            slots.append(xs.at[len(fresh)])
        for h in range(0, count, 8):
            group = range(h, min(h + 8, count))
            columns = [jnp.concatenate([slots[q + i][...] for i in range(3)], axis=0) for q in group]
            summed = jnp.dot(wide_ref[...], jnp.concatenate(columns, axis=1), preferred_element_type=F32)
            act = [
                silu(summed[:, (q - h) * width : (q - h + 1) * width] + cb_ref[...]).astype(BF16) for q in group
            ]
            mixed = jnp.dot(mix_ref[:, :channels], jnp.concatenate(act, axis=1), preferred_element_type=F32)
            for q in group:
                term = mixed[:, (q - h) * width : (q - h + 1) * width]
                made_ref[jnp.where(flip, count - 1 - q, q)] = (own_ref[low + q] + term).astype(BF16)

    if stage == OPEN:

        @pl.when(first)
        def _():
            own_rows(made_ref, count)

        @pl.when(jnp.logical_not(first))
        def _():
            convolve()

        return

    before = to_output(ready_ref, low - ready, ready, 0)
    if stage == CLOSING:

        @pl.when(first)
        def _():
            rest = refs[3]
            own_rows(rest, rows - low)
            after = to_output(rest, low, rows - low, 1)
            before.start()
            after.start()
            before.wait()
            after.wait()

    @pl.when(jnp.logical_not(first))
    def _():
        before.start()
        convolve()
        if stage == LAST:
            after = to_output(made_ref, low, count, 1)
            after.start()
            after.wait()
        before.wait()


def incoming_rows(out, made, own, weights, kept, pieces, low, stage):
    wide, mix, cb = weights
    rows, channels, width = own.shape
    held = kept.shape[0] + sum(piece.shape[1] for piece in pieces) + (stage == LAST)
    count = held - 2
    ready = 0 if made is None else made.shape[0]

    def row_array(size):
        return jax.ShapeDtypeStruct((size, channels, width), BF16)

    operands = [own, wide, mix, cb, kept, *pieces]
    in_specs = [VMEM] * len(operands)
    out_shape, out_specs, aliases = [], [], {}
    if ready:
        operands.append(made)
        in_specs.append(VMEM)
        if out is not None:
            aliases = {len(operands): 0}
            operands.append(out)
            in_specs.append(ANY)
        out_shape.append(row_array(rows))
        out_specs.append(ANY)
    if stage != LAST:
        out_shape += [row_array(count), jax.ShapeDtypeStruct((2, 3 * channels, width), BF16)]
        out_specs += [VMEM] * 2
    scratch = [pltpu.VMEM((held, 3 * channels, width), BF16)]
    if stage == LAST:
        scratch.append(pltpu.VMEM((count, channels, width), BF16))
    if stage == CLOSING:
        scratch.append(pltpu.VMEM((rows - low, channels, width), BF16))
    if ready:
        scratch.append(pltpu.SemaphoreType.DMA((2,)))
    results = pl.pallas_call(
        functools.partial(
            incoming_kernel, pieces=len(pieces), low=low, count=count, ready=ready, stage=stage
        ),
        out_shape=out_shape,
        in_specs=in_specs,
        out_specs=out_specs,
        input_output_aliases=aliases,
        scratch_shapes=scratch,
        compiler_params=PARAMS,
        cost_estimate=cost(0, 0),
    )(*operands)
    if stage == LAST:
        return results[0], None, None
    return (results[0] if ready else None), results[-2], results[-1]


def per_device(video, w_spatial, b_spatial, w_temporal, b_temporal):
    frames, rows, width, channels = video.shape
    x = jnp.transpose(video, (0, 1, 3, 2))
    sizes, steps = [3, rows - 10, 4, 2, 1], [(0, 2), (2, 3), (3, 4), (4, 5)]
    places = [sum(sizes[:k]) for k in range(len(sizes))]
    spans = [(frames - 1, 1, place, size) for place, size in zip(places, sizes)]

    (head,) = pl.pallas_call(
        functools.partial(slice_kernel, spans=spans[:1]),
        out_shape=row_shapes(x, spans[:1]),
        in_specs=[ANY],
        out_specs=[VMEM],
        scratch_shapes=[pltpu.SemaphoreType.DMA((1,))],
        compiler_params=pltpu.CompilerParams(vmem_limit_bytes=HEAD_LIMIT),
    )(x)
    whole = [(0, frames, 0, rows)]
    (x,) = pl.pallas_call(
        functools.partial(load_kernel, spans=whole),
        out_shape=row_shapes(x, whole),
        in_specs=[ANY] * 2,
        out_specs=[VMEM],
        scratch_shapes=[pltpu.SemaphoreType.DMA((1,))],
        compiler_params=pltpu.CompilerParams(vmem_limit_bytes=LOAD_LIMIT),
        cost_estimate=cost(0, 0),
    )(x, head)
    ending = (frames - 1, 1, places[-2], sizes[-2] + sizes[-1])
    kept_spans = [(0, frames, 0, 1), spans[1]]
    boundary, second = pl.pallas_call(
        functools.partial(keep_kernel, spans=kept_spans),
        out_shape=row_shapes(x, kept_spans),
        in_specs=[VMEM],
        out_specs=[VMEM] * 2,
        compiler_params=PARAMS,
        cost_estimate=cost(0, 0),
    )(x)
    arrived = [lax.ppermute(piece, "frames", ring("frames")) for piece in (head, second)]
    beside = lax.ppermute(boundary, "rows", ring("rows"))

    square = jax.ShapeDtypeStruct((3 * channels, 3 * channels), BF16)
    broad = jax.ShapeDtypeStruct((channels, 9 * channels), BF16)
    flat = jax.ShapeDtypeStruct((channels, 3 * channels), BF16)
    bias = jax.ShapeDtypeStruct((channels, width), F32)
    conv, wide, mix, cb, mb, piece, tail = pl.pallas_call(
        functools.partial(prepare_kernel, spans=[spans[2], ending]),
        out_shape=[square, broad, flat, bias, bias] + row_shapes(x, [spans[2], ending]),
        in_specs=[VMEM] * 5,
        out_specs=[VMEM] * 7,
        compiler_params=PARAMS,
        cost_estimate=cost(0, 2 * 12 * channels * channels * 2),
    )(x, w_spatial, b_spatial.reshape(1, channels), w_temporal, b_temporal.reshape(1, channels))
    arrived.append(lax.ppermute(piece, "frames", ring("frames")))
    relayed = next_odd(tail, "frames")

    own = pl.pallas_call(
        functools.partial(own_kernel, group=next(g for g in (8, 4, 3, 2, 1) if rows % g == 0)),
        out_shape=jax.ShapeDtypeStruct((rows, channels, width), F32),
        in_specs=[VMEM] * 6 + [ANY],
        out_specs=VMEM,
        scratch_shapes=[pltpu.VMEM((frames, rows + 2, channels, width), BF16)],
        compiler_params=PARAMS,
        cost_estimate=cost(2 * rows * width * channels * channels * 20, 8 * rows * channels * width),
    )(x, beside, conv, mix, cb, mb, arrived[0])
    own, arrived[0] = lax.optimization_barrier((own, arrived[0]))
    edge, *pieces = pl.pallas_call(
        edge_kernel,
        out_shape=[jax.ShapeDtypeStruct((1, channels, width), BF16)] + row_shapes(x, spans[-2:]),
        in_specs=[VMEM] * 3 + [ANY],
        out_specs=[VMEM] * 3,
        compiler_params=PARAMS,
        cost_estimate=cost(0, 0),
    )(arrived[0], tail, relayed, arrived[1])
    arrived += [within_pairs(pieces[0], "frames", True), within_pairs(pieces[1], "frames", True)]
    kept = lax.ppermute(edge, "rows", ring("rows"))

    weights = (wide, mix, cb)
    out, made, low = None, None, 0
    for k, (begin, end) in enumerate(steps):
        stage = LAST if end == len(arrived) else min(k, LATE)
        out, made, kept = incoming_rows(out, made, own, weights, kept, arrived[begin:end], low, stage)
        low = places[end - 1] + sizes[end - 1] - 1
    return jnp.transpose(out[None], (0, 1, 3, 2))


def solution(mesh):
    in_specs = (P(("batch", "frames"), "rows", None, None), P(), P(), P(), P())
    out_specs = P(("batch", "frames"), "rows", None, None)
    return jax.shard_map(
        per_device, mesh=mesh, in_specs=in_specs, out_specs=out_specs, check_vma=False
    )
```

```python
import functools

import jax
import jax.numpy as jnp
from jax import lax
from jax.experimental import pallas as pl
from jax.experimental.pallas import tpu as pltpu
from jax.sharding import PartitionSpec as P

F32 = jnp.float32
BF16 = jnp.bfloat16
VMEM = pl.BlockSpec(memory_space=pltpu.VMEM)
ANY = pl.BlockSpec(memory_space=pl.ANY)
HEAD_LIMIT = 53 * 2**20
LOAD_LIMIT = 50 * 2**20
OPEN, CLOSING, LATE, LAST = range(4)
PARAMS = pltpu.CompilerParams(vmem_limit_bytes=20 * 2**20)


def flipped():
    return lax.axis_index("rows") == 0


def first_row(place, size, rows):
    return jnp.where(flipped(), rows - place - size, place)


def ring(axis):
    count = lax.axis_size(axis)
    return [(i, (i + 1) % count) for i in range(count)]


def next_odd(piece, axis):
    count = lax.axis_size(axis)
    return lax.ppermute(piece, axis, [(i, (i + 2) % count) for i in range(1, count, 2)])


def within_pairs(piece, axis, keep):
    count = lax.axis_size(axis)
    route = ring(axis) if count % 2 else [(i, i ^ 1) for i in range(count)]
    return lax.ppermute(piece, axis, [(a, b) for a, b in route if b or keep])


def cost(flops, moved):
    return pl.CostEstimate(flops=flops, bytes_accessed=moved, transcendentals=0)


def silu(v):
    half = 0.5 * v
    return half + half * jnp.tanh(half)


def span_of(x_ref, span):
    frame, count, place, size = span
    return x_ref.at[pl.ds(frame, count), pl.ds(first_row(place, size, x_ref.shape[1]), size)]


def keep_rows(x_ref, outs, spans):
    for out, span in zip(outs, spans):
        out[...] = span_of(x_ref, span)[...]


def load_kernel(x_ref, head_ref, *refs, spans):
    slice_kernel(x_ref, *refs, spans=spans)


def keep_kernel(x_ref, *outs, spans):
    keep_rows(x_ref, outs, spans)


def row_shapes(x, spans):
    return [jax.ShapeDtypeStruct((count, size) + x.shape[2:], x.dtype) for _, count, _, size in spans]


def slice_kernel(x_ref, *refs, spans):
    outs, sem = refs[:-1], refs[-1]
    copies = [
        pltpu.make_async_copy(span_of(x_ref, span), out, sem.at[k])
        for k, (out, span) in enumerate(zip(outs, spans))
    ]
    for copy in copies:
        copy.start()
    for copy in copies:
        copy.wait()


def edge_kernel(piece_ref, tail_ref, relayed_ref, second_ref, out_ref, *tail_out_refs):
    size = piece_ref.shape[1]
    out_ref[0] = piece_ref[0, jnp.where(flipped(), size - 1, 0)]
    count = lax.axis_size("frames")
    relay = jnp.logical_and(count % 2 == 0, lax.rem(lax.axis_index("frames"), 2) == 1)

    def cut(source_ref):
        place = 0
        for ref in tail_out_refs:
            ref[...] = span_of(source_ref, (0, 1, place, ref.shape[1]))[...]
            place += ref.shape[1]

    pl.when(relay)(lambda: cut(relayed_ref))
    pl.when(jnp.logical_not(relay))(lambda: cut(tail_ref))


def prepare_kernel(x_ref, ws_ref, bs_ref, wt_ref, bt_ref, conv_ref, wide_ref, mix_ref, cb_ref, mb_ref, *piece_refs, spans):
    keep_rows(x_ref, piece_refs, spans)
    taps, channels = ws_ref.shape[0], ws_ref.shape[2]
    wide = []
    for i in range(taps):
        wide.append(ws_ref[jnp.where(flipped(), taps - 1 - i, i)].reshape(taps * channels, channels))
    wide_ref[...] = jnp.concatenate(wide, axis=0).T
    for j in range(taps):
        blocks = [part[j * channels : (j + 1) * channels] for part in wide]
        conv_ref[j * channels : (j + 1) * channels, :] = jnp.concatenate(blocks, axis=0).T
    mix_ref[...] = wt_ref[...].reshape(taps * channels, channels).T
    width = cb_ref.shape[1]
    cb_ref[...] = jnp.broadcast_to(bs_ref[...], (width, channels)).T
    mb_ref[...] = jnp.broadcast_to(bt_ref[...], (width, channels)).T


def conv_rows(columns, conv, bias, channels, width):
    stacked = jnp.concatenate(columns, axis=1)
    products = jnp.dot(conv, stacked, preferred_element_type=F32)
    lane = lax.broadcasted_iota(jnp.int32, (1, width), 1)
    rows = []
    for q in range(len(columns)):
        part = products[:, q * width : (q + 1) * width]
        left = jnp.where(lane == 0, 0.0, pltpu.roll(part[:channels], 1, 1))
        right = jnp.where(lane == width - 1, 0.0, pltpu.roll(part[2 * channels :], width - 1, 1))
        rows.append(silu(left + part[channels : 2 * channels] + right + bias).astype(BF16))
    return jnp.concatenate(rows, axis=1)


def shifted_rows(row):
    width = row.shape[-1]
    lane = lax.broadcasted_iota(jnp.int32, (1, width), 1)
    wide = row.astype(F32)
    left = jnp.where(lane == 0, 0.0, pltpu.roll(wide, 1, 1)).astype(BF16)
    right = jnp.where(lane == width - 1, 0.0, pltpu.roll(wide, width - 1, 1)).astype(BF16)
    return jnp.concatenate([left, row, right], axis=0)


def own_kernel(x_ref, beside_ref, conv_ref, mix_ref, cb_ref, mb_ref, early_ref, out_ref, xs, *, group):
    frames, rows, channels, width = x_ref.shape
    for f in range(frames):
        xs[f, 0] = beside_ref[f, 0]
        xs[f, rows + 1] = jnp.zeros((channels, width), BF16)

    def fill(s, carry):
        for f in range(frames):
            xs[f, s + 1] = x_ref[f, first_row(s, 1, rows)]
        return carry

    lax.fori_loop(0, rows, fill, 0)

    def body(p, carry):
        h = p * group
        parts = []
        for f in range(frames):
            columns = [xs[f, pl.ds(h + q, 3)].reshape(3 * channels, width) for q in range(group)]
            parts.append(conv_rows(columns, conv_ref[...], cb_ref[...], channels, width))
        mixed = jnp.dot(mix_ref[:, channels:], jnp.concatenate(parts, axis=0), preferred_element_type=F32)
        for q in range(group):
            out_ref[h + q] = mixed[:, q * width : (q + 1) * width] + mb_ref[...]
        return carry

    lax.fori_loop(0, rows // group, body, 0)


def incoming_kernel(own_ref, wide_ref, mix_ref, cb_ref, *refs, pieces, low, count, ready, stage):
    rows, channels, width = own_ref.shape
    flip = flipped()
    first = lax.axis_index("frames") == 0
    kept_ref, piece_refs, refs = refs[0], refs[1 : 1 + pieces], refs[1 + pieces :]
    ready_ref = out_ref = sem = None
    if ready:
        ready_ref, refs = refs[0], refs[1 + (low > ready) :]
        out_ref, refs, sem = refs[0], refs[1:-1], refs[-1]
    if stage == LAST:
        xs, made_ref = refs
    else:
        made_ref, carry_ref, xs = refs[:3]

    def to_output(source, place, size, k):
        target = out_ref.at[pl.ds(first_row(place, size, rows), size)]
        return pltpu.make_async_copy(source, target, sem.at[k])

    def own_rows(target, size):
        for q in range(size):
            target[jnp.where(flip, size - 1 - q, q)] = own_ref[low + q].astype(BF16)

    def convolve():
        slots = [] if stage == OPEN else [kept_ref.at[k] for k in range(kept_ref.shape[0])]
        fresh = [kept_ref.at[0]] if stage == OPEN else []
        for ref in piece_refs:
            size = ref.shape[1]
            fresh += [ref.at[0, jnp.where(flip, size - 1 - k, k)] for k in range(size)]
        total = len(slots) + len(fresh)
        for k, ref in enumerate(fresh):
            place = len(slots)
            slot = xs.at[k] if stage == LAST or place < total - 2 else carry_ref.at[place - total + 2]
            slot[...] = shifted_rows(ref[...])
            slots.append(slot)
        if stage == LAST:
            xs[len(fresh)] = jnp.zeros((3 * channels, width), BF16)
            slots.append(xs.at[len(fresh)])
        for h in range(0, count, 8):
            group = range(h, min(h + 8, count))
            columns = [jnp.concatenate([slots[q + i][...] for i in range(3)], axis=0) for q in group]
            summed = jnp.dot(wide_ref[...], jnp.concatenate(columns, axis=1), preferred_element_type=F32)
            act = [
                silu(summed[:, (q - h) * width : (q - h + 1) * width] + cb_ref[...]).astype(BF16) for q in group
            ]
            mixed = jnp.dot(mix_ref[:, :channels], jnp.concatenate(act, axis=1), preferred_element_type=F32)
            for q in group:
                term = mixed[:, (q - h) * width : (q - h + 1) * width]
                made_ref[jnp.where(flip, count - 1 - q, q)] = (own_ref[low + q] + term).astype(BF16)

    if stage == OPEN:

        @pl.when(first)
        def _():
            own_rows(made_ref, count)

        @pl.when(jnp.logical_not(first))
        def _():
            convolve()

        return

    before = to_output(ready_ref, low - ready, ready, 0)
    if stage == CLOSING:

        @pl.when(first)
        def _():
            rest = refs[3]
            own_rows(rest, rows - low)
            after = to_output(rest, low, rows - low, 1)
            before.start()
            after.start()
            before.wait()
            after.wait()

    @pl.when(jnp.logical_not(first))
    def _():
        before.start()
        convolve()
        if stage == LAST:
            after = to_output(made_ref, low, count, 1)
            after.start()
            after.wait()
        before.wait()


def incoming_rows(out, made, own, weights, kept, pieces, low, stage):
    wide, mix, cb = weights
    rows, channels, width = own.shape
    held = kept.shape[0] + sum(piece.shape[1] for piece in pieces) + (stage == LAST)
    count = held - 2
    ready = 0 if made is None else made.shape[0]

    def row_array(size):
        return jax.ShapeDtypeStruct((size, channels, width), BF16)

    operands = [own, wide, mix, cb, kept, *pieces]
    in_specs = [VMEM] * len(operands)
    out_shape, out_specs, aliases = [], [], {}
    if ready:
        operands.append(made)
        in_specs.append(VMEM)
        if out is not None:
            aliases = {len(operands): 0}
            operands.append(out)
            in_specs.append(ANY)
        out_shape.append(row_array(rows))
        out_specs.append(ANY)
    if stage != LAST:
        out_shape += [row_array(count), jax.ShapeDtypeStruct((2, 3 * channels, width), BF16)]
        out_specs += [VMEM] * 2
    scratch = [pltpu.VMEM((held, 3 * channels, width), BF16)]
    if stage == LAST:
        scratch.append(pltpu.VMEM((count, channels, width), BF16))
    if stage == CLOSING:
        scratch.append(pltpu.VMEM((rows - low, channels, width), BF16))
    if ready:
        scratch.append(pltpu.SemaphoreType.DMA((2,)))
    results = pl.pallas_call(
        functools.partial(
            incoming_kernel, pieces=len(pieces), low=low, count=count, ready=ready, stage=stage
        ),
        out_shape=out_shape,
        in_specs=in_specs,
        out_specs=out_specs,
        input_output_aliases=aliases,
        scratch_shapes=scratch,
        compiler_params=PARAMS,
        cost_estimate=cost(0, 0),
    )(*operands)
    if stage == LAST:
        return results[0], None, None
    return (results[0] if ready else None), results[-2], results[-1]


def per_device(video, w_spatial, b_spatial, w_temporal, b_temporal):
    frames, rows, width, channels = video.shape
    x = jnp.transpose(video, (0, 1, 3, 2))
    sizes, steps = [3, rows - 10, 4, 2, 1], [(0, 2), (2, 3), (3, 4), (4, 5)]
    places = [sum(sizes[:k]) for k in range(len(sizes))]
    spans = [(frames - 1, 1, place, size) for place, size in zip(places, sizes)]

    (head,) = pl.pallas_call(
        functools.partial(slice_kernel, spans=spans[:1]),
        out_shape=row_shapes(x, spans[:1]),
        in_specs=[ANY],
        out_specs=[VMEM],
        scratch_shapes=[pltpu.SemaphoreType.DMA((1,))],
        compiler_params=pltpu.CompilerParams(vmem_limit_bytes=HEAD_LIMIT),
    )(x)
    whole = [(0, frames, 0, rows)]
    (x,) = pl.pallas_call(
        functools.partial(load_kernel, spans=whole),
        out_shape=row_shapes(x, whole),
        in_specs=[ANY] * 2,
        out_specs=[VMEM],
        scratch_shapes=[pltpu.SemaphoreType.DMA((1,))],
        compiler_params=pltpu.CompilerParams(vmem_limit_bytes=LOAD_LIMIT),
        cost_estimate=cost(0, 0),
    )(x, head)
    ending = (frames - 1, 1, places[-2], sizes[-2] + sizes[-1])
    kept_spans = [(0, frames, 0, 1), spans[1]]
    boundary, second = pl.pallas_call(
        functools.partial(keep_kernel, spans=kept_spans),
        out_shape=row_shapes(x, kept_spans),
        in_specs=[VMEM],
        out_specs=[VMEM] * 2,
        compiler_params=PARAMS,
        cost_estimate=cost(0, 0),
    )(x)
    arrived = [lax.ppermute(piece, "frames", ring("frames")) for piece in (head, second)]
    beside = lax.ppermute(boundary, "rows", ring("rows"))

    square = jax.ShapeDtypeStruct((3 * channels, 3 * channels), BF16)
    broad = jax.ShapeDtypeStruct((channels, 9 * channels), BF16)
    flat = jax.ShapeDtypeStruct((channels, 3 * channels), BF16)
    bias = jax.ShapeDtypeStruct((channels, width), F32)
    conv, wide, mix, cb, mb, piece, tail = pl.pallas_call(
        functools.partial(prepare_kernel, spans=[spans[2], ending]),
        out_shape=[square, broad, flat, bias, bias] + row_shapes(x, [spans[2], ending]),
        in_specs=[VMEM] * 5,
        out_specs=[VMEM] * 7,
        compiler_params=PARAMS,
        cost_estimate=cost(0, 2 * 12 * channels * channels * 2),
    )(x, w_spatial, b_spatial.reshape(1, channels), w_temporal, b_temporal.reshape(1, channels))
    arrived.append(lax.ppermute(piece, "frames", ring("frames")))
    relayed = next_odd(tail, "frames")

    own = pl.pallas_call(
        functools.partial(own_kernel, group=next(g for g in (8, 4, 3, 2, 1) if rows % g == 0)),
        out_shape=jax.ShapeDtypeStruct((rows, channels, width), F32),
        in_specs=[VMEM] * 6 + [ANY],
        out_specs=VMEM,
        scratch_shapes=[pltpu.VMEM((frames, rows + 2, channels, width), BF16)],
        compiler_params=PARAMS,
        cost_estimate=cost(2 * rows * width * channels * channels * 20, 8 * rows * channels * width),
    )(x, beside, conv, mix, cb, mb, arrived[0])
    own, arrived[0] = lax.optimization_barrier((own, arrived[0]))
    edge, *pieces = pl.pallas_call(
        edge_kernel,
        out_shape=[jax.ShapeDtypeStruct((1, channels, width), BF16)] + row_shapes(x, spans[-2:]),
        in_specs=[VMEM] * 3 + [ANY],
        out_specs=[VMEM] * 3,
        compiler_params=PARAMS,
        cost_estimate=cost(0, 0),
    )(arrived[0], tail, relayed, arrived[1])
    arrived += [within_pairs(pieces[0], "frames", True), within_pairs(pieces[1], "frames", False)]
    kept = lax.ppermute(edge, "rows", ring("rows"))

    weights = (wide, mix, cb)
    out, made, low = None, None, 0
    for k, (begin, end) in enumerate(steps):
        stage = LAST if end == len(arrived) else min(k, LATE)
        out, made, kept = incoming_rows(out, made, own, weights, kept, arrived[begin:end], low, stage)
        low = places[end - 1] + sizes[end - 1] - 1
    return jnp.transpose(out[None], (0, 1, 3, 2))


def solution(mesh):
    in_specs = (P(("batch", "frames"), "rows", None, None), P(), P(), P(), P())
    out_specs = P(("batch", "frames"), "rows", None, None)
    return jax.shard_map(
        per_device, mesh=mesh, in_specs=in_specs, out_specs=out_specs, check_vma=False
    )
```

```python
import functools

import jax
import jax.numpy as jnp
from jax import lax
from jax.experimental import pallas as pl
from jax.experimental.pallas import tpu as pltpu
from jax.sharding import PartitionSpec as P

F32 = jnp.float32
BF16 = jnp.bfloat16
VMEM = pl.BlockSpec(memory_space=pltpu.VMEM)
ANY = pl.BlockSpec(memory_space=pl.ANY)
HEAD_LIMIT = 53 * 2**20
LOAD_LIMIT = 50 * 2**20
OPEN, CLOSING, LATE, LAST = range(4)
PARAMS = pltpu.CompilerParams(vmem_limit_bytes=20 * 2**20)


def flipped():
    return lax.axis_index("rows") == 0


def first_row(place, size, rows):
    return jnp.where(flipped(), rows - place - size, place)


def ring(axis):
    count = lax.axis_size(axis)
    return [(i, (i + 1) % count) for i in range(count)]


def next_odd(piece, axis):
    count = lax.axis_size(axis)
    return lax.ppermute(piece, axis, [(i, (i + 2) % count) for i in range(1, count, 2)])


def within_pairs(piece, axis, keep):
    count = lax.axis_size(axis)
    route = ring(axis) if count % 2 else [(i, i ^ 1) for i in range(count)]
    return lax.ppermute(piece, axis, [(a, b) for a, b in route if b or keep])


def cost(flops, moved):
    return pl.CostEstimate(flops=flops, bytes_accessed=moved, transcendentals=0)


def silu(v):
    half = 0.5 * v
    return half + half * jnp.tanh(half)


def span_of(x_ref, span):
    frame, count, place, size = span
    return x_ref.at[pl.ds(frame, count), pl.ds(first_row(place, size, x_ref.shape[1]), size)]


def keep_rows(x_ref, outs, spans):
    for out, span in zip(outs, spans):
        out[...] = span_of(x_ref, span)[...]


def load_kernel(x_ref, head_ref, *refs, spans):
    slice_kernel(x_ref, *refs, spans=spans)


def keep_kernel(x_ref, *outs, spans):
    keep_rows(x_ref, outs, spans)


def row_shapes(x, spans):
    return [jax.ShapeDtypeStruct((count, size) + x.shape[2:], x.dtype) for _, count, _, size in spans]


def slice_kernel(x_ref, *refs, spans):
    outs, sem = refs[:-1], refs[-1]
    copies = [
        pltpu.make_async_copy(span_of(x_ref, span), out, sem.at[k])
        for k, (out, span) in enumerate(zip(outs, spans))
    ]
    for copy in copies:
        copy.start()
    for copy in copies:
        copy.wait()


def edge_kernel(piece_ref, tail_ref, relayed_ref, second_ref, out_ref, *tail_out_refs):
    size = piece_ref.shape[1]
    out_ref[0] = piece_ref[0, jnp.where(flipped(), size - 1, 0)]
    count = lax.axis_size("frames")
    relay = jnp.logical_and(count % 2 == 0, lax.rem(lax.axis_index("frames"), 2) == 1)

    def cut(source_ref):
        place = 0
        for ref in tail_out_refs:
            ref[...] = span_of(source_ref, (0, 1, place, ref.shape[1]))[...]
            place += ref.shape[1]

    pl.when(relay)(lambda: cut(relayed_ref))
    pl.when(jnp.logical_not(relay))(lambda: cut(tail_ref))


def prepare_kernel(x_ref, ws_ref, bs_ref, wt_ref, bt_ref, conv_ref, wide_ref, mix_ref, cb_ref, mb_ref, *piece_refs, spans):
    keep_rows(x_ref, piece_refs, spans)
    taps, channels = ws_ref.shape[0], ws_ref.shape[2]
    wide = []
    for i in range(taps):
        wide.append(ws_ref[jnp.where(flipped(), taps - 1 - i, i)].reshape(taps * channels, channels))
    wide_ref[...] = jnp.concatenate(wide, axis=0).T
    for j in range(taps):
        blocks = [part[j * channels : (j + 1) * channels] for part in wide]
        conv_ref[j * channels : (j + 1) * channels, :] = jnp.concatenate(blocks, axis=0).T
    mix_ref[...] = wt_ref[...].reshape(taps * channels, channels).T
    width = cb_ref.shape[1]
    cb_ref[...] = jnp.broadcast_to(bs_ref[...], (width, channels)).T
    mb_ref[...] = jnp.broadcast_to(bt_ref[...], (width, channels)).T


def conv_rows(columns, conv, bias, channels, width):
    stacked = jnp.concatenate(columns, axis=1)
    products = jnp.dot(conv, stacked, preferred_element_type=F32)
    lane = lax.broadcasted_iota(jnp.int32, (1, width), 1)
    rows = []
    for q in range(len(columns)):
        part = products[:, q * width : (q + 1) * width]
        left = jnp.where(lane == 0, 0.0, pltpu.roll(part[:channels], 1, 1))
        right = jnp.where(lane == width - 1, 0.0, pltpu.roll(part[2 * channels :], width - 1, 1))
        rows.append(silu(left + part[channels : 2 * channels] + right + bias).astype(BF16))
    return jnp.concatenate(rows, axis=1)


def shifted_rows(row):
    width = row.shape[-1]
    lane = lax.broadcasted_iota(jnp.int32, (1, width), 1)
    wide = row.astype(F32)
    left = jnp.where(lane == 0, 0.0, pltpu.roll(wide, 1, 1)).astype(BF16)
    right = jnp.where(lane == width - 1, 0.0, pltpu.roll(wide, width - 1, 1)).astype(BF16)
    return jnp.concatenate([left, row, right], axis=0)


def own_kernel(x_ref, beside_ref, conv_ref, mix_ref, cb_ref, mb_ref, early_ref, out_ref, xs, *, group):
    frames, rows, channels, width = x_ref.shape
    for f in range(frames):
        xs[f, 0] = beside_ref[f, 0]
        xs[f, rows + 1] = jnp.zeros((channels, width), BF16)

    def fill(s, carry):
        for f in range(frames):
            xs[f, s + 1] = x_ref[f, first_row(s, 1, rows)]
        return carry

    lax.fori_loop(0, rows, fill, 0)

    def body(p, carry):
        h = p * group
        parts = []
        for f in range(frames):
            columns = [xs[f, pl.ds(h + q, 3)].reshape(3 * channels, width) for q in range(group)]
            parts.append(conv_rows(columns, conv_ref[...], cb_ref[...], channels, width))
        mixed = jnp.dot(mix_ref[:, channels:], jnp.concatenate(parts, axis=0), preferred_element_type=F32)
        for q in range(group):
            out_ref[h + q] = mixed[:, q * width : (q + 1) * width] + mb_ref[...]
        return carry

    lax.fori_loop(0, rows // group, body, 0)


def incoming_kernel(own_ref, wide_ref, mix_ref, cb_ref, *refs, pieces, low, count, ready, stage):
    rows, channels, width = own_ref.shape
    flip = flipped()
    first = lax.axis_index("frames") == 0
    kept_ref, piece_refs, refs = refs[0], refs[1 : 1 + pieces], refs[1 + pieces :]
    ready_ref = out_ref = sem = None
    if ready:
        ready_ref, refs = refs[0], refs[1 + (low > ready) :]
        out_ref, refs, sem = refs[0], refs[1:-1], refs[-1]
    if stage == LAST:
        xs, made_ref = refs
    else:
        made_ref, carry_ref, xs = refs[:3]

    def to_output(source, place, size, k):
        target = out_ref.at[pl.ds(first_row(place, size, rows), size)]
        return pltpu.make_async_copy(source, target, sem.at[k])

    def own_rows(target, size):
        for q in range(size):
            target[jnp.where(flip, size - 1 - q, q)] = own_ref[low + q].astype(BF16)

    def convolve():
        slots = [] if stage == OPEN else [kept_ref.at[k] for k in range(kept_ref.shape[0])]
        fresh = [kept_ref.at[0]] if stage == OPEN else []
        for ref in piece_refs:
            size = ref.shape[1]
            fresh += [ref.at[0, jnp.where(flip, size - 1 - k, k)] for k in range(size)]
        total = len(slots) + len(fresh)
        for k, ref in enumerate(fresh):
            place = len(slots)
            slot = xs.at[k] if stage == LAST or place < total - 2 else carry_ref.at[place - total + 2]
            slot[...] = shifted_rows(ref[...])
            slots.append(slot)
        if stage == LAST:
            xs[len(fresh)] = jnp.zeros((3 * channels, width), BF16)
            slots.append(xs.at[len(fresh)])
        for h in range(0, count, 8):
            group = range(h, min(h + 8, count))
            columns = [jnp.concatenate([slots[q + i][...] for i in range(3)], axis=0) for q in group]
            summed = jnp.dot(wide_ref[...], jnp.concatenate(columns, axis=1), preferred_element_type=F32)
            act = [
                silu(summed[:, (q - h) * width : (q - h + 1) * width] + cb_ref[...]).astype(BF16) for q in group
            ]
            mixed = jnp.dot(mix_ref[:, :channels], jnp.concatenate(act, axis=1), preferred_element_type=F32)
            for q in group:
                term = mixed[:, (q - h) * width : (q - h + 1) * width]
                made_ref[jnp.where(flip, count - 1 - q, q)] = (own_ref[low + q] + term).astype(BF16)

    if stage == OPEN:

        @pl.when(first)
        def _():
            own_rows(made_ref, count)

        @pl.when(jnp.logical_not(first))
        def _():
            convolve()

        return

    before = to_output(ready_ref, low - ready, ready, 0)
    if stage == CLOSING:

        @pl.when(first)
        def _():
            rest = refs[3]
            own_rows(rest, rows - low)
            after = to_output(rest, low, rows - low, 1)
            before.start()
            after.start()
            before.wait()
            after.wait()

    @pl.when(jnp.logical_not(first))
    def _():
        before.start()
        convolve()
        if stage == LAST:
            after = to_output(made_ref, low, count, 1)
            after.start()
            after.wait()
        before.wait()


def incoming_rows(out, made, own, weights, kept, pieces, low, stage):
    wide, mix, cb = weights
    rows, channels, width = own.shape
    held = kept.shape[0] + sum(piece.shape[1] for piece in pieces) + (stage == LAST)
    count = held - 2
    ready = 0 if made is None else made.shape[0]

    def row_array(size):
        return jax.ShapeDtypeStruct((size, channels, width), BF16)

    operands = [own, wide, mix, cb, kept, *pieces]
    in_specs = [VMEM] * len(operands)
    out_shape, out_specs, aliases = [], [], {}
    if ready:
        operands.append(made)
        in_specs.append(VMEM)
        if out is not None:
            aliases = {len(operands): 0}
            operands.append(out)
            in_specs.append(ANY)
        out_shape.append(row_array(rows))
        out_specs.append(ANY)
    if stage != LAST:
        out_shape += [row_array(count), jax.ShapeDtypeStruct((2, 3 * channels, width), BF16)]
        out_specs += [VMEM] * 2
    scratch = [pltpu.VMEM((held, 3 * channels, width), BF16)]
    if stage == LAST:
        scratch.append(pltpu.VMEM((count, channels, width), BF16))
    if stage == CLOSING:
        scratch.append(pltpu.VMEM((rows - low, channels, width), BF16))
    if ready:
        scratch.append(pltpu.SemaphoreType.DMA((2,)))
    results = pl.pallas_call(
        functools.partial(
            incoming_kernel, pieces=len(pieces), low=low, count=count, ready=ready, stage=stage
        ),
        out_shape=out_shape,
        in_specs=in_specs,
        out_specs=out_specs,
        input_output_aliases=aliases,
        scratch_shapes=scratch,
        compiler_params=PARAMS,
        cost_estimate=cost(0, 0),
    )(*operands)
    if stage == LAST:
        return results[0], None, None
    return (results[0] if ready else None), results[-2], results[-1]


def per_device(video, w_spatial, b_spatial, w_temporal, b_temporal):
    frames, rows, width, channels = video.shape
    x = jnp.transpose(video, (0, 1, 3, 2))
    sizes, steps = [4, rows - 11, 4, 2, 1], [(0, 2), (2, 3), (3, 4), (4, 5)]
    places = [sum(sizes[:k]) for k in range(len(sizes))]
    spans = [(frames - 1, 1, place, size) for place, size in zip(places, sizes)]

    (head,) = pl.pallas_call(
        functools.partial(slice_kernel, spans=spans[:1]),
        out_shape=row_shapes(x, spans[:1]),
        in_specs=[ANY],
        out_specs=[VMEM],
        scratch_shapes=[pltpu.SemaphoreType.DMA((1,))],
        compiler_params=pltpu.CompilerParams(vmem_limit_bytes=HEAD_LIMIT),
    )(x)
    whole = [(0, frames, 0, rows)]
    (x,) = pl.pallas_call(
        functools.partial(load_kernel, spans=whole),
        out_shape=row_shapes(x, whole),
        in_specs=[ANY] * 2,
        out_specs=[VMEM],
        scratch_shapes=[pltpu.SemaphoreType.DMA((1,))],
        compiler_params=pltpu.CompilerParams(vmem_limit_bytes=LOAD_LIMIT),
        cost_estimate=cost(0, 0),
    )(x, head)
    ending = (frames - 1, 1, places[-2], sizes[-2] + sizes[-1])
    kept_spans = [(0, frames, 0, 1), spans[1]]
    boundary, second = pl.pallas_call(
        functools.partial(keep_kernel, spans=kept_spans),
        out_shape=row_shapes(x, kept_spans),
        in_specs=[VMEM],
        out_specs=[VMEM] * 2,
        compiler_params=PARAMS,
        cost_estimate=cost(0, 0),
    )(x)
    arrived = [lax.ppermute(piece, "frames", ring("frames")) for piece in (head, second)]
    beside = lax.ppermute(boundary, "rows", ring("rows"))

    square = jax.ShapeDtypeStruct((3 * channels, 3 * channels), BF16)
    broad = jax.ShapeDtypeStruct((channels, 9 * channels), BF16)
    flat = jax.ShapeDtypeStruct((channels, 3 * channels), BF16)
    bias = jax.ShapeDtypeStruct((channels, width), F32)
    conv, wide, mix, cb, mb, piece, tail = pl.pallas_call(
        functools.partial(prepare_kernel, spans=[spans[2], ending]),
        out_shape=[square, broad, flat, bias, bias] + row_shapes(x, [spans[2], ending]),
        in_specs=[VMEM] * 5,
        out_specs=[VMEM] * 7,
        compiler_params=PARAMS,
        cost_estimate=cost(0, 2 * 12 * channels * channels * 2),
    )(x, w_spatial, b_spatial.reshape(1, channels), w_temporal, b_temporal.reshape(1, channels))
    arrived.append(lax.ppermute(piece, "frames", ring("frames")))
    relayed = next_odd(tail, "frames")

    own = pl.pallas_call(
        functools.partial(own_kernel, group=next(g for g in (8, 4, 3, 2, 1) if rows % g == 0)),
        out_shape=jax.ShapeDtypeStruct((rows, channels, width), F32),
        in_specs=[VMEM] * 6 + [ANY],
        out_specs=VMEM,
        scratch_shapes=[pltpu.VMEM((frames, rows + 2, channels, width), BF16)],
        compiler_params=PARAMS,
        cost_estimate=cost(2 * rows * width * channels * channels * 20, 8 * rows * channels * width),
    )(x, beside, conv, mix, cb, mb, arrived[0])
    own, arrived[0] = lax.optimization_barrier((own, arrived[0]))
    edge, *pieces = pl.pallas_call(
        edge_kernel,
        out_shape=[jax.ShapeDtypeStruct((1, channels, width), BF16)] + row_shapes(x, spans[-2:]),
        in_specs=[VMEM] * 3 + [ANY],
        out_specs=[VMEM] * 3,
        compiler_params=PARAMS,
        cost_estimate=cost(0, 0),
    )(arrived[0], tail, relayed, arrived[1])
    arrived += [within_pairs(pieces[0], "frames", True), within_pairs(pieces[1], "frames", True)]
    kept = lax.ppermute(edge, "rows", ring("rows"))

    weights = (wide, mix, cb)
    out, made, low = None, None, 0
    for k, (begin, end) in enumerate(steps):
        stage = LAST if end == len(arrived) else min(k, LATE)
        out, made, kept = incoming_rows(out, made, own, weights, kept, arrived[begin:end], low, stage)
        low = places[end - 1] + sizes[end - 1] - 1
    return jnp.transpose(out[None], (0, 1, 3, 2))


def solution(mesh):
    in_specs = (P(("batch", "frames"), "rows", None, None), P(), P(), P(), P())
    out_specs = P(("batch", "frames"), "rows", None, None)
    return jax.shard_map(
        per_device, mesh=mesh, in_specs=in_specs, out_specs=out_specs, check_vma=False
    )
```

```python
import functools

import jax
import jax.numpy as jnp
from jax import lax
from jax.experimental import pallas as pl
from jax.experimental.pallas import tpu as pltpu
from jax.sharding import PartitionSpec as P

F32 = jnp.float32
BF16 = jnp.bfloat16
VMEM = pl.BlockSpec(memory_space=pltpu.VMEM)
ANY = pl.BlockSpec(memory_space=pl.ANY)
HEAD_LIMIT = 53 * 2**20
LOAD_LIMIT = 50 * 2**20
OPEN, CLOSING, LATE, LAST = range(4)
PARAMS = pltpu.CompilerParams(vmem_limit_bytes=20 * 2**20)


def flipped():
    return lax.axis_index("rows") == 0


def first_row(place, size, rows):
    return jnp.where(flipped(), rows - place - size, place)


def ring(axis):
    count = lax.axis_size(axis)
    return [(i, (i + 1) % count) for i in range(count)]


def next_odd(piece, axis):
    count = lax.axis_size(axis)
    return lax.ppermute(piece, axis, [(i, (i + 2) % count) for i in range(1, count, 2)])


def within_pairs(piece, axis, keep):
    count = lax.axis_size(axis)
    route = ring(axis) if count % 2 else [(i, i ^ 1) for i in range(count)]
    return lax.ppermute(piece, axis, [(a, b) for a, b in route if b or keep])


def cost(flops, moved):
    return pl.CostEstimate(flops=flops, bytes_accessed=moved, transcendentals=0)


def silu(v):
    half = 0.5 * v
    return half + half * jnp.tanh(half)


def span_of(x_ref, span):
    frame, count, place, size = span
    return x_ref.at[pl.ds(frame, count), pl.ds(first_row(place, size, x_ref.shape[1]), size)]


def keep_rows(x_ref, outs, spans):
    for out, span in zip(outs, spans):
        out[...] = span_of(x_ref, span)[...]


def load_kernel(x_ref, head_ref, *refs, spans):
    slice_kernel(x_ref, *refs, spans=spans)


def keep_kernel(x_ref, *outs, spans):
    keep_rows(x_ref, outs, spans)


def row_shapes(x, spans):
    return [jax.ShapeDtypeStruct((count, size) + x.shape[2:], x.dtype) for _, count, _, size in spans]


def slice_kernel(x_ref, *refs, spans):
    outs, sem = refs[:-1], refs[-1]
    copies = [
        pltpu.make_async_copy(span_of(x_ref, span), out, sem.at[k])
        for k, (out, span) in enumerate(zip(outs, spans))
    ]
    for copy in copies:
        copy.start()
    for copy in copies:
        copy.wait()


def edge_kernel(piece_ref, tail_ref, relayed_ref, second_ref, out_ref, *tail_out_refs):
    size = piece_ref.shape[1]
    out_ref[0] = piece_ref[0, jnp.where(flipped(), size - 1, 0)]
    count = lax.axis_size("frames")
    relay = jnp.logical_and(count % 2 == 0, lax.rem(lax.axis_index("frames"), 2) == 1)

    def cut(source_ref):
        place = 0
        for ref in tail_out_refs:
            ref[...] = span_of(source_ref, (0, 1, place, ref.shape[1]))[...]
            place += ref.shape[1]

    pl.when(relay)(lambda: cut(relayed_ref))
    pl.when(jnp.logical_not(relay))(lambda: cut(tail_ref))


def prepare_kernel(x_ref, ws_ref, bs_ref, wt_ref, bt_ref, conv_ref, wide_ref, mix_ref, cb_ref, mb_ref, *piece_refs, spans):
    keep_rows(x_ref, piece_refs, spans)
    taps, channels = ws_ref.shape[0], ws_ref.shape[2]
    wide = []
    for i in range(taps):
        wide.append(ws_ref[jnp.where(flipped(), taps - 1 - i, i)].reshape(taps * channels, channels))
    wide_ref[...] = jnp.concatenate(wide, axis=0).T
    for j in range(taps):
        blocks = [part[j * channels : (j + 1) * channels] for part in wide]
        conv_ref[j * channels : (j + 1) * channels, :] = jnp.concatenate(blocks, axis=0).T
    mix_ref[...] = wt_ref[...].reshape(taps * channels, channels).T
    width = cb_ref.shape[1]
    cb_ref[...] = jnp.broadcast_to(bs_ref[...], (width, channels)).T
    mb_ref[...] = jnp.broadcast_to(bt_ref[...], (width, channels)).T


def conv_rows(columns, conv, bias, channels, width):
    stacked = jnp.concatenate(columns, axis=1)
    products = jnp.dot(conv, stacked, preferred_element_type=F32)
    lane = lax.broadcasted_iota(jnp.int32, (1, width), 1)
    rows = []
    for q in range(len(columns)):
        part = products[:, q * width : (q + 1) * width]
        left = jnp.where(lane == 0, 0.0, pltpu.roll(part[:channels], 1, 1))
        right = jnp.where(lane == width - 1, 0.0, pltpu.roll(part[2 * channels :], width - 1, 1))
        rows.append(silu(left + part[channels : 2 * channels] + right + bias).astype(BF16))
    return jnp.concatenate(rows, axis=1)


def shifted_rows(row):
    width = row.shape[-1]
    lane = lax.broadcasted_iota(jnp.int32, (1, width), 1)
    wide = row.astype(F32)
    left = jnp.where(lane == 0, 0.0, pltpu.roll(wide, 1, 1)).astype(BF16)
    right = jnp.where(lane == width - 1, 0.0, pltpu.roll(wide, width - 1, 1)).astype(BF16)
    return jnp.concatenate([left, row, right], axis=0)


def own_kernel(x_ref, beside_ref, conv_ref, mix_ref, cb_ref, mb_ref, early_ref, out_ref, xs, *, group):
    frames, rows, channels, width = x_ref.shape
    for f in range(frames):
        xs[f, 0] = beside_ref[f, 0]
        xs[f, rows + 1] = jnp.zeros((channels, width), BF16)

    def fill(s, carry):
        for f in range(frames):
            xs[f, s + 1] = x_ref[f, first_row(s, 1, rows)]
        return carry

    lax.fori_loop(0, rows, fill, 0)

    def body(p, carry):
        h = p * group
        parts = []
        for f in range(frames):
            columns = [xs[f, pl.ds(h + q, 3)].reshape(3 * channels, width) for q in range(group)]
            parts.append(conv_rows(columns, conv_ref[...], cb_ref[...], channels, width))
        mixed = jnp.dot(mix_ref[:, channels:], jnp.concatenate(parts, axis=0), preferred_element_type=F32)
        for q in range(group):
            out_ref[h + q] = mixed[:, q * width : (q + 1) * width] + mb_ref[...]
        return carry

    lax.fori_loop(0, rows // group, body, 0)


def incoming_kernel(own_ref, wide_ref, mix_ref, cb_ref, *refs, pieces, low, count, ready, stage):
    rows, channels, width = own_ref.shape
    flip = flipped()
    first = lax.axis_index("frames") == 0
    kept_ref, piece_refs, refs = refs[0], refs[1 : 1 + pieces], refs[1 + pieces :]
    ready_ref = out_ref = sem = None
    if ready:
        ready_ref, refs = refs[0], refs[1 + (low > ready) :]
        out_ref, refs, sem = refs[0], refs[1:-1], refs[-1]
    if stage == LAST:
        xs, made_ref = refs
    else:
        made_ref, carry_ref, xs = refs[:3]

    def to_output(source, place, size, k):
        target = out_ref.at[pl.ds(first_row(place, size, rows), size)]
        return pltpu.make_async_copy(source, target, sem.at[k])

    def own_rows(target, size):
        for q in range(size):
            target[jnp.where(flip, size - 1 - q, q)] = own_ref[low + q].astype(BF16)

    def convolve():
        slots = [] if stage == OPEN else [kept_ref.at[k] for k in range(kept_ref.shape[0])]
        fresh = [kept_ref.at[0]] if stage == OPEN else []
        for ref in piece_refs:
            size = ref.shape[1]
            fresh += [ref.at[0, jnp.where(flip, size - 1 - k, k)] for k in range(size)]
        total = len(slots) + len(fresh)
        for k, ref in enumerate(fresh):
            place = len(slots)
            slot = xs.at[k] if stage == LAST or place < total - 2 else carry_ref.at[place - total + 2]
            slot[...] = shifted_rows(ref[...])
            slots.append(slot)
        if stage == LAST:
            xs[len(fresh)] = jnp.zeros((3 * channels, width), BF16)
            slots.append(xs.at[len(fresh)])
        for h in range(0, count, 8):
            group = range(h, min(h + 8, count))
            columns = [jnp.concatenate([slots[q + i][...] for i in range(3)], axis=0) for q in group]
            summed = jnp.dot(wide_ref[...], jnp.concatenate(columns, axis=1), preferred_element_type=F32)
            act = [
                silu(summed[:, (q - h) * width : (q - h + 1) * width] + cb_ref[...]).astype(BF16) for q in group
            ]
            mixed = jnp.dot(mix_ref[:, :channels], jnp.concatenate(act, axis=1), preferred_element_type=F32)
            for q in group:
                term = mixed[:, (q - h) * width : (q - h + 1) * width]
                made_ref[jnp.where(flip, count - 1 - q, q)] = (own_ref[low + q] + term).astype(BF16)

    if stage == OPEN:

        @pl.when(first)
        def _():
            own_rows(made_ref, count)

        @pl.when(jnp.logical_not(first))
        def _():
            convolve()

        return

    before = to_output(ready_ref, low - ready, ready, 0)
    if stage == CLOSING:

        @pl.when(first)
        def _():
            rest = refs[3]
            own_rows(rest, rows - low)
            after = to_output(rest, low, rows - low, 1)
            before.start()
            after.start()
            before.wait()
            after.wait()

    @pl.when(jnp.logical_not(first))
    def _():
        if stage != LAST:
            before.start()
        convolve()
        if stage == LAST:
            after = to_output(made_ref, low, count, 1)
            after.start()
            before.start()
            after.wait()
        before.wait()


def incoming_rows(out, made, own, weights, kept, pieces, low, stage):
    wide, mix, cb = weights
    rows, channels, width = own.shape
    held = kept.shape[0] + sum(piece.shape[1] for piece in pieces) + (stage == LAST)
    count = held - 2
    ready = 0 if made is None else made.shape[0]

    def row_array(size):
        return jax.ShapeDtypeStruct((size, channels, width), BF16)

    operands = [own, wide, mix, cb, kept, *pieces]
    in_specs = [VMEM] * len(operands)
    out_shape, out_specs, aliases = [], [], {}
    if ready:
        operands.append(made)
        in_specs.append(VMEM)
        if out is not None:
            aliases = {len(operands): 0}
            operands.append(out)
            in_specs.append(ANY)
        out_shape.append(row_array(rows))
        out_specs.append(ANY)
    if stage != LAST:
        out_shape += [row_array(count), jax.ShapeDtypeStruct((2, 3 * channels, width), BF16)]
        out_specs += [VMEM] * 2
    scratch = [pltpu.VMEM((held, 3 * channels, width), BF16)]
    if stage == LAST:
        scratch.append(pltpu.VMEM((count, channels, width), BF16))
    if stage == CLOSING:
        scratch.append(pltpu.VMEM((rows - low, channels, width), BF16))
    if ready:
        scratch.append(pltpu.SemaphoreType.DMA((2,)))
    results = pl.pallas_call(
        functools.partial(
            incoming_kernel, pieces=len(pieces), low=low, count=count, ready=ready, stage=stage
        ),
        out_shape=out_shape,
        in_specs=in_specs,
        out_specs=out_specs,
        input_output_aliases=aliases,
        scratch_shapes=scratch,
        compiler_params=PARAMS,
        cost_estimate=cost(0, 0),
    )(*operands)
    if stage == LAST:
        return results[0], None, None
    return (results[0] if ready else None), results[-2], results[-1]


def per_device(video, w_spatial, b_spatial, w_temporal, b_temporal):
    frames, rows, width, channels = video.shape
    x = jnp.transpose(video, (0, 1, 3, 2))
    sizes, steps = [3, rows - 10, 4, 2, 1], [(0, 2), (2, 3), (3, 4), (4, 5)]
    places = [sum(sizes[:k]) for k in range(len(sizes))]
    spans = [(frames - 1, 1, place, size) for place, size in zip(places, sizes)]

    (head,) = pl.pallas_call(
        functools.partial(slice_kernel, spans=spans[:1]),
        out_shape=row_shapes(x, spans[:1]),
        in_specs=[ANY],
        out_specs=[VMEM],
        scratch_shapes=[pltpu.SemaphoreType.DMA((1,))],
        compiler_params=pltpu.CompilerParams(vmem_limit_bytes=HEAD_LIMIT),
    )(x)
    whole = [(0, frames, 0, rows)]
    (x,) = pl.pallas_call(
        functools.partial(load_kernel, spans=whole),
        out_shape=row_shapes(x, whole),
        in_specs=[ANY] * 2,
        out_specs=[VMEM],
        scratch_shapes=[pltpu.SemaphoreType.DMA((1,))],
        compiler_params=pltpu.CompilerParams(vmem_limit_bytes=LOAD_LIMIT),
        cost_estimate=cost(0, 0),
    )(x, head)
    ending = (frames - 1, 1, places[-2], sizes[-2] + sizes[-1])
    kept_spans = [(0, frames, 0, 1), spans[1]]
    boundary, second = pl.pallas_call(
        functools.partial(keep_kernel, spans=kept_spans),
        out_shape=row_shapes(x, kept_spans),
        in_specs=[VMEM],
        out_specs=[VMEM] * 2,
        compiler_params=PARAMS,
        cost_estimate=cost(0, 0),
    )(x)
    arrived = [lax.ppermute(piece, "frames", ring("frames")) for piece in (head, second)]
    beside = lax.ppermute(boundary, "rows", ring("rows"))

    square = jax.ShapeDtypeStruct((3 * channels, 3 * channels), BF16)
    broad = jax.ShapeDtypeStruct((channels, 9 * channels), BF16)
    flat = jax.ShapeDtypeStruct((channels, 3 * channels), BF16)
    bias = jax.ShapeDtypeStruct((channels, width), F32)
    conv, wide, mix, cb, mb, piece, tail = pl.pallas_call(
        functools.partial(prepare_kernel, spans=[spans[2], ending]),
        out_shape=[square, broad, flat, bias, bias] + row_shapes(x, [spans[2], ending]),
        in_specs=[VMEM] * 5,
        out_specs=[VMEM] * 7,
        compiler_params=PARAMS,
        cost_estimate=cost(0, 2 * 12 * channels * channels * 2),
    )(x, w_spatial, b_spatial.reshape(1, channels), w_temporal, b_temporal.reshape(1, channels))
    arrived.append(lax.ppermute(piece, "frames", ring("frames")))
    relayed = next_odd(tail, "frames")

    own = pl.pallas_call(
        functools.partial(own_kernel, group=next(g for g in (8, 4, 3, 2, 1) if rows % g == 0)),
        out_shape=jax.ShapeDtypeStruct((rows, channels, width), F32),
        in_specs=[VMEM] * 6 + [ANY],
        out_specs=VMEM,
        scratch_shapes=[pltpu.VMEM((frames, rows + 2, channels, width), BF16)],
        compiler_params=PARAMS,
        cost_estimate=cost(2 * rows * width * channels * channels * 20, 8 * rows * channels * width),
    )(x, beside, conv, mix, cb, mb, arrived[0])
    own, arrived[0] = lax.optimization_barrier((own, arrived[0]))
    edge, *pieces = pl.pallas_call(
        edge_kernel,
        out_shape=[jax.ShapeDtypeStruct((1, channels, width), BF16)] + row_shapes(x, spans[-2:]),
        in_specs=[VMEM] * 3 + [ANY],
        out_specs=[VMEM] * 3,
        compiler_params=PARAMS,
        cost_estimate=cost(0, 0),
    )(arrived[0], tail, relayed, arrived[1])
    arrived += [within_pairs(pieces[0], "frames", True), within_pairs(pieces[1], "frames", True)]
    kept = lax.ppermute(edge, "rows", ring("rows"))

    weights = (wide, mix, cb)
    out, made, low = None, None, 0
    for k, (begin, end) in enumerate(steps):
        stage = LAST if end == len(arrived) else min(k, LATE)
        out, made, kept = incoming_rows(out, made, own, weights, kept, arrived[begin:end], low, stage)
        low = places[end - 1] + sizes[end - 1] - 1
    return jnp.transpose(out[None], (0, 1, 3, 2))


def solution(mesh):
    in_specs = (P(("batch", "frames"), "rows", None, None), P(), P(), P(), P())
    out_specs = P(("batch", "frames"), "rows", None, None)
    return jax.shard_map(
        per_device, mesh=mesh, in_specs=in_specs, out_specs=out_specs, check_vma=False
    )
```
